768 devices in a mesh: gx: 12 (over z), gy: 16 (over y, core), gz: 4 (over x).
Axes of the slice: x: 4, y: 8, z: 12, core: 2. Of those that a mesh axis runs over, the one named last changes fastest.
Arguments:
- solution: float32 [3, 96, 256, 512], P(None, 'gx', 'gy', 'gz'), may hold values from -6 to 6
- residual: float32 [3, 96, 256, 512], P(None, 'gx', 'gy', 'gz'), may hold values from -15 to 15
- density_bins: int32 [96, 256, 512], P('gx', 'gy', 'gz'), may hold values from 0 to 15
- fixed_dofs: int32 [3, 96, 256, 512], P(None, 'gx', 'gy', 'gz'), may hold values from 0 to 1
Outputs:
- solution_next: float32 [3, 96, 256, 512], P(None, 'gx', 'gy', 'gz')
- residual_next: float32 [3, 96, 256, 512], P(None, 'gx', 'gy', 'gz')
- direction: float32 [3, 96, 256, 512], P(None, 'gx', 'gy', 'gz')
The draws below stay inside these ranges and needn't reach their ends.
All inputs are finite; a program needn't handle non-finite values.
Results may differ from the reference program's by a relative error of at most 0.0003.
Values sent between devices are 32-bit elements; how exact they have to be, the bound alone decides.
No kernel may reach another device: no remote copies, remote signals or barrier semaphores. Data moves between devices by JAX's collectives and lax.ppermute only.
A program may use at most 64 MiB of HBM per device.

```python
import jax
import jax.numpy as jnp

CX = 8
COMP = 3
SWEEPS = 3
BINS = 16
NX = 96
NY = 256
NZ = 512


def draw_residual(key, part):
    key = jax.random.fold_in(key, 11)
    along_x = jnp.arange(NX, dtype=jnp.float32) / (NX - 1)
    along_y = jnp.arange(NY, dtype=jnp.float32) / (NY - 1)
    along_z = jnp.arange(NZ, dtype=jnp.float32) / (NZ - 1)
    smooth = (along_z * along_z)[None, None, :] + 0.0 * along_y[None, :, None]
    base = jnp.clip(jax.random.normal(key, (COMP, NX, NY, NZ), jnp.float32), -4.0, 4.0)
    scale = (1.0 + 2.0 * along_x)[:, None, None] + 0.0 * along_y[None, :, None]
    return (base * scale[None] + smooth[None]).astype(jnp.float32)


def draw_density_bins(key, part):
    key = jax.random.fold_in(key, 23)
    key_flip, key_soft, key_hard = jax.random.split(key, 3)
    flip = jax.random.randint(key_flip, (), 0, 2)
    layer = (jnp.arange(NX, dtype=jnp.int32) // CX + flip) % 2
    softer = jax.random.randint(key_soft, (NX, NY, NZ), 0, 6)
    harder = jax.random.randint(key_hard, (NX, NY, NZ), 10, 16)
    return jnp.where(layer[:, None, None] == 0, softer, harder).astype(jnp.int32)


def draw_fixed_dofs(key, part):
    key = jax.random.fold_in(key, 37)
    level = 1 + 7 * jnp.arange(NZ, dtype=jnp.int32) // (NZ - 1)
    picks = jax.random.randint(key, (COMP, NX, NY, NZ), 0, 16)
    return (picks < level[None, None, None, :]).astype(jnp.int32)


def block_scale(stream_key, extent, pieces, low, high):
    gain, own = 1.0, jax.random.fold_in(stream_key, 6)
    for axis_at, parts in pieces:
        heights = jnp.exp(jax.random.uniform(jax.random.fold_in(own, axis_at), (parts,), jnp.float32, low / len(pieces), high / len(pieces)))
        gain = gain * jnp.repeat(heights, extent[axis_at] // parts).reshape([-1 if axis == axis_at else 1 for axis in range(len(extent))])
    return gain


def centred(key, dims, width, bound, cuts=(), held_as=jnp.bfloat16):
    entries = jax.random.normal(key, dims, jnp.float32) * width
    if len(cuts) > 0:
        entries = block_scale(key, dims, cuts, -0.22, 0.18) * entries
    return jnp.clip(entries, min=-bound, max=bound).astype(held_as)


def setup_inputs(seed: int = 0) -> dict:
    keys = jax.random.split(jax.random.key(seed), 5)
    solution = centred(keys[0], (COMP, NX, NY, NZ), 1.0, 6.0, ((1, 12), (2, 16), (3, 4)), jnp.float32)
    residual = draw_residual(jax.random.fold_in(keys[4], 71), 0)
    density_bins = draw_density_bins(jax.random.fold_in(keys[4], 71), 0)
    fixed_dofs = draw_fixed_dofs(jax.random.fold_in(keys[4], 71), 0)
    return dict(solution=solution, residual=residual, density_bins=density_bins, fixed_dofs=fixed_dofs)


damping = 0.6
eig_center = 1.05
eig_halfwidth = 0.95


def stiffness(density_bins):
    fraction = (density_bins.astype(jnp.float32) + 1.0) / BINS
    return 0.05 + 0.95 * fraction * fraction * fraction


def couplings(padded):
    center = padded[1:-1, 1:-1, 1:-1]

    def shared(other):
        return jnp.where(other > 0.0, 0.5 * (center + other), 0.0)

    upper = jnp.stack([shared(padded[2:, 1:-1, 1:-1]), shared(padded[1:-1, 2:, 1:-1]), shared(padded[1:-1, 1:-1, 2:])])
    lower = jnp.stack([shared(padded[:-2, 1:-1, 1:-1]), shared(padded[1:-1, :-2, 1:-1]), shared(padded[1:-1, 1:-1, :-2])])
    return upper, lower


def level_apply(field, padded, upper, lower, spring):
    total = spring * field
    total = total + upper[0] * (field - padded[:, 2:, 1:-1, 1:-1]) + lower[0] * (field - padded[:, :-2, 1:-1, 1:-1])
    total = total + upper[1] * (field - padded[:, 1:-1, 2:, 1:-1]) + lower[1] * (field - padded[:, 1:-1, :-2, 1:-1])
    total = total + upper[2] * (field - padded[:, 1:-1, 1:-1, 2:]) + lower[2] * (field - padded[:, 1:-1, 1:-1, :-2])
    return total


def level_diagonal(upper, lower, spring):
    return jnp.sum(upper, axis=0) + jnp.sum(lower, axis=0) + spring


def restrict(field):
    channels, size_x, size_y, size_z = field.shape
    return field.reshape(channels, size_x // 2, 2, size_y // 2, 2, size_z // 2, 2).sum(axis=(2, 4, 6))


def prolong(field):
    return jnp.repeat(jnp.repeat(jnp.repeat(field, 2, axis=1), 2, axis=2), 2, axis=3)


def coarse_links(links, offset):
    size_x, size_y, size_z = links.shape[1:]
    along_x = links[0][offset::2].reshape(size_x // 2, size_y // 2, 2, size_z // 2, 2).sum(axis=(2, 4))
    along_y = links[1][:, offset::2].reshape(size_x // 2, 2, size_y // 2, size_z // 2, 2).sum(axis=(1, 4))
    along_z = links[2][:, :, offset::2].reshape(size_x // 2, 2, size_y // 2, 2, size_z // 2).sum(axis=(1, 3))
    return jnp.stack([along_x, along_y, along_z])


def zero_rim(field):
    return jnp.pad(field, ((0, 0), (1, 1), (1, 1), (1, 1)))


def chebyshev(rhs, upper, lower, spring, diagonal, with_rim):
    ratio = eig_center / eig_halfwidth
    factor = 1.0 / ratio
    update = rhs / (eig_center * diagonal)
    iterate = update
    for step_index in range(SWEEPS - 1):
        remainder = rhs - level_apply(iterate, with_rim(iterate), upper, lower, spring)
        next_factor = 1.0 / (2.0 * ratio - factor)
        update = next_factor * factor * update + (2.0 * next_factor / eig_halfwidth) * remainder / diagonal
        iterate = iterate + update
        factor = next_factor
    return iterate


def reference(solution, residual, density_bins, fixed_dofs):
    fixed = fixed_dofs.astype(jnp.float32)
    free = 1.0 - fixed
    modulus = stiffness(density_bins)
    fine_upper, fine_lower = couplings(jnp.pad(modulus, 1))
    fine_spring = 0.1 * modulus
    fine_diag = free * level_diagonal(fine_upper, fine_lower, fine_spring) + fixed

    def fine_apply(field):
        masked = free * field
        return free * level_apply(masked, zero_rim(masked), fine_upper, fine_lower, fine_spring) + fixed * field

    mid_upper = coarse_links(fine_upper, 1)
    mid_lower = coarse_links(fine_lower, 0)
    mid_spring = restrict(fine_spring[None])[0]
    mid_diag = level_diagonal(mid_upper, mid_lower, mid_spring)
    low_upper = coarse_links(mid_upper, 1)
    low_lower = coarse_links(mid_lower, 0)
    low_spring = restrict(mid_spring[None])[0]
    low_diag = level_diagonal(low_upper, low_lower, low_spring)

    fine_corr = damping * residual / fine_diag
    mid_rhs = restrict(residual - fine_apply(fine_corr))
    mid_corr = damping * mid_rhs / mid_diag
    coarse_rhs = restrict(mid_rhs - level_apply(mid_corr, zero_rim(mid_corr), mid_upper, mid_lower, mid_spring))
    coarse_corr = chebyshev(coarse_rhs, low_upper, low_lower, low_spring, low_diag, zero_rim)
    mid_corr = mid_corr + prolong(coarse_corr)
    mid_corr = mid_corr + damping * (mid_rhs - level_apply(mid_corr, zero_rim(mid_corr), mid_upper, mid_lower, mid_spring)) / mid_diag
    fine_corr = fine_corr + prolong(mid_corr)
    direction = fine_corr + damping * (residual - fine_apply(fine_corr)) / fine_diag
    image = fine_apply(direction)
    alpha = jnp.sum(residual * direction) / jnp.sum(direction * image)
    return solution + alpha * direction, residual - alpha * image, direction
```

```python
import functools

import jax
import jax.numpy as jnp
from jax import lax
from jax.experimental import pallas as pl
from jax.experimental.pallas import tpu as pltpu
from jax.sharding import Mesh
from jax.sharding import PartitionSpec as P

BINS = 16
damping = 0.6
keep = 1.0 - damping
eig_center = 1.05
eig_halfwidth = 0.95

F32 = jnp.float32
CX, CY, CZ = 8, 16, 128
LANES = 2 * CZ
ROWS = CY + 16
PLANES = CX + 16
ZH = 16
FIELDS = 7
GYX = CX + 2

VMEM = pl.BlockSpec(memory_space=pltpu.VMEM)
SMEM = pl.BlockSpec(memory_space=pltpu.SMEM)


def call(kernel, outs, scratch=()):
    return pl.pallas_call(
        kernel,
        out_shape=[jax.ShapeDtypeStruct(s, F32) for s in outs],
        out_specs=[VMEM] * len(outs),
        scratch_shapes=[pltpu.VMEM(s, F32) for s in scratch],
        compiler_params=pltpu.CompilerParams(vmem_limit_bytes=48 * 1024 * 1024),
    )


def before(v, k, axis):
    return pltpu.roll(v, k, axis)


def after(v, k, axis):
    return pltpu.roll(v, v.shape[axis] - k, axis)


def lane_of(shape):
    return lax.broadcasted_iota(jnp.int32, shape, len(shape) - 1)


def pair_sum(v, k):
    low = lane_of(v.shape) % (2 * k) < k
    return v + jnp.where(low, after(v, k, 1), before(v, k, 1))


def odd_group(v, k):
    low = lane_of(v.shape) % (2 * k) < k
    return jnp.where(low, after(v, k, 1), v)


def neighbours(ux, ux_prev, uy, uz, here, prev, nxt, k):
    return (
        ux * nxt
        + ux_prev * prev
        + uy * after(here, 1, 0)
        + before(uy * here, 1, 0)
        + uz * after(here, k, 1)
        + before(uz * here, k, 1)
    )


def gather_kernel(density, residual, fixed, main, to_right, to_left):
    lane = lane_of((CY, CZ))

    def stage(field, values):
        right = jnp.zeros((CY, CZ), F32)
        left = jnp.zeros((CY, CZ), F32)
        for x, v in enumerate(values):
            main[field, x] = v
            mine = (lane >= ZH * x) & (lane < ZH * (x + 1))
            right = jnp.where(mine, pltpu.roll(v, (ZH * x + ZH) % CZ, 1), right)
            left = jnp.where(mine, pltpu.roll(v, ZH * x, 1) if x else v, left)
        to_right[field] = right
        to_left[field] = left

    def modulus(bins):
        f = (bins.astype(F32) + 1.0) / BINS
        return 0.05 + 0.95 * f * f * f

    stage(0, [modulus(density[x]) for x in range(CX)])
    for c in range(3):
        stage(1 + c, [residual[c, x] for x in range(CX)])
        stage(4 + c, [1.0 - fixed[c, x].astype(F32) for x in range(CX)])


def restrict_rows(tmp, v):
    n = v.shape[0] // 2
    for h in range(2):
        tmp[h] = v[:, CZ * h : CZ * (h + 1)]
    return [jnp.concatenate([tmp[h, pl.ds(i, n, stride=2), :] for h in range(2)], axis=1) for i in range(2)]


def repeat_rows(tmp, v):
    n = v.shape[0]
    for h in range(2):
        for i in range(2):
            tmp[h, pl.ds(i, n, stride=2), :] = v[:, CZ * h : CZ * (h + 1)]
    return jnp.concatenate([tmp[0], tmp[1]], axis=1)


def fine_kernel(
    ends, x0, xl, xr, yl, yr,
    o_r, o_free, o_ux, o_uy, o_uz, o_ig, o_mc, o_mux, o_muy, o_muz, o_mig, o_right, o_left, o_own,
    ext, ux, uy, uz, mm, mux, muy, muz, mig, mrhs, mc, cx_, cy_, cz_, cg, tmp32, tmp16,
):
    lane = lane_of((CY, CZ))
    lane8 = lane_of((8, CZ))

    def assemble(f, _):
        for b, brick in enumerate((xl, x0, xr)):
            parts = (
                (0, 8, lambda p: yl[f, GYX * b + p], lane8),
                (8, CY, lambda p: brick[f, p], lane),
                (8 + CY, 8, lambda p: yr[f, GYX * b + p], lane8),
            )
            for start, rows, get, at in parts:
                from_left, from_right = get(CX), get(CX + 1)
                for p in range(CX):
                    v = get(p)
                    le = pltpu.roll(from_left, (CZ - ZH - ZH * p) % CZ, 1) if p < 7 else from_left
                    ri = pltpu.roll(from_right, CZ - ZH * p, 1) if p else from_right
                    ext[f, CX * b + p, start : start + rows, 0:CZ] = v
                    ext[f, CX * b + p, start : start + rows, CZ:LANES] = jnp.where(
                        at < ZH, ri, jnp.where(at >= CZ - ZH, le, v)
                    )
        return 0

    lax.fori_loop(0, FIELDS, assemble, 0)

    lo_x, hi_x, lo_y, hi_y, lo_z, hi_z = (ends[i] for i in range(6))
    shape = (ROWS, LANES)
    row = lax.broadcasted_iota(jnp.int32, shape, 0)
    col = lane_of(shape)
    half_y = jnp.where(((row == 7) & (lo_y == 1)) | ((row == 7 + CY) & (hi_y == 1)), 0.0, 0.5)
    half_z = jnp.where(((col == LANES - 1) & (lo_z == 1)) | ((col == CZ - 1) & (hi_z == 1)), 0.0, 0.5)

    def links(p, _):
        here = ext[0, p]
        cut = ((p == 7) & (lo_x == 1)) | ((p == 7 + CX) & (hi_x == 1))
        ux[p] = jnp.where(cut, 0.0, 0.5) * (here + ext[0, jnp.minimum(p + 1, PLANES - 1)])
        uy[p] = half_y * (here + after(here, 1, 0))
        uz[p] = half_z * (here + after(here, 1, 1))
        return 0

    lax.fori_loop(0, PLANES, links, 0)

    def smooth(p, _):
        g = 0.1 * ext[0, p] + ux[p] + ux[p - 1]
        g = g + uy[p] + before(uy[p], 1, 0) + uz[p] + before(uz[p], 1, 1)
        ig = damping / g
        for c in range(3):
            mm[c, p] = ext[4 + c, p] * ext[1 + c, p] * ig

        @pl.when((p >= 6) & (p < 18))
        def _():
            o_ig[p - 6] = ig
            o_ux[p - 6] = ux[p]
            o_uy[p - 6] = uy[p]
            o_uz[p - 6] = uz[p]
            for c in range(3):
                o_r[c, p - 6] = ext[1 + c, p]
                o_free[c, p - 6] = ext[4 + c, p]

        return 0

    lax.fori_loop(1, PLANES - 1, smooth, 0)

    def mid_links(q, _):
        p = 2 * q
        a, b = restrict_rows(tmp32, ux[p + 1])
        mux[q] = pair_sum(a + b, 1)
        _, b = restrict_rows(tmp32, uy[p] + uy[p + 1])
        muy[q] = pair_sum(b, 1)
        a, b = restrict_rows(tmp32, uz[p] + uz[p + 1])
        muz[q] = odd_group(a + b, 1)
        a, b = restrict_rows(tmp32, ext[0, p] + ext[0, p + 1])
        mig[q] = 0.1 * pair_sum(a + b, 1)
        return 0

    lax.fori_loop(0, 12, mid_links, 0)

    def mid_rhs(q, _):
        p = 2 * q
        g = mig[q] + mux[q] + mux[q - 1]
        g = g + muy[q] + before(muy[q], 1, 0) + muz[q] + before(muz[q], 2, 1)
        ig = damping / g
        for c in range(3):
            total = jnp.zeros(shape, F32)
            for i in range(2):
                near = neighbours(ux[p + i], ux[p + i - 1], uy[p + i], uz[p + i], mm[c, p + i], mm[c, p + i - 1], mm[c, p + i + 1], 1)
                total = total + keep * ext[1 + c, p + i] + ext[4 + c, p + i] * near
            a, b = restrict_rows(tmp32, total)
            rhs = pair_sum(a + b, 1)
            mrhs[c, q] = rhs
            mc[c, q] = ig * rhs

        @pl.when((q >= 2) & (q < 10))
        def _():
            o_mig[q - 2] = ig
            o_mux[q - 2] = mux[q]
            o_muy[q - 2] = muy[q]
            o_muz[q - 2] = muz[q]
            for c in range(3):
                o_mc[c, q - 2] = mc[c, q]

        return 0

    lax.fori_loop(1, 11, mid_rhs, 0)

    for s in range(5):
        q = 2 * s
        a, b = restrict_rows(tmp16, mux[q + 1])
        cx_[s] = pair_sum(a + b, 2)
        _, b = restrict_rows(tmp16, muy[q] + muy[q + 1])
        cy_[s] = pair_sum(b, 2)
        a, b = restrict_rows(tmp16, muz[q] + muz[q + 1])
        cz_[s] = odd_group(a + b, 2)
        a, b = restrict_rows(tmp16, mig[q] + mig[q + 1])
        cg[s] = pair_sum(a + b, 2)

    quad = lane_of((8, LANES)) % 4
    for s in range(1, 5):
        g = cg[s] + cx_[s] + cx_[s - 1]
        g = g + cy_[s] + before(cy_[s], 1, 0) + cz_[s] + before(cz_[s], 4, 1)
        rhs = []
        for c in range(3):
            total = jnp.zeros((ROWS // 2, LANES), F32)
            for q in (2 * s, 2 * s + 1):
                near = neighbours(mux[q], mux[q - 1], muy[q], muz[q], mc[c, q], mc[c, q - 1], mc[c, q + 1], 2)
                total = total + keep * mrhs[c, q] + near
            a, b = restrict_rows(tmp16, total)
            rhs.append(pair_sum(a + b, 2))
        first = jnp.where(quad == 0, rhs[0], jnp.where(quad == 1, rhs[1], jnp.where(quad == 2, rhs[2], g)))
        second = jnp.where(quad == 0, cx_[s], jnp.where(quad == 1, cy_[s], cz_[s]))
        for i, v in enumerate((first, second)):
            if s <= 3:
                o_right[i, s - 1] = v
            if s >= 2:
                o_left[i, s - 2] = v
            if s in (2, 3):
                o_own[i, s - 2] = v


def turn_kernel(xl, own, xr, up, down):
    for i in range(2):
        for s in range(8):
            for j in range(3):
                for out, first in ((up, 3), (down, 2)):
                    at = slice(first + j, first + j + 1)
                    src = xl[i, s, at] if s < 3 else own[i, s - 3, at] if s < 5 else xr[i, s - 5, at]
                    out[i, j, s : s + 1] = src


def solve_kernel(
    xl, own, xr, yl, yr, r, free, ux, uy, uz, ig, mc, mux, muy, muz, mig,
    direction, image, sums,
    packed, cc, pm, pf, m1, base, d, tmp16,
):
    quad = lane_of((16, LANES)) % 4
    field = [[None] * 8 for _ in range(7)]
    for i in range(2):
        for s in range(8):
            packed[...] = jnp.zeros((16, LANES), F32)
            packed[4:8] = xl[i, s, 2:6] if s < 3 else own[i, s - 3, 2:6] if s < 5 else xr[i, s - 5, 2:6]
            for j in range(3):
                packed[1 + j : 2 + j] = yl[i, j, s : s + 1]
                packed[8 + j : 9 + j] = yr[i, j, s : s + 1]
            v = packed[...]
            for k in range(4 if i == 0 else 3):
                field[4 * i + k][s] = pair_sum(pair_sum(jnp.where(quad == k, v, 0.0), 1), 2)
    g = [jnp.where(v > 0.0, v, 1.0) for v in field[3]]
    inv = [1.0 / v for v in g]
    cx_, cy_, cz_ = field[4], field[5], field[6]
    ratio = eig_center / eig_halfwidth
    q0 = 1.0 / ratio
    q1 = 1.0 / (2.0 * ratio - q0)
    q2 = 1.0 / (2.0 * ratio - q1)
    for c in range(3):
        rhs = field[c]
        update = [rhs[s] * inv[s] * (1.0 / eig_center) for s in range(8)]
        iterate = list(update)
        for q_old, q_new, lo, hi in ((q0, q1, 1, 7), (q1, q2, 2, 6)):
            new = list(iterate)
            for s in range(lo, hi):
                near = neighbours(cx_[s], cx_[s - 1], cy_[s], cz_[s], iterate[s], iterate[s - 1], iterate[s + 1], 4)
                rest = rhs[s] - g[s] * iterate[s] + near
                update[s] = (q_new * q_old) * update[s] + (2.0 * q_new / eig_halfwidth) * (rest * inv[s])
                new[s] = iterate[s] + update[s]
            iterate = new
        for s in range(4):
            tmp16[...] = iterate[2 + s]
            v = tmp16[2:10]
            v = repeat_rows(cc, v)
            pm[c, 2 * s] = mc[c, 2 * s] + v
            pm[c, 2 * s + 1] = mc[c, 2 * s + 1] + v

    def mid(q, _):
        for c in range(3):
            near = neighbours(mux[q], mux[q - 1], muy[q], muz[q], pm[c, q], pm[c, q - 1], pm[c, q + 1], 2)
            v = keep * pm[c, q] + mc[c, q] + mig[q] * near
            v = repeat_rows(pf, v)
            for i in range(2):
                p = 2 * (q - 1) + i
                fr = free[c, p]
                fc = r[c, p] * (fr * ig[p] + damping * (1.0 - fr))
                corr = fc + v
                m1[c, p] = fr * corr
                base[c, p] = keep * corr + fc
        return 0

    lax.fori_loop(1, 7, mid, 0)

    def fine(p, _):
        for c in range(3):
            near = neighbours(ux[p], ux[p - 1], uy[p], uz[p], m1[c, p], m1[c, p - 1], m1[c, p + 1], 1)
            d[c, p] = base[c, p] + free[c, p] * ig[p] * near
        return 0

    lax.fori_loop(1, 11, fine, 0)

    mine = slice(8, 8 + CY)

    def last(p, total):
        first, second = total
        for c in range(3):
            here = free[c, p] * d[c, p]
            prev = free[c, p - 1] * d[c, p - 1]
            nxt = free[c, p + 1] * d[c, p + 1]
            near = neighbours(ux[p], ux[p - 1], uy[p], uz[p], here, prev, nxt, 1)
            fr = free[c, p]
            im = fr * (damping / ig[p] * d[c, p] - near) + (1.0 - fr) * d[c, p]
            im = im[mine, 0:CZ]
            dd = d[c, p, mine, 0:CZ]
            direction[c, p - 2] = dd
            image[c, p - 2] = im
            first = first + r[c, p, mine, 0:CZ] * dd
            second = second + dd * im
        return first, second

    zero = jnp.zeros((CY, CZ), F32)
    first, second = lax.fori_loop(2, 10, last, (zero, zero))
    sums[0:1] = jnp.sum(first, axis=0, keepdims=True)
    sums[1:2] = jnp.sum(second, axis=0, keepdims=True)


def ring(count, step):
    return [(i, (i + step) % count) for i in range(count)]


def all_sum(v, axes):
    n = 1
    for axis in axes:
        n *= lax.axis_size(axis)
    sent = jnp.broadcast_to(v[None], (n,) + v.shape)
    return lax.all_to_all(sent, axes, 0, 0).sum(axis=0)


def shards(solution, residual, density_bins, fixed_dofs):
    nx, nc, nz = lax.axis_size("gx"), lax.axis_size("gc"), lax.axis_size("gz")
    ny = 2 * nc
    y_axes = ("gc", "co")
    ix, iz = lax.axis_index("gx"), lax.axis_index("gz")
    iy = 2 * lax.axis_index("gc") + lax.axis_index("co")
    ends = jnp.stack([ix == 0, ix == nx - 1, iy == 0, iy == ny - 1, iz == 0, iz == nz - 1]).astype(jnp.int32)

    def both(v, axes, count):
        up, down = v if isinstance(v, tuple) else (v, v)
        return lax.ppermute(up, axes, ring(count, 1)), lax.ppermute(down, axes, ring(count, -1))

    main, to_right, to_left = call(gather_kernel, [(FIELDS, CX, CY, CZ), (FIELDS, CY, CZ), (FIELDS, CY, CZ)])(
        density_bins, residual, fixed_dofs
    )
    zl, zr = both((to_right, to_left), "gz", nz)
    x0 = jnp.concatenate([main, zl[:, None], zr[:, None]], axis=1)
    xl, xr = both(x0, "gx", nx)
    wide = [xl, x0, xr]
    yl, yr = both(
        (
            jnp.concatenate([v[:, :, 8:16] for v in wide], axis=1),
            jnp.concatenate([v[:, :, 0:8] for v in wide], axis=1),
        ),
        y_axes,
        ny,
    )

    full = (12, ROWS, LANES)
    half = (8, ROWS // 2, LANES)
    all_f = (PLANES, ROWS, LANES)
    all_m = (12, ROWS // 2, LANES)
    outs = [(3,) + full, (3,) + full, full, full, full, full, (3,) + half, half, half, half, half]
    outs += [(2, 3, 8, LANES), (2, 3, 8, LANES), (2, 2, 8, LANES)]
    scratch = [(FIELDS,) + all_f, all_f, all_f, all_f, (3,) + all_f, all_m, all_m, all_m, all_m, (3,) + all_m, (3,) + all_m]
    scratch += [(5, 8, LANES)] * 4 + [(2, ROWS, CZ), (2, ROWS // 2, CZ)]
    fine = pl.pallas_call(
        fine_kernel,
        out_shape=[jax.ShapeDtypeStruct(s, F32) for s in outs],
        in_specs=[SMEM] + [VMEM] * 5,
        out_specs=[VMEM] * len(outs),
        scratch_shapes=[pltpu.VMEM(s, F32) for s in scratch],
        compiler_params=pltpu.CompilerParams(vmem_limit_bytes=48 * 1024 * 1024),
    )(ends, x0, xl, xr, yl, yr)
    kept, (to_right, to_left, own) = fine[:-3], fine[-3:]
    cl, cr = both((to_right, to_left), "gx", nx)
    up, down = call(turn_kernel, [(2, 3, 8, LANES)] * 2)(cl, own, cr)
    dl, dr = both((up, down), y_axes, ny)
    direction, image, sums = call(
        solve_kernel,
        [(3, CX, CY, CZ), (3, CX, CY, CZ), (2, CZ)],
        [(16, LANES), (2, ROWS // 2, CZ), (3,) + half, (2, ROWS, CZ), (3,) + full, (3,) + full, (3,) + full, (16, LANES)],
    )(cl, own, cr, dl, dr, *kept)
    sums = jnp.broadcast_to(jnp.sum(sums, axis=1)[:, None, None], (2, 4, CZ)).reshape(8, CZ)
    sums = all_sum(all_sum(sums, ("gc", "gz")), ("gx", "co"))
    alpha = sums[0, 0] / sums[4, 0]
    return (solution + alpha * direction, residual - alpha * image, direction)


def solution(mesh):
    nx, ny, nz = mesh.devices.shape
    split = Mesh(mesh.devices.reshape(nx, ny // 2, 2, nz), ("gx", "gc", "co", "gz"))
    field = P(None, "gx", ("gc", "co"), "gz")
    return jax.shard_map(
        shards,
        mesh=split,
        in_specs=(field, field, P("gx", ("gc", "co"), "gz"), field),
        out_specs=(field, field, field),
        check_vma=False,
    )
```

```python
import functools

import jax
import jax.numpy as jnp
from jax import lax
from jax.experimental import pallas as pl
from jax.experimental.pallas import tpu as pltpu
from jax.sharding import Mesh
from jax.sharding import PartitionSpec as P

BINS = 16
damping = 0.6
keep = 1.0 - damping
eig_center = 1.05
eig_halfwidth = 0.95

F32 = jnp.float32
CX, CY, CZ = 8, 16, 128
LANES = 2 * CZ
ROWS = CY + 16
PLANES = CX + 16
ZH = 16
LIMIT = 20 * 1024 * 1024
FIELDS = 7
GYX = CX + 2

VMEM = pl.BlockSpec(memory_space=pltpu.VMEM)
SMEM = pl.BlockSpec(memory_space=pltpu.SMEM)


def call(kernel, outs, scratch=()):
    return pl.pallas_call(
        kernel,
        out_shape=[jax.ShapeDtypeStruct(s, F32) for s in outs],
        out_specs=[VMEM] * len(outs),
        scratch_shapes=[pltpu.VMEM(s, F32) for s in scratch],
        compiler_params=pltpu.CompilerParams(vmem_limit_bytes=LIMIT),
    )


def before(v, k, axis):
    return pltpu.roll(v, k, axis)


def after(v, k, axis):
    return pltpu.roll(v, v.shape[axis] - k, axis)


def lane_of(shape):
    return lax.broadcasted_iota(jnp.int32, shape, len(shape) - 1)


def pair_sum(v, k):
    low = lane_of(v.shape) % (2 * k) < k
    return v + jnp.where(low, after(v, k, 1), before(v, k, 1))


def odd_group(v, k):
    low = lane_of(v.shape) % (2 * k) < k
    return jnp.where(low, after(v, k, 1), v)


def neighbours(ux, ux_prev, uy, uz, here, prev, nxt, k):
    return (
        ux * nxt
        + ux_prev * prev
        + uy * after(here, 1, 0)
        + before(uy * here, 1, 0)
        + uz * after(here, k, 1)
        + before(uz * here, k, 1)
    )


def gather_kernel(density_in, residual_in, fixed_in, main, to_right, to_left, density, residual, fixed, sems):
    pairs = ((density_in, density), (residual_in, residual), (fixed_in, fixed))
    copies = [pltpu.make_async_copy(a, b, sems.at[i]) for i, (a, b) in enumerate(pairs)]
    for copy in copies:
        copy.start()
    for copy in copies:
        copy.wait()
    lane = lane_of((CY, CZ))

    def stage(field, values):
        right = jnp.zeros((CY, CZ), F32)
        left = jnp.zeros((CY, CZ), F32)
        for x, v in enumerate(values):
            main[field, x] = v
            mine = (lane >= ZH * x) & (lane < ZH * (x + 1))
            right = jnp.where(mine, pltpu.roll(v, (ZH * x + ZH) % CZ, 1), right)
            left = jnp.where(mine, pltpu.roll(v, ZH * x, 1) if x else v, left)
        to_right[field] = right
        to_left[field] = left

    def modulus(bins):
        f = (bins.astype(F32) + 1.0) / BINS
        return 0.05 + 0.95 * f * f * f

    stage(0, [modulus(density[x]) for x in range(CX)])
    for c in range(3):
        stage(1 + c, [residual[c, x] for x in range(CX)])
        stage(4 + c, [1.0 - fixed[c, x].astype(F32) for x in range(CX)])


def restrict_rows(tmp, v):
    n = v.shape[0] // 2
    for h in range(2):
        tmp[h] = v[:, CZ * h : CZ * (h + 1)]
    return [jnp.concatenate([tmp[h, pl.ds(i, n, stride=2), :] for h in range(2)], axis=1) for i in range(2)]


def repeat_rows(tmp, v):
    n = v.shape[0]
    for h in range(2):
        for i in range(2):
            tmp[h, pl.ds(i, n, stride=2), :] = v[:, CZ * h : CZ * (h + 1)]
    return jnp.concatenate([tmp[0], tmp[1]], axis=1)


def fine_kernel(
    ends, x0, xl, xr, yl, yr,
    o_r, o_free, o_ux, o_uy, o_uz, o_ig, o_mc, o_mux, o_muy, o_muz, o_mig, o_right, o_left, o_own,
    ext, ux, uy, uz, mm, mux, muy, muz, mig, mrhs, mc, cx_, cy_, cz_, cg, tmp32, tmp16,
):
    lane = lane_of((CY, CZ))
    lane8 = lane_of((8, CZ))

    def assemble(f, _):
        for b, brick in enumerate((xl, x0, xr)):
            parts = (
                (0, 8, lambda p: yl[f, GYX * b + p], lane8),
                (8, CY, lambda p: brick[f, p], lane),
                (8 + CY, 8, lambda p: yr[f, GYX * b + p], lane8),
            )
            for start, rows, get, at in parts:
                from_left, from_right = get(CX), get(CX + 1)
                for p in range(CX):
                    v = get(p)
                    le = pltpu.roll(from_left, (CZ - ZH - ZH * p) % CZ, 1) if p < 7 else from_left
                    ri = pltpu.roll(from_right, CZ - ZH * p, 1) if p else from_right
                    ext[f, CX * b + p, start : start + rows, 0:CZ] = v
                    ext[f, CX * b + p, start : start + rows, CZ:LANES] = jnp.where(
                        at < ZH, ri, jnp.where(at >= CZ - ZH, le, v)
                    )
        return 0

    lax.fori_loop(0, FIELDS, assemble, 0)

    lo_x, hi_x, lo_y, hi_y, lo_z, hi_z = (ends[i] for i in range(6))
    shape = (ROWS, LANES)
    row = lax.broadcasted_iota(jnp.int32, shape, 0)
    col = lane_of(shape)
    half_y = jnp.where(((row == 7) & (lo_y == 1)) | ((row == 7 + CY) & (hi_y == 1)), 0.0, 0.5)
    half_z = jnp.where(((col == LANES - 1) & (lo_z == 1)) | ((col == CZ - 1) & (hi_z == 1)), 0.0, 0.5)

    def links(p, _):
        here = ext[0, p]
        cut = ((p == 7) & (lo_x == 1)) | ((p == 7 + CX) & (hi_x == 1))
        ux[p] = jnp.where(cut, 0.0, 0.5) * (here + ext[0, jnp.minimum(p + 1, PLANES - 1)])
        uy[p] = half_y * (here + after(here, 1, 0))
        uz[p] = half_z * (here + after(here, 1, 1))
        return 0

    lax.fori_loop(0, PLANES, links, 0)

    def smooth(p, _):
        g = 0.1 * ext[0, p] + ux[p] + ux[p - 1]
        g = g + uy[p] + before(uy[p], 1, 0) + uz[p] + before(uz[p], 1, 1)
        ig = damping / g
        for c in range(3):
            mm[c, p] = ext[4 + c, p] * ext[1 + c, p] * ig

        @pl.when((p >= 6) & (p < 18))
        def _():
            o_ig[p - 6] = ig
            o_ux[p - 6] = ux[p]
            o_uy[p - 6] = uy[p]
            o_uz[p - 6] = uz[p]
            for c in range(3):
                o_r[c, p - 6] = ext[1 + c, p]
                o_free[c, p - 6] = ext[4 + c, p]

        return 0

    lax.fori_loop(1, PLANES - 1, smooth, 0)

    def mid_links(q, _):
        p = 2 * q
        a, b = restrict_rows(tmp32, ux[p + 1])
        mux[q] = pair_sum(a + b, 1)
        _, b = restrict_rows(tmp32, uy[p] + uy[p + 1])
        muy[q] = pair_sum(b, 1)
        a, b = restrict_rows(tmp32, uz[p] + uz[p + 1])
        muz[q] = odd_group(a + b, 1)
        a, b = restrict_rows(tmp32, ext[0, p] + ext[0, p + 1])
        mig[q] = 0.1 * pair_sum(a + b, 1)
        return 0

    lax.fori_loop(0, 12, mid_links, 0)

    def mid_rhs(q, _):
        p = 2 * q
        g = mig[q] + mux[q] + mux[q - 1]
        g = g + muy[q] + before(muy[q], 1, 0) + muz[q] + before(muz[q], 2, 1)
        ig = damping / g
        for c in range(3):
            total = jnp.zeros(shape, F32)
            for i in range(2):
                near = neighbours(ux[p + i], ux[p + i - 1], uy[p + i], uz[p + i], mm[c, p + i], mm[c, p + i - 1], mm[c, p + i + 1], 1)
                total = total + keep * ext[1 + c, p + i] + ext[4 + c, p + i] * near
            a, b = restrict_rows(tmp32, total)
            rhs = pair_sum(a + b, 1)
            mrhs[c, q] = rhs
            mc[c, q] = ig * rhs

        @pl.when((q >= 2) & (q < 10))
        def _():
            o_mig[q - 2] = ig
            o_mux[q - 2] = mux[q]
            o_muy[q - 2] = muy[q]
            o_muz[q - 2] = muz[q]
            for c in range(3):
                o_mc[c, q - 2] = mc[c, q]

        return 0

    lax.fori_loop(1, 11, mid_rhs, 0)

    for s in range(5):
        q = 2 * s
        a, b = restrict_rows(tmp16, mux[q + 1])
        cx_[s] = pair_sum(a + b, 2)
        _, b = restrict_rows(tmp16, muy[q] + muy[q + 1])
        cy_[s] = pair_sum(b, 2)
        a, b = restrict_rows(tmp16, muz[q] + muz[q + 1])
        cz_[s] = odd_group(a + b, 2)
        a, b = restrict_rows(tmp16, mig[q] + mig[q + 1])
        cg[s] = pair_sum(a + b, 2)

    quad = lane_of((8, LANES)) % 4
    for s in range(1, 5):
        g = cg[s] + cx_[s] + cx_[s - 1]
        g = g + cy_[s] + before(cy_[s], 1, 0) + cz_[s] + before(cz_[s], 4, 1)
        rhs = []
        for c in range(3):
            total = jnp.zeros((ROWS // 2, LANES), F32)
            for q in (2 * s, 2 * s + 1):
                near = neighbours(mux[q], mux[q - 1], muy[q], muz[q], mc[c, q], mc[c, q - 1], mc[c, q + 1], 2)
                total = total + keep * mrhs[c, q] + near
            a, b = restrict_rows(tmp16, total)
            rhs.append(pair_sum(a + b, 2))
        first = jnp.where(quad == 0, rhs[0], jnp.where(quad == 1, rhs[1], jnp.where(quad == 2, rhs[2], g)))
        second = jnp.where(quad == 0, cx_[s], jnp.where(quad == 1, cy_[s], cz_[s]))
        for i, v in enumerate((first, second)):
            if s <= 3:
                o_right[i, s - 1] = v
            if s >= 2:
                o_left[i, s - 2] = v
            if s in (2, 3):
                o_own[i, s - 2] = v


def turn_kernel(xl, own, xr, up, down):
    for i in range(2):
        for s in range(8):
            for j in range(3):
                for out, first in ((up, 3), (down, 2)):
                    at = slice(first + j, first + j + 1)
                    src = xl[i, s, at] if s < 3 else own[i, s - 3, at] if s < 5 else xr[i, s - 5, at]
                    out[i, j, s : s + 1] = src


def solve_kernel(
    xl, own, xr, yl, yr, r, free, ux, uy, uz, ig, mc, mux, muy, muz, mig,
    direction, image, sums,
    packed, cc, pm, pf, m1, base, d, tmp16,
):
    quad = lane_of((16, LANES)) % 4
    field = [[None] * 8 for _ in range(7)]
    for i in range(2):
        for s in range(8):
            packed[...] = jnp.zeros((16, LANES), F32)
            packed[4:8] = xl[i, s, 2:6] if s < 3 else own[i, s - 3, 2:6] if s < 5 else xr[i, s - 5, 2:6]
            for j in range(3):
                packed[1 + j : 2 + j] = yl[i, j, s : s + 1]
                packed[8 + j : 9 + j] = yr[i, j, s : s + 1]
            v = packed[...]
            for k in range(4 if i == 0 else 3):
                field[4 * i + k][s] = pair_sum(pair_sum(jnp.where(quad == k, v, 0.0), 1), 2)
    g = [jnp.where(v > 0.0, v, 1.0) for v in field[3]]
    inv = [1.0 / v for v in g]
    cx_, cy_, cz_ = field[4], field[5], field[6]
    ratio = eig_center / eig_halfwidth
    q0 = 1.0 / ratio
    q1 = 1.0 / (2.0 * ratio - q0)
    q2 = 1.0 / (2.0 * ratio - q1)
    for c in range(3):
        rhs = field[c]
        update = [rhs[s] * inv[s] * (1.0 / eig_center) for s in range(8)]
        iterate = list(update)
        for q_old, q_new, lo, hi in ((q0, q1, 1, 7), (q1, q2, 2, 6)):
            new = list(iterate)
            for s in range(lo, hi):
                near = neighbours(cx_[s], cx_[s - 1], cy_[s], cz_[s], iterate[s], iterate[s - 1], iterate[s + 1], 4)
                rest = rhs[s] - g[s] * iterate[s] + near
                update[s] = (q_new * q_old) * update[s] + (2.0 * q_new / eig_halfwidth) * (rest * inv[s])
                new[s] = iterate[s] + update[s]
            iterate = new
        for s in range(4):
            tmp16[...] = iterate[2 + s]
            v = tmp16[2:10]
            v = repeat_rows(cc, v)
            pm[c, 2 * s] = mc[c, 2 * s] + v
            pm[c, 2 * s + 1] = mc[c, 2 * s + 1] + v

    def mid(q, _):
        for c in range(3):
            near = neighbours(mux[q], mux[q - 1], muy[q], muz[q], pm[c, q], pm[c, q - 1], pm[c, q + 1], 2)
            v = keep * pm[c, q] + mc[c, q] + mig[q] * near
            v = repeat_rows(pf, v)
            for i in range(2):
                p = 2 * (q - 1) + i
                fr = free[c, p]
                fc = r[c, p] * (fr * ig[p] + damping * (1.0 - fr))
                corr = fc + v
                m1[c, p] = fr * corr
                base[c, p] = keep * corr + fc
        return 0

    lax.fori_loop(1, 7, mid, 0)

    def fine(p, _):
        for c in range(3):
            near = neighbours(ux[p], ux[p - 1], uy[p], uz[p], m1[c, p], m1[c, p - 1], m1[c, p + 1], 1)
            d[c, p] = base[c, p] + free[c, p] * ig[p] * near
        return 0

    lax.fori_loop(1, 11, fine, 0)

    mine = slice(8, 8 + CY)

    def last(p, total):
        first, second = total
        for c in range(3):
            here = free[c, p] * d[c, p]
            prev = free[c, p - 1] * d[c, p - 1]
            nxt = free[c, p + 1] * d[c, p + 1]
            near = neighbours(ux[p], ux[p - 1], uy[p], uz[p], here, prev, nxt, 1)
            fr = free[c, p]
            im = fr * (damping / ig[p] * d[c, p] - near) + (1.0 - fr) * d[c, p]
            im = im[mine, 0:CZ]
            dd = d[c, p, mine, 0:CZ]
            direction[c, p - 2] = dd
            image[c, p - 2] = im
            first = first + r[c, p, mine, 0:CZ] * dd
            second = second + dd * im
        return first, second

    zero = jnp.zeros((CY, CZ), F32)
    first, second = lax.fori_loop(2, 10, last, (zero, zero))
    sums[0:1] = jnp.full((1, CZ), jnp.sum(first), F32)
    sums[1:2] = jnp.full((1, CZ), jnp.sum(second), F32)


def ring(count, step):
    return [(i, (i + step) % count) for i in range(count)]


def all_sum(v, axes):
    n = 1
    for axis in axes:
        n *= lax.axis_size(axis)
    sent = jnp.broadcast_to(v[None], (n,) + v.shape)
    return lax.all_to_all(sent, axes, 0, 0).sum(axis=0)


def shards(solution, residual, density_bins, fixed_dofs):
    nx, nc, nz = lax.axis_size("gx"), lax.axis_size("gc"), lax.axis_size("gz")
    ny = 2 * nc
    y_axes = ("gc", "co")
    ix, iz = lax.axis_index("gx"), lax.axis_index("gz")
    iy = 2 * lax.axis_index("gc") + lax.axis_index("co")
    ends = jnp.stack([ix == 0, ix == nx - 1, iy == 0, iy == ny - 1, iz == 0, iz == nz - 1]).astype(jnp.int32)

    def both(v, axes, count):
        up, down = v if isinstance(v, tuple) else (v, v)
        return lax.ppermute(up, axes, ring(count, 1)), lax.ppermute(down, axes, ring(count, -1))

    shapes = [(FIELDS, CX, CY, CZ), (FIELDS, CY, CZ), (FIELDS, CY, CZ)]
    main, to_right, to_left = pl.pallas_call(
        gather_kernel,
        out_shape=[jax.ShapeDtypeStruct(s, F32) for s in shapes],
        in_specs=[pl.BlockSpec(memory_space=pltpu.HBM)] * 3,
        out_specs=[VMEM] * 3,
        scratch_shapes=[
            pltpu.VMEM((CX, CY, CZ), jnp.int32),
            pltpu.VMEM((3, CX, CY, CZ), F32),
            pltpu.VMEM((3, CX, CY, CZ), jnp.int32),
            pltpu.SemaphoreType.DMA((3,)),
        ],
        compiler_params=pltpu.CompilerParams(vmem_limit_bytes=LIMIT),
    )(density_bins, residual, fixed_dofs)
    zl, zr = both((to_right, to_left), "gz", nz)
    x0 = jnp.concatenate([main, zl[:, None], zr[:, None]], axis=1)
    xl, xr = both(x0, "gx", nx)
    wide = [xl, x0, xr]
    yl, yr = both(
        (
            jnp.concatenate([v[:, :, 8:16] for v in wide], axis=1),
            jnp.concatenate([v[:, :, 0:8] for v in wide], axis=1),
        ),
        y_axes,
        ny,
    )

    full = (12, ROWS, LANES)
    half = (8, ROWS // 2, LANES)
    all_f = (PLANES, ROWS, LANES)
    all_m = (12, ROWS // 2, LANES)
    outs = [(3,) + full, (3,) + full, full, full, full, full, (3,) + half, half, half, half, half]
    outs += [(2, 3, 8, LANES), (2, 3, 8, LANES), (2, 2, 8, LANES)]
    scratch = [(FIELDS,) + all_f, all_f, all_f, all_f, (3,) + all_f, all_m, all_m, all_m, all_m, (3,) + all_m, (3,) + all_m]
    scratch += [(5, 8, LANES)] * 4 + [(2, ROWS, CZ), (2, ROWS // 2, CZ)]
    fine = pl.pallas_call(
        fine_kernel,
        out_shape=[jax.ShapeDtypeStruct(s, F32) for s in outs],
        in_specs=[SMEM] + [VMEM] * 5,
        out_specs=[VMEM] * len(outs),
        scratch_shapes=[pltpu.VMEM(s, F32) for s in scratch],
        compiler_params=pltpu.CompilerParams(vmem_limit_bytes=LIMIT),
    )(ends, x0, xl, xr, yl, yr)
    kept, (to_right, to_left, own) = fine[:-3], fine[-3:]
    cl, cr = both((to_right, to_left), "gx", nx)
    up, down = call(turn_kernel, [(2, 3, 8, LANES)] * 2)(cl, own, cr)
    dl, dr = both((up, down), y_axes, ny)
    direction, image, sums = call(
        solve_kernel,
        [(3, CX, CY, CZ), (3, CX, CY, CZ), (2, CZ)],
        [(16, LANES), (2, ROWS // 2, CZ), (3,) + half, (2, ROWS, CZ), (3,) + full, (3,) + full, (3,) + full, (16, LANES)],
    )(cl, own, cr, dl, dr, *kept)
    sums = all_sum(all_sum(sums, ("gc", "gz")), ("gx", "co"))
    alpha = (sums[0] / sums[1])[None, None, None]
    return (solution + alpha * direction, residual - alpha * image, direction)


def solution(mesh):
    nx, ny, nz = mesh.devices.shape
    split = Mesh(mesh.devices.reshape(nx, ny // 2, 2, nz), ("gx", "gc", "co", "gz"))
    field = P(None, "gx", ("gc", "co"), "gz")
    return jax.shard_map(
        shards,
        mesh=split,
        in_specs=(field, field, P("gx", ("gc", "co"), "gz"), field),
        out_specs=(field, field, field),
        check_vma=False,
    )
```

```python
import functools

import jax
import jax.numpy as jnp
from jax import lax
from jax.experimental import pallas as pl
from jax.experimental.pallas import tpu as pltpu
from jax.sharding import Mesh
from jax.sharding import PartitionSpec as P

BINS = 16
damping = 0.6
keep = 1.0 - damping
eig_center = 1.05
eig_halfwidth = 0.95

F32 = jnp.float32
CX, CY, CZ = 8, 16, 128
LANES = 2 * CZ
ROWS = CY + 16
PLANES = CX + 16
ZH = 16
LIMIT = 20 * 1024 * 1024
FIELDS = 7
GYX = CX + 2

VMEM = pl.BlockSpec(memory_space=pltpu.VMEM)
SMEM = pl.BlockSpec(memory_space=pltpu.SMEM)


def call(kernel, outs, scratch=()):
    return pl.pallas_call(
        kernel,
        out_shape=[jax.ShapeDtypeStruct(s, F32) for s in outs],
        out_specs=[VMEM] * len(outs),
        scratch_shapes=[pltpu.VMEM(s, F32) for s in scratch],
        compiler_params=pltpu.CompilerParams(vmem_limit_bytes=LIMIT),
    )


def before(v, k, axis):
    return pltpu.roll(v, k, axis)


def after(v, k, axis):
    return pltpu.roll(v, v.shape[axis] - k, axis)


def lane_of(shape):
    return lax.broadcasted_iota(jnp.int32, shape, len(shape) - 1)


def pair_sum(v, k):
    low = lane_of(v.shape) % (2 * k) < k
    return v + jnp.where(low, after(v, k, 1), before(v, k, 1))


def odd_group(v, k):
    low = lane_of(v.shape) % (2 * k) < k
    return jnp.where(low, after(v, k, 1), v)


def neighbours(ux, ux_prev, uy, uz, here, prev, nxt, k):
    return (
        ux * nxt
        + ux_prev * prev
        + uy * after(here, 1, 0)
        + before(uy * here, 1, 0)
        + uz * after(here, k, 1)
        + before(uz * here, k, 1)
    )


def gather_kernel(density, residual, fixed, main, to_right, to_left):
    lane = lane_of((CY, CZ))

    def stage(field, values):
        right = jnp.zeros((CY, CZ), F32)
        left = jnp.zeros((CY, CZ), F32)
        for x, v in enumerate(values):
            main[field, x] = v
            mine = (lane >= ZH * x) & (lane < ZH * (x + 1))
            right = jnp.where(mine, pltpu.roll(v, (ZH * x + ZH) % CZ, 1), right)
            left = jnp.where(mine, pltpu.roll(v, ZH * x, 1) if x else v, left)
        to_right[field] = right
        to_left[field] = left

    def modulus(bins):
        f = (bins.astype(F32) + 1.0) / BINS
        return 0.05 + 0.95 * f * f * f

    stage(0, [modulus(density[x]) for x in range(CX)])
    for c in range(3):
        stage(1 + c, [residual[c, x] for x in range(CX)])
        stage(4 + c, [1.0 - fixed[c, x].astype(F32) for x in range(CX)])


def steps(start, stop, each, body):
    def step(i, _):
        for j in range(each):
            body(start + each * i + j)
        return 0

    lax.fori_loop(0, (stop - start) // each, step, 0)


def restrict_rows(tmp, v):
    n = v.shape[0] // 2
    for h in range(2):
        tmp[h] = v[:, CZ * h : CZ * (h + 1)]
    return [jnp.concatenate([tmp[h, pl.ds(i, n, stride=2), :] for h in range(2)], axis=1) for i in range(2)]


def repeat_rows(tmp, v):
    n = v.shape[0]
    for h in range(2):
        for i in range(2):
            tmp[h, pl.ds(i, n, stride=2), :] = v[:, CZ * h : CZ * (h + 1)]
    return jnp.concatenate([tmp[0], tmp[1]], axis=1)


def fine_kernel(
    ends, xl, x0, xr, yll, yl0, ylr, yrl, yr0, yrr,
    ext, ux, uy, uz, inv, mux, muy, muz, mig, mc, o_right, o_left, o_own,
    mm, spring, mrhs, cx_, cy_, cz_, cg, tmp32, tmp16,
):
    lane = lane_of((CY, CZ))
    lane8 = lane_of((8, CZ))

    def assemble(f, _):
        for b, (lower, brick, upper) in enumerate(((yll, xl, yrl), (yl0, x0, yr0), (ylr, xr, yrr))):
            parts = (
                (0, 8, lambda p: lower[f, p], lane8),
                (8, CY, lambda p: brick[f, p], lane),
                (8 + CY, 8, lambda p: upper[f, p], lane8),
            )
            for start, rows, get, at in parts:
                from_left, from_right = get(CX), get(CX + 1)
                for p in range(CX):
                    v = get(p)
                    le = pltpu.roll(from_left, (CZ - ZH - ZH * p) % CZ, 1) if p < 7 else from_left
                    ri = pltpu.roll(from_right, CZ - ZH * p, 1) if p else from_right
                    ext[f, CX * b + p, start : start + rows, 0:CZ] = v
                    ext[f, CX * b + p, start : start + rows, CZ:LANES] = jnp.where(
                        at < ZH, ri, jnp.where(at >= CZ - ZH, le, v)
                    )
        return 0

    lax.fori_loop(0, FIELDS, assemble, 0)

    lo_x, hi_x, lo_y, hi_y, lo_z, hi_z = (ends[i] for i in range(6))
    shape = (ROWS, LANES)
    row = lax.broadcasted_iota(jnp.int32, shape, 0)
    col = lane_of(shape)
    half_y = jnp.where(((row == 7) & (lo_y == 1)) | ((row == 7 + CY) & (hi_y == 1)), 0.0, 0.5)
    half_z = jnp.where(((col == LANES - 1) & (lo_z == 1)) | ((col == CZ - 1) & (hi_z == 1)), 0.0, 0.5)

    def links(p):
        here = ext[0, p]
        cut = ((p == 7) & (lo_x == 1)) | ((p == 7 + CX) & (hi_x == 1))
        ux[p] = jnp.where(cut, 0.0, 0.5) * (here + ext[0, jnp.minimum(p + 1, PLANES - 1)])
        uy[p] = half_y * (here + after(here, 1, 0))
        uz[p] = half_z * (here + after(here, 1, 1))

    steps(0, PLANES, 4, links)

    def smooth(p):
        g = 0.1 * ext[0, p] + ux[p] + ux[p - 1]
        g = g + uy[p] + before(uy[p], 1, 0) + uz[p] + before(uz[p], 1, 1)
        ig = damping / g
        inv[p] = ig
        for c in range(3):
            mm[c, p] = ext[4 + c, p] * ext[1 + c, p] * ig

    steps(1, PLANES - 1, 2, smooth)

    def mid_links(q, tmp32=tmp32):
        p = 2 * q
        a, b = restrict_rows(tmp32, ux[p + 1])
        mux[q] = pair_sum(a + b, 1)
        _, b = restrict_rows(tmp32, uy[p] + uy[p + 1])
        muy[q] = pair_sum(b, 1)
        a, b = restrict_rows(tmp32, uz[p] + uz[p + 1])
        muz[q] = odd_group(a + b, 1)
        a, b = restrict_rows(tmp32, ext[0, p] + ext[0, p + 1])
        spring[q] = 0.1 * pair_sum(a + b, 1)

    steps(0, 12, 2, mid_links)

    def mid_rhs(q):
        p = 2 * q
        g = spring[q] + mux[q] + mux[q - 1]
        g = g + muy[q] + before(muy[q], 1, 0) + muz[q] + before(muz[q], 2, 1)
        ig = damping / g
        mig[q] = ig
        for c in range(3):
            total = jnp.zeros(shape, F32)
            for i in range(2):
                near = neighbours(ux[p + i], ux[p + i - 1], uy[p + i], uz[p + i], mm[c, p + i], mm[c, p + i - 1], mm[c, p + i + 1], 1)
                total = total + keep * ext[1 + c, p + i] + ext[4 + c, p + i] * near
            a, b = restrict_rows(tmp32, total)
            rhs = pair_sum(a + b, 1)
            mrhs[c, q] = rhs
            mc[c, q] = ig * rhs

    steps(1, 11, 2, mid_rhs)

    for s in range(5):
        q = 2 * s
        a, b = restrict_rows(tmp16, mux[q + 1])
        cx_[s] = pair_sum(a + b, 2)
        _, b = restrict_rows(tmp16, muy[q] + muy[q + 1])
        cy_[s] = pair_sum(b, 2)
        a, b = restrict_rows(tmp16, muz[q] + muz[q + 1])
        cz_[s] = odd_group(a + b, 2)
        a, b = restrict_rows(tmp16, spring[q] + spring[q + 1])
        cg[s] = pair_sum(a + b, 2)

    quad = lane_of((8, LANES)) % 4
    for s in range(1, 5):
        g = cg[s] + cx_[s] + cx_[s - 1]
        g = g + cy_[s] + before(cy_[s], 1, 0) + cz_[s] + before(cz_[s], 4, 1)
        rhs = []
        for c in range(3):
            total = jnp.zeros((ROWS // 2, LANES), F32)
            for q in (2 * s, 2 * s + 1):
                near = neighbours(mux[q], mux[q - 1], muy[q], muz[q], mc[c, q], mc[c, q - 1], mc[c, q + 1], 2)
                total = total + keep * mrhs[c, q] + near
            a, b = restrict_rows(tmp16, total)
            rhs.append(pair_sum(a + b, 2))
        first = jnp.where(quad == 0, rhs[0], jnp.where(quad == 1, rhs[1], jnp.where(quad == 2, rhs[2], g)))
        second = jnp.where(quad == 0, cx_[s], jnp.where(quad == 1, cy_[s], cz_[s]))
        for i, v in enumerate((first, second)):
            if s <= 3:
                o_right[i, s - 1] = v
            if s >= 2:
                o_left[i, s - 2] = v
            if s in (2, 3):
                o_own[i, s - 2] = v


def turn_kernel(xl, own, xr, up, down):
    for i in range(2):
        for s in range(8):
            for j in range(3):
                for out, first in ((up, 3), (down, 2)):
                    at = slice(first + j, first + j + 1)
                    src = xl[i, s, at] if s < 3 else own[i, s - 3, at] if s < 5 else xr[i, s - 5, at]
                    out[i, j, s : s + 1] = src


def solve_kernel(
    xl, own, xr, yl, yr, ext, ux_, uy_, uz_, ig_, mux_, muy_, muz_, mig_, mc_,
    direction, image, sums,
    packed, cc, pm, pf, m1, base, d, tmp16,
):
    r, free = ext.at[1:4, 6:18], ext.at[4:7, 6:18]
    ux, uy, uz, ig = (a.at[6:18] for a in (ux_, uy_, uz_, ig_))
    mux, muy, muz, mig, mc = *(a.at[2:10] for a in (mux_, muy_, muz_, mig_)), mc_.at[:, 2:10]
    quad = lane_of((16, LANES)) % 4
    field = [[None] * 8 for _ in range(7)]
    for i in range(2):
        for s in range(8):
            packed[...] = jnp.zeros((16, LANES), F32)
            packed[4:8] = xl[i, s, 2:6] if s < 3 else own[i, s - 3, 2:6] if s < 5 else xr[i, s - 5, 2:6]
            for j in range(3):
                packed[1 + j : 2 + j] = yl[i, j, s : s + 1]
                packed[8 + j : 9 + j] = yr[i, j, s : s + 1]
            v = packed[...]
            for k in range(4 if i == 0 else 3):
                field[4 * i + k][s] = pair_sum(pair_sum(jnp.where(quad == k, v, 0.0), 1), 2)
    g = [jnp.where(v > 0.0, v, 1.0) for v in field[3]]
    inv = [1.0 / v for v in g]
    cx_, cy_, cz_ = field[4], field[5], field[6]
    ratio = eig_center / eig_halfwidth
    q0 = 1.0 / ratio
    q1 = 1.0 / (2.0 * ratio - q0)
    q2 = 1.0 / (2.0 * ratio - q1)
    for c in range(3):
        rhs = field[c]
        update = [rhs[s] * inv[s] * (1.0 / eig_center) for s in range(8)]
        iterate = list(update)
        for q_old, q_new, lo, hi in ((q0, q1, 1, 7), (q1, q2, 2, 6)):
            new = list(iterate)
            for s in range(lo, hi):
                near = neighbours(cx_[s], cx_[s - 1], cy_[s], cz_[s], iterate[s], iterate[s - 1], iterate[s + 1], 4)
                rest = rhs[s] - g[s] * iterate[s] + near
                update[s] = (q_new * q_old) * update[s] + (2.0 * q_new / eig_halfwidth) * (rest * inv[s])
                new[s] = iterate[s] + update[s]
            iterate = new
        for s in range(4):
            tmp16[...] = iterate[2 + s]
            v = tmp16[2:10]
            v = repeat_rows(cc, v)
            pm[c, 2 * s] = mc[c, 2 * s] + v
            pm[c, 2 * s + 1] = mc[c, 2 * s + 1] + v

    def mid(q, _):
        for c in range(3):
            near = neighbours(mux[q], mux[q - 1], muy[q], muz[q], pm[c, q], pm[c, q - 1], pm[c, q + 1], 2)
            v = keep * pm[c, q] + mc[c, q] + mig[q] * near
            v = repeat_rows(pf, v)
            for i in range(2):
                p = 2 * (q - 1) + i
                fr = free[c, p]
                fc = r[c, p] * (fr * ig[p] + damping * (1.0 - fr))
                corr = fc + v
                m1[c, p] = fr * corr
                base[c, p] = keep * corr + fc
        return 0

    lax.fori_loop(1, 7, mid, 0)

    def fine(p, _):
        for c in range(3):
            near = neighbours(ux[p], ux[p - 1], uy[p], uz[p], m1[c, p], m1[c, p - 1], m1[c, p + 1], 1)
            d[c, p] = base[c, p] + free[c, p] * ig[p] * near
        return 0

    lax.fori_loop(1, 11, fine, 0)

    mine = slice(8, 8 + CY)

    def last(p, total):
        first, second = total
        for c in range(3):
            here = free[c, p] * d[c, p]
            prev = free[c, p - 1] * d[c, p - 1]
            nxt = free[c, p + 1] * d[c, p + 1]
            near = neighbours(ux[p], ux[p - 1], uy[p], uz[p], here, prev, nxt, 1)
            fr = free[c, p]
            im = fr * (damping / ig[p] * d[c, p] - near) + (1.0 - fr) * d[c, p]
            im = im[mine, 0:CZ]
            dd = d[c, p, mine, 0:CZ]
            direction[c, p - 2] = dd
            image[c, p - 2] = im
            first = first + r[c, p, mine, 0:CZ] * dd
            second = second + dd * im
        return first, second

    zero = jnp.zeros((CY, CZ), F32)
    first, second = lax.fori_loop(2, 10, last, (zero, zero))
    sums[0:1] = jnp.full((1, CZ), jnp.sum(first), F32)
    sums[1:2] = jnp.full((1, CZ), jnp.sum(second), F32)


def ring(count, step):
    return [(i, (i + step) % count) for i in range(count)]


def all_sum(v, axes):
    n = 1
    for axis in axes:
        n *= lax.axis_size(axis)
    sent = jnp.broadcast_to(v[None], (n,) + v.shape)
    return lax.all_to_all(sent, axes, 0, 0).sum(axis=0)


def shards(solution, residual, density_bins, fixed_dofs):
    nx, nc, nz = lax.axis_size("gx"), lax.axis_size("gc"), lax.axis_size("gz")
    ny = 2 * nc
    y_axes = ("gc", "co")
    ix, iz = lax.axis_index("gx"), lax.axis_index("gz")
    iy = 2 * lax.axis_index("gc") + lax.axis_index("co")
    ends = jnp.stack([ix == 0, ix == nx - 1, iy == 0, iy == ny - 1, iz == 0, iz == nz - 1]).astype(jnp.int32)

    def both(v, axes, count):
        up, down = v if isinstance(v, tuple) else (v, v)
        return lax.ppermute(up, axes, ring(count, 1)), lax.ppermute(down, axes, ring(count, -1))

    main, to_right, to_left = call(gather_kernel, [(FIELDS, CX, CY, CZ), (FIELDS, CY, CZ), (FIELDS, CY, CZ)])(
        density_bins, residual, fixed_dofs
    )
    zl, zr = both((to_right, to_left), "gz", nz)
    x0 = jnp.concatenate([main, zl[:, None], zr[:, None]], axis=1)
    xl, xr = both(x0, "gx", nx)
    halves = [both((v[:, :, 8:16], v[:, :, 0:8]), y_axes, ny) for v in (xl, x0, xr)]
    yl, yr = zip(*halves)

    full = (12, ROWS, LANES)
    half = (8, ROWS // 2, LANES)
    all_f = (PLANES, ROWS, LANES)
    all_m = (12, ROWS // 2, LANES)
    outs = [(FIELDS,) + all_f, all_f, all_f, all_f, all_f, all_m, all_m, all_m, all_m, (3,) + all_m]
    outs += [(2, 3, 8, LANES), (2, 3, 8, LANES), (2, 2, 8, LANES)]
    scratch = [(3,) + all_f, all_m, (3,) + all_m]
    scratch += [(5, 8, LANES)] * 4 + [(2, ROWS, CZ), (2, ROWS // 2, CZ)]
    fine = pl.pallas_call(
        fine_kernel,
        out_shape=[jax.ShapeDtypeStruct(s, F32) for s in outs],
        in_specs=[SMEM] + [VMEM] * 9,
        out_specs=[VMEM] * len(outs),
        scratch_shapes=[pltpu.VMEM(s, F32) for s in scratch],
        compiler_params=pltpu.CompilerParams(vmem_limit_bytes=LIMIT),
    )(ends, xl, x0, xr, *yl, *yr)
    kept, (to_right, to_left, own) = fine[:-3], fine[-3:]
    cl, cr = both((to_right, to_left), "gx", nx)
    up, down = call(turn_kernel, [(2, 3, 8, LANES)] * 2)(cl, own, cr)
    dl, dr = both((up, down), y_axes, ny)
    direction, image, sums = call(
        solve_kernel,
        [(3, CX, CY, CZ), (3, CX, CY, CZ), (2, CZ)],
        [(16, LANES), (2, ROWS // 2, CZ), (3,) + half, (2, ROWS, CZ), (3,) + full, (3,) + full, (3,) + full, (16, LANES)],
    )(cl, own, cr, dl, dr, *kept)
    sums = all_sum(all_sum(sums, ("gc", "gz")), ("gx", "co"))
    alpha = (sums[0] / sums[1])[None, None, None]
    return (solution + alpha * direction, residual - alpha * image, direction)


def solution(mesh):
    nx, ny, nz = mesh.devices.shape
    split = Mesh(mesh.devices.reshape(nx, ny // 2, 2, nz), ("gx", "gc", "co", "gz"))
    field = P(None, "gx", ("gc", "co"), "gz")
    return jax.shard_map(
        shards,
        mesh=split,
        in_specs=(field, field, P("gx", ("gc", "co"), "gz"), field),
        out_specs=(field, field, field),
        check_vma=False,
    )
```

```python
import functools

import jax
import jax.numpy as jnp
from jax import lax
from jax.experimental import pallas as pl
from jax.experimental.pallas import tpu as pltpu
from jax.sharding import Mesh
from jax.sharding import PartitionSpec as P

BINS = 16
damping = 0.6
keep = 1.0 - damping
eig_center = 1.05
eig_halfwidth = 0.95

F32 = jnp.float32
CX, CY, CZ = 8, 16, 128
LANES = 2 * CZ
ROWS = CY + 16
PLANES = CX + 16
ZH = 16
LIMIT = 20 * 1024 * 1024
FIELDS = 7

VMEM = pl.BlockSpec(memory_space=pltpu.VMEM)
SMEM = pl.BlockSpec(memory_space=pltpu.SMEM)


def call(kernel, outs, scratch=()):
    return pl.pallas_call(
        kernel,
        out_shape=[jax.ShapeDtypeStruct(s, F32) for s in outs],
        out_specs=[VMEM] * len(outs),
        scratch_shapes=[pltpu.VMEM(s, F32) for s in scratch],
        compiler_params=pltpu.CompilerParams(vmem_limit_bytes=LIMIT),
    )


def before(v, k, axis):
    return pltpu.roll(v, k, axis)


def after(v, k, axis):
    return pltpu.roll(v, v.shape[axis] - k, axis)


def lane_of(shape):
    return lax.broadcasted_iota(jnp.int32, shape, len(shape) - 1)


def pair_sum(v, k):
    low = lane_of(v.shape) % (2 * k) < k
    return v + jnp.where(low, after(v, k, 1), before(v, k, 1))


def odd_group(v, k):
    low = lane_of(v.shape) % (2 * k) < k
    return jnp.where(low, after(v, k, 1), v)


def neighbours(ux, ux_prev, uy, uz, here, prev, nxt, k):
    return (
        ux * nxt
        + ux_prev * prev
        + uy * after(here, 1, 0)
        + before(uy * here, 1, 0)
        + uz * after(here, k, 1)
        + before(uz * here, k, 1)
    )


def gather_kernel(density, residual, fixed, main, up, down):
    f = (density[...].astype(F32) + 1.0) / BINS
    main[0] = 0.05 + 0.95 * f * f * f
    main[1:4] = residual[...]
    main[4:7] = 1.0 - fixed[...].astype(F32)
    up[...] = main[:, :, 8:16]
    down[...] = main[:, :, 0:8]


def edge_kernel(xl, x0, xr, to_right, to_left, up_l, down_l, up_r, down_r):
    lane = lane_of((CY, CZ))

    def field(f, _):
        for b, brick in enumerate((xl, x0, xr)):
            right = jnp.zeros((CY, CZ), F32)
            left = jnp.zeros((CY, CZ), F32)
            for p in range(CX):
                v = brick[f, p]
                mine = (lane >= ZH * p) & (lane < ZH * (p + 1))
                right = jnp.where(mine, pltpu.roll(v, (ZH * p + ZH) % CZ, 1) if p < 7 else v, right)
                left = jnp.where(mine, pltpu.roll(v, ZH * p, 1) if p else v, left)
            to_right[f, b] = right
            to_left[f, b] = left
        for brick, up, down in ((xl, up_l, down_l), (xr, up_r, down_r)):
            up[f] = brick[f, :, 8:16]
            down[f] = brick[f, :, 0:8]
        return 0

    lax.fori_loop(0, FIELDS, field, 0)


def half_kernel(zl, zr, up, down):
    for i, v in enumerate((zl, zr)):
        up[:, 3 * i : 3 * i + 3] = v[:, :, 8:16]
        down[:, 3 * i : 3 * i + 3] = v[:, :, 0:8]


def steps(start, stop, each, body):
    def step(i, _):
        for j in range(each):
            body(start + each * i + j)
        return 0

    lax.fori_loop(0, (stop - start) // each, step, 0)


def restrict_rows(tmp, v):
    n = v.shape[0] // 2
    for h in range(2):
        tmp[h] = v[:, CZ * h : CZ * (h + 1)]
    return [jnp.concatenate([tmp[h, pl.ds(i, n, stride=2), :] for h in range(2)], axis=1) for i in range(2)]


def repeat_rows(tmp, v):
    n = v.shape[0]
    for h in range(2):
        for i in range(2):
            tmp[h, pl.ds(i, n, stride=2), :] = v[:, CZ * h : CZ * (h + 1)]
    return jnp.concatenate([tmp[0], tmp[1]], axis=1)


def fine_kernel(
    ends, xl, x0, xr, yll, yl0, ylr, yrl, yr0, yrr, zl, zr, zlower, zupper,
    ext, ux, uy, uz, inv, mux, muy, muz, mig, mc, o_right, o_left, o_own,
    mm, spring, mrhs, cx_, cy_, cz_, cg, tmp32, tmp16,
):
    lane = lane_of((CY, CZ))
    lane8 = lane_of((8, CZ))

    def assemble(f, _):
        for b, (lower, brick, upper) in enumerate(((yll, xl, yrl), (yl0, x0, yr0), (ylr, xr, yrr))):
            parts = (
                (0, 8, lower, zlower[f, b], zlower[f, 3 + b], lane8),
                (8, CY, brick, zl[f, b], zr[f, b], lane),
                (8 + CY, 8, upper, zupper[f, b], zupper[f, 3 + b], lane8),
            )
            for start, rows, src, from_left, from_right, at in parts:
                for p in range(CX):
                    v = src[f, p]
                    le = pltpu.roll(from_left, (CZ - ZH - ZH * p) % CZ, 1) if p < 7 else from_left
                    ri = pltpu.roll(from_right, CZ - ZH * p, 1) if p else from_right
                    ext[f, CX * b + p, start : start + rows, 0:CZ] = v
                    ext[f, CX * b + p, start : start + rows, CZ:LANES] = jnp.where(
                        at < ZH, ri, jnp.where(at >= CZ - ZH, le, v)
                    )
        return 0

    lax.fori_loop(0, FIELDS, assemble, 0)

    lo_x, hi_x, lo_y, hi_y, lo_z, hi_z = (ends[i] for i in range(6))
    shape = (ROWS, LANES)
    row = lax.broadcasted_iota(jnp.int32, shape, 0)
    col = lane_of(shape)
    half_y = jnp.where(((row == 7) & (lo_y == 1)) | ((row == 7 + CY) & (hi_y == 1)), 0.0, 0.5)
    half_z = jnp.where(((col == LANES - 1) & (lo_z == 1)) | ((col == CZ - 1) & (hi_z == 1)), 0.0, 0.5)

    def links(p):
        here = ext[0, p]
        cut = ((p == 7) & (lo_x == 1)) | ((p == 7 + CX) & (hi_x == 1))
        ux[p] = jnp.where(cut, 0.0, 0.5) * (here + ext[0, jnp.minimum(p + 1, PLANES - 1)])
        uy[p] = half_y * (here + after(here, 1, 0))
        uz[p] = half_z * (here + after(here, 1, 1))

    steps(0, PLANES, 4, links)

    def smooth(p):
        g = 0.1 * ext[0, p] + ux[p] + ux[p - 1]
        g = g + uy[p] + before(uy[p], 1, 0) + uz[p] + before(uz[p], 1, 1)
        ig = damping / g
        inv[p] = ig
        for c in range(3):
            mm[c, p] = ext[4 + c, p] * ext[1 + c, p] * ig

    steps(1, PLANES - 1, 2, smooth)

    def mid_links(q, tmp32=tmp32):
        p = 2 * q
        a, b = restrict_rows(tmp32, ux[p + 1])
        mux[q] = pair_sum(a + b, 1)
        _, b = restrict_rows(tmp32, uy[p] + uy[p + 1])
        muy[q] = pair_sum(b, 1)
        a, b = restrict_rows(tmp32, uz[p] + uz[p + 1])
        muz[q] = odd_group(a + b, 1)
        a, b = restrict_rows(tmp32, ext[0, p] + ext[0, p + 1])
        spring[q] = 0.1 * pair_sum(a + b, 1)

    steps(0, 12, 2, mid_links)

    def mid_rhs(q):
        p = 2 * q
        g = spring[q] + mux[q] + mux[q - 1]
        g = g + muy[q] + before(muy[q], 1, 0) + muz[q] + before(muz[q], 2, 1)
        ig = damping / g
        mig[q] = ig
        for c in range(3):
            total = jnp.zeros(shape, F32)
            for i in range(2):
                near = neighbours(ux[p + i], ux[p + i - 1], uy[p + i], uz[p + i], mm[c, p + i], mm[c, p + i - 1], mm[c, p + i + 1], 1)
                total = total + keep * ext[1 + c, p + i] + ext[4 + c, p + i] * near
            a, b = restrict_rows(tmp32, total)
            rhs = pair_sum(a + b, 1)
            mrhs[c, q] = rhs
            mc[c, q] = ig * rhs

    steps(1, 11, 2, mid_rhs)

    for s in range(5):
        q = 2 * s
        a, b = restrict_rows(tmp16, mux[q + 1])
        cx_[s] = pair_sum(a + b, 2)
        _, b = restrict_rows(tmp16, muy[q] + muy[q + 1])
        cy_[s] = pair_sum(b, 2)
        a, b = restrict_rows(tmp16, muz[q] + muz[q + 1])
        cz_[s] = odd_group(a + b, 2)
        a, b = restrict_rows(tmp16, spring[q] + spring[q + 1])
        cg[s] = pair_sum(a + b, 2)

    quad = lane_of((8, LANES)) % 4
    for s in range(1, 5):
        g = cg[s] + cx_[s] + cx_[s - 1]
        g = g + cy_[s] + before(cy_[s], 1, 0) + cz_[s] + before(cz_[s], 4, 1)
        rhs = []
        for c in range(3):
            total = jnp.zeros((ROWS // 2, LANES), F32)
            for q in (2 * s, 2 * s + 1):
                near = neighbours(mux[q], mux[q - 1], muy[q], muz[q], mc[c, q], mc[c, q - 1], mc[c, q + 1], 2)
                total = total + keep * mrhs[c, q] + near
            a, b = restrict_rows(tmp16, total)
            rhs.append(pair_sum(a + b, 2))
        first = jnp.where(quad == 0, rhs[0], jnp.where(quad == 1, rhs[1], jnp.where(quad == 2, rhs[2], g)))
        second = jnp.where(quad == 0, cx_[s], jnp.where(quad == 1, cy_[s], cz_[s]))
        for i, v in enumerate((first, second)):
            if s <= 3:
                o_right[i, s - 1] = v
            if s >= 2:
                o_left[i, s - 2] = v
            if s in (2, 3):
                o_own[i, s - 2] = v


def turn_kernel(xl, own, xr, up, down):
    for i in range(2):
        for s in range(8):
            for j in range(3):
                for out, first in ((up, 3), (down, 2)):
                    at = slice(first + j, first + j + 1)
                    src = xl[i, s, at] if s < 3 else own[i, s - 3, at] if s < 5 else xr[i, s - 5, at]
                    out[i, j, s : s + 1] = src


def solve_kernel(
    xl, own, xr, yl, yr, ext, ux_, uy_, uz_, ig_, mux_, muy_, muz_, mig_, mc_,
    direction, image, sums,
    packed, cc, pm, pf, m1, base, d, tmp16,
):
    r, free = ext.at[1:4, 6:18], ext.at[4:7, 6:18]
    ux, uy, uz, ig = (a.at[6:18] for a in (ux_, uy_, uz_, ig_))
    mux, muy, muz, mig, mc = *(a.at[2:10] for a in (mux_, muy_, muz_, mig_)), mc_.at[:, 2:10]
    quad = lane_of((16, LANES)) % 4
    field = [[None] * 8 for _ in range(7)]
    for i in range(2):
        for s in range(8):
            packed[...] = jnp.zeros((16, LANES), F32)
            packed[4:8] = xl[i, s, 2:6] if s < 3 else own[i, s - 3, 2:6] if s < 5 else xr[i, s - 5, 2:6]
            for j in range(3):
                packed[1 + j : 2 + j] = yl[i, j, s : s + 1]
                packed[8 + j : 9 + j] = yr[i, j, s : s + 1]
            v = packed[...]
            for k in range(4 if i == 0 else 3):
                field[4 * i + k][s] = pair_sum(pair_sum(jnp.where(quad == k, v, 0.0), 1), 2)
    g = [jnp.where(v > 0.0, v, 1.0) for v in field[3]]
    inv = [1.0 / v for v in g]
    cx_, cy_, cz_ = field[4], field[5], field[6]
    ratio = eig_center / eig_halfwidth
    q0 = 1.0 / ratio
    q1 = 1.0 / (2.0 * ratio - q0)
    q2 = 1.0 / (2.0 * ratio - q1)
    for c in range(3):
        rhs = field[c]
        update = [rhs[s] * inv[s] * (1.0 / eig_center) for s in range(8)]
        iterate = list(update)
        for q_old, q_new, lo, hi in ((q0, q1, 1, 7), (q1, q2, 2, 6)):
            new = list(iterate)
            for s in range(lo, hi):
                near = neighbours(cx_[s], cx_[s - 1], cy_[s], cz_[s], iterate[s], iterate[s - 1], iterate[s + 1], 4)
                rest = rhs[s] - g[s] * iterate[s] + near
                update[s] = (q_new * q_old) * update[s] + (2.0 * q_new / eig_halfwidth) * (rest * inv[s])
                new[s] = iterate[s] + update[s]
            iterate = new
        for s in range(4):
            tmp16[...] = iterate[2 + s]
            v = tmp16[2:10]
            v = repeat_rows(cc, v)
            pm[c, 2 * s] = mc[c, 2 * s] + v
            pm[c, 2 * s + 1] = mc[c, 2 * s + 1] + v

    def mid(q, _):
        for c in range(3):
            near = neighbours(mux[q], mux[q - 1], muy[q], muz[q], pm[c, q], pm[c, q - 1], pm[c, q + 1], 2)
            v = keep * pm[c, q] + mc[c, q] + mig[q] * near
            v = repeat_rows(pf, v)
            for i in range(2):
                p = 2 * (q - 1) + i
                fr = free[c, p]
                fc = r[c, p] * (fr * ig[p] + damping * (1.0 - fr))
                corr = fc + v
                m1[c, p] = fr * corr
                base[c, p] = keep * corr + fc
        return 0

    lax.fori_loop(1, 7, mid, 0)

    def fine(p, _):
        for c in range(3):
            near = neighbours(ux[p], ux[p - 1], uy[p], uz[p], m1[c, p], m1[c, p - 1], m1[c, p + 1], 1)
            d[c, p] = base[c, p] + free[c, p] * ig[p] * near
        return 0

    lax.fori_loop(1, 11, fine, 0)

    mine = slice(8, 8 + CY)

    def last(p, total):
        first, second = total
        for c in range(3):
            here = free[c, p] * d[c, p]
            prev = free[c, p - 1] * d[c, p - 1]
            nxt = free[c, p + 1] * d[c, p + 1]
            near = neighbours(ux[p], ux[p - 1], uy[p], uz[p], here, prev, nxt, 1)
            fr = free[c, p]
            im = fr * (damping / ig[p] * d[c, p] - near) + (1.0 - fr) * d[c, p]
            im = im[mine, 0:CZ]
            dd = d[c, p, mine, 0:CZ]
            direction[c, p - 2] = dd
            image[c, p - 2] = im
            first = first + r[c, p, mine, 0:CZ] * dd
            second = second + dd * im
        return first, second

    zero = jnp.zeros((CY, CZ), F32)
    first, second = lax.fori_loop(2, 10, last, (zero, zero))
    sums[0:1] = jnp.full((1, CZ), jnp.sum(first), F32)
    sums[1:2] = jnp.full((1, CZ), jnp.sum(second), F32)


def ring(count, step):
    return [(i, (i + step) % count) for i in range(count)]


def all_sum(v, axes):
    n = 1
    for axis in axes:
        n *= lax.axis_size(axis)
    sent = jnp.broadcast_to(v[None], (n,) + v.shape)
    return lax.all_to_all(sent, axes, 0, 0).sum(axis=0)


def shards(solution, residual, density_bins, fixed_dofs):
    nx, nc, nz = lax.axis_size("gx"), lax.axis_size("gc"), lax.axis_size("gz")
    ny = 2 * nc
    y_axes = ("gc", "co")
    ix, iz = lax.axis_index("gx"), lax.axis_index("gz")
    iy = 2 * lax.axis_index("gc") + lax.axis_index("co")
    ends = jnp.stack([ix == 0, ix == nx - 1, iy == 0, iy == ny - 1, iz == 0, iz == nz - 1]).astype(jnp.int32)

    def both(v, axes, count):
        up, down = v if isinstance(v, tuple) else (v, v)
        return lax.ppermute(up, axes, ring(count, 1)), lax.ppermute(down, axes, ring(count, -1))

    brick, slab = (FIELDS, CX, CY, CZ), (FIELDS, CX, 8, CZ)
    packs, halves = (FIELDS, 3, CY, CZ), (FIELDS, 6, 8, CZ)
    x0, up, down = call(gather_kernel, [brick, slab, slab])(density_bins, residual, fixed_dofs)
    xl, xr = both(x0, "gx", nx)
    yl0, yr0 = both((up, down), y_axes, ny)
    to_right, to_left, up_l, down_l, up_r, down_r = call(edge_kernel, [packs, packs, slab, slab, slab, slab])(xl, x0, xr)
    zl, zr = both((to_right, to_left), "gz", nz)
    yll, yrl = both((up_l, down_l), y_axes, ny)
    ylr, yrr = both((up_r, down_r), y_axes, ny)
    zlower, zupper = both(tuple(call(half_kernel, [halves, halves])(zl, zr)), y_axes, ny)

    full = (12, ROWS, LANES)
    half = (8, ROWS // 2, LANES)
    all_f = (PLANES, ROWS, LANES)
    all_m = (12, ROWS // 2, LANES)
    outs = [(FIELDS,) + all_f, all_f, all_f, all_f, all_f, all_m, all_m, all_m, all_m, (3,) + all_m]
    outs += [(2, 3, 8, LANES), (2, 3, 8, LANES), (2, 2, 8, LANES)]
    scratch = [(3,) + all_f, all_m, (3,) + all_m]
    scratch += [(5, 8, LANES)] * 4 + [(2, ROWS, CZ), (2, ROWS // 2, CZ)]
    fine = pl.pallas_call(
        fine_kernel,
        out_shape=[jax.ShapeDtypeStruct(s, F32) for s in outs],
        in_specs=[SMEM] + [VMEM] * 13,
        out_specs=[VMEM] * len(outs),
        scratch_shapes=[pltpu.VMEM(s, F32) for s in scratch],
        compiler_params=pltpu.CompilerParams(vmem_limit_bytes=LIMIT),
    )(ends, xl, x0, xr, yll, yl0, ylr, yrl, yr0, yrr, zl, zr, zlower, zupper)
    kept, (to_right, to_left, own) = fine[:-3], fine[-3:]
    cl, cr = both((to_right, to_left), "gx", nx)
    up, down = call(turn_kernel, [(2, 3, 8, LANES)] * 2)(cl, own, cr)
    dl, dr = both((up, down), y_axes, ny)
    direction, image, sums = call(
        solve_kernel,
        [(3, CX, CY, CZ), (3, CX, CY, CZ), (2, CZ)],
        [(16, LANES), (2, ROWS // 2, CZ), (3,) + half, (2, ROWS, CZ), (3,) + full, (3,) + full, (3,) + full, (16, LANES)],
    )(cl, own, cr, dl, dr, *kept)
    sums = all_sum(all_sum(sums, ("gc", "gz")), ("gx", "co"))
    alpha = (sums[0] / sums[1])[None, None, None]
    return (solution + alpha * direction, residual - alpha * image, direction)


def solution(mesh):
    nx, ny, nz = mesh.devices.shape
    split = Mesh(mesh.devices.reshape(nx, ny // 2, 2, nz), ("gx", "gc", "co", "gz"))
    field = P(None, "gx", ("gc", "co"), "gz")
    return jax.shard_map(
        shards,
        mesh=split,
        in_specs=(field, field, P("gx", ("gc", "co"), "gz"), field),
        out_specs=(field, field, field),
        check_vma=False,
    )
```

```python
import functools

import jax
import jax.numpy as jnp
from jax import lax
from jax.experimental import pallas as pl
from jax.experimental.pallas import tpu as pltpu
from jax.sharding import Mesh
from jax.sharding import PartitionSpec as P

BINS = 16
damping = 0.6
keep = 1.0 - damping
eig_center = 1.05
eig_halfwidth = 0.95

F32 = jnp.float32
CX, CY, CZ = 8, 16, 128
LANES = 2 * CZ
ROWS = CY + 16
PLANES = CX + 16
ZH = 16
LIMIT = 20 * 1024 * 1024
FIELDS = 7

VMEM = pl.BlockSpec(memory_space=pltpu.VMEM)
SMEM = pl.BlockSpec(memory_space=pltpu.SMEM)


def call(kernel, outs, scratch=()):
    return pl.pallas_call(
        kernel,
        out_shape=[jax.ShapeDtypeStruct(s, F32) for s in outs],
        out_specs=[VMEM] * len(outs),
        scratch_shapes=[pltpu.VMEM(s, F32) for s in scratch],
        compiler_params=pltpu.CompilerParams(vmem_limit_bytes=LIMIT),
    )


def before(v, k, axis):
    return pltpu.roll(v, k, axis)


def after(v, k, axis):
    return pltpu.roll(v, v.shape[axis] - k, axis)


def lane_of(shape):
    return lax.broadcasted_iota(jnp.int32, shape, len(shape) - 1)


def pair_sum(v, k):
    low = lane_of(v.shape) % (2 * k) < k
    return v + jnp.where(low, after(v, k, 1), before(v, k, 1))


def odd_group(v, k):
    low = lane_of(v.shape) % (2 * k) < k
    return jnp.where(low, after(v, k, 1), v)


def neighbours(ux, ux_prev, uy, uz, here, prev, nxt, k):
    return (
        ux * nxt
        + ux_prev * prev
        + uy * after(here, 1, 0)
        + before(uy * here, 1, 0)
        + uz * after(here, k, 1)
        + before(uz * here, k, 1)
    )


def slab_kernel(brick, up, down):
    up[...] = brick[:, :, 8:16]
    down[...] = brick[:, :, 0:8]


def edge_kernel(xl, x0, xr, to_right, to_left, up, down):
    block = lane_of((CY, CZ)) // ZH

    def field(f, _):
        for b, brick in enumerate((xl, x0, xr)):
            turned = [pltpu.roll(brick[f, p], ZH * p, 1) if p else brick[f, p] for p in range(CX)]
            right, left = turned[0], turned[0]
            for p in range(1, CX):
                right = jnp.where(block == p - 1, turned[p], right)
                left = jnp.where(block == p, turned[p], left)
            to_right[f, b] = right
            to_left[f, b] = left
        for i, brick in ((0, xl), (CX, xr)):
            up[f, i : i + CX] = brick[f, :, 8:16]
            down[f, i : i + CX] = brick[f, :, 0:8]
        return 0

    lax.fori_loop(0, FIELDS, field, 0)


def half_kernel(zl, zr, up, down):
    for i, v in enumerate((zl, zr)):
        up[:, 3 * i : 3 * i + 3] = v[:, :, 8:16]
        down[:, 3 * i : 3 * i + 3] = v[:, :, 0:8]


def steps(start, stop, each, body):
    def step(i, _):
        for j in range(each):
            body(start + each * i + j)
        return 0

    lax.fori_loop(0, (stop - start) // each, step, 0)


def restrict_rows(tmp, v):
    n = v.shape[0] // 2
    for h in range(2):
        tmp[h] = v[:, CZ * h : CZ * (h + 1)]
    return [jnp.concatenate([tmp[h, pl.ds(i, n, stride=2), :] for h in range(2)], axis=1) for i in range(2)]


def repeat_rows(tmp, v):
    n = v.shape[0]
    for h in range(2):
        for i in range(2):
            tmp[h, pl.ds(i, n, stride=2), :] = v[:, CZ * h : CZ * (h + 1)]
    return jnp.concatenate([tmp[0], tmp[1]], axis=1)


def fine_kernel(
    ends, xl, x0, xr, lower0, upper0, lower, upper, zl, zr, zlower, zupper,
    ext, ux, uy, uz, inv, mux, muy, muz, mig, mc, o_right, o_left, o_own,
    mm, spring, mrhs, cx_, cy_, cz_, cg, tmp32, tmp16,
):
    block = lane_of((CY, CZ)) // ZH
    block8 = lane_of((8, CZ)) // ZH

    def assemble(f, _):
        for b, brick in enumerate((xl, x0, xr)):
            below, above, first = (lower0, upper0, 0) if b == 1 else (lower, upper, 0 if b == 0 else CX)
            parts = (
                (0, 8, below, first, zlower[f, b], zlower[f, 3 + b], block8),
                (8, CY, brick, 0, zl[f, b], zr[f, b], block),
                (8 + CY, 8, above, first, zupper[f, b], zupper[f, 3 + b], block8),
            )
            for start, rows, src, offset, from_left, from_right, at in parts:
                for p in range(CX):
                    halo = jnp.where(at == p, from_right, from_left)
                    ext[f, CX * b + p, start : start + rows, 0:CZ] = src[f, offset + p]
                    ext[f, CX * b + p, start : start + rows, CZ:LANES] = pltpu.roll(halo, CZ - ZH * p, 1) if p else halo
        return 0

    lax.fori_loop(0, FIELDS, assemble, 0)

    lo_x, hi_x, lo_y, hi_y, lo_z, hi_z = (ends[i] for i in range(6))
    shape = (ROWS, LANES)
    row = lax.broadcasted_iota(jnp.int32, shape, 0)
    col = lane_of(shape)
    half_y = jnp.where(((row == 7) & (lo_y == 1)) | ((row == 7 + CY) & (hi_y == 1)), 0.0, 0.5)
    half_z = jnp.where(((col == LANES - 1) & (lo_z == 1)) | ((col == CZ - 1) & (hi_z == 1)), 0.0, 0.5)

    def links(p):
        here = ext[0, p]
        cut = ((p == 7) & (lo_x == 1)) | ((p == 7 + CX) & (hi_x == 1))
        ux[p] = jnp.where(cut, 0.0, 0.5) * (here + ext[0, jnp.minimum(p + 1, PLANES - 1)])
        uy[p] = half_y * (here + after(here, 1, 0))
        uz[p] = half_z * (here + after(here, 1, 1))

    steps(0, PLANES, 4, links)

    def smooth(p):
        g = 0.1 * ext[0, p] + ux[p] + ux[p - 1]
        g = g + uy[p] + before(uy[p], 1, 0) + uz[p] + before(uz[p], 1, 1)
        ig = damping / g
        inv[p] = ig
        for c in range(3):
            mm[c, p] = ext[4 + c, p] * ext[1 + c, p] * ig

    steps(1, PLANES - 1, 2, smooth)

    def mid_links(q, tmp32=tmp32):
        p = 2 * q
        a, b = restrict_rows(tmp32, ux[p + 1])
        mux[q] = pair_sum(a + b, 1)
        _, b = restrict_rows(tmp32, uy[p] + uy[p + 1])
        muy[q] = pair_sum(b, 1)
        a, b = restrict_rows(tmp32, uz[p] + uz[p + 1])
        muz[q] = odd_group(a + b, 1)
        a, b = restrict_rows(tmp32, ext[0, p] + ext[0, p + 1])
        spring[q] = 0.1 * pair_sum(a + b, 1)

    steps(0, 12, 2, mid_links)

    def mid_rhs(q):
        p = 2 * q
        g = spring[q] + mux[q] + mux[q - 1]
        g = g + muy[q] + before(muy[q], 1, 0) + muz[q] + before(muz[q], 2, 1)
        ig = damping / g
        mig[q] = ig
        for c in range(3):
            total = jnp.zeros(shape, F32)
            for i in range(2):
                near = neighbours(ux[p + i], ux[p + i - 1], uy[p + i], uz[p + i], mm[c, p + i], mm[c, p + i - 1], mm[c, p + i + 1], 1)
                total = total + keep * ext[1 + c, p + i] + ext[4 + c, p + i] * near
            a, b = restrict_rows(tmp32, total)
            rhs = pair_sum(a + b, 1)
            mrhs[c, q] = rhs
            mc[c, q] = ig * rhs

    steps(1, 11, 2, mid_rhs)

    for s in range(5):
        q = 2 * s
        a, b = restrict_rows(tmp16, mux[q + 1])
        cx_[s] = pair_sum(a + b, 2)
        _, b = restrict_rows(tmp16, muy[q] + muy[q + 1])
        cy_[s] = pair_sum(b, 2)
        a, b = restrict_rows(tmp16, muz[q] + muz[q + 1])
        cz_[s] = odd_group(a + b, 2)
        a, b = restrict_rows(tmp16, spring[q] + spring[q + 1])
        cg[s] = pair_sum(a + b, 2)

    quad = lane_of((8, LANES)) % 4
    for s in range(1, 5):
        g = cg[s] + cx_[s] + cx_[s - 1]
        g = g + cy_[s] + before(cy_[s], 1, 0) + cz_[s] + before(cz_[s], 4, 1)
        rhs = []
        for c in range(3):
            total = jnp.zeros((ROWS // 2, LANES), F32)
            for q in (2 * s, 2 * s + 1):
                near = neighbours(mux[q], mux[q - 1], muy[q], muz[q], mc[c, q], mc[c, q - 1], mc[c, q + 1], 2)
                total = total + keep * mrhs[c, q] + near
            a, b = restrict_rows(tmp16, total)
            rhs.append(pair_sum(a + b, 2))
        first = jnp.where(quad == 0, rhs[0], jnp.where(quad == 1, rhs[1], jnp.where(quad == 2, rhs[2], g)))
        second = jnp.where(quad == 0, cx_[s], jnp.where(quad == 1, cy_[s], cz_[s]))
        for i, v in enumerate((first, second)):
            if s <= 3:
                o_right[i, s - 1] = v
            if s >= 2:
                o_left[i, s - 2] = v
            if s in (2, 3):
                o_own[i, s - 2] = v


def unpack(v, quad, count):
    at = {0: v}
    for k in range(1, 4):
        at[k] = before(v, k, 1)
    for k in range(1, count):
        at[-k] = after(v, k, 1)
    return [
        jnp.where(quad == 0, at[-j], jnp.where(quad == 1, at[1 - j], jnp.where(quad == 2, at[2 - j], at[3 - j])))
        for j in range(count)
    ]


def turn_kernel(xl, own, xr, up, down):
    for i in range(2):
        for s in range(8):
            for j in range(3):
                for out, first in ((up, 3), (down, 2)):
                    at = slice(first + j, first + j + 1)
                    src = xl[i, s, at] if s < 3 else own[i, s - 3, at] if s < 5 else xr[i, s - 5, at]
                    out[i, j, s : s + 1] = src


def solve_kernel(
    xl, own, xr, yl, yr, ext, ux_, uy_, uz_, ig_, mux_, muy_, muz_, mig_, mc_,
    direction, image, sums,
    packed, cc, pm, pf, m1, base, d, tmp16,
):
    r, free = ext.at[1:4, 6:18], ext.at[4:7, 6:18]
    ux, uy, uz, ig = (a.at[6:18] for a in (ux_, uy_, uz_, ig_))
    mux, muy, muz, mig, mc = *(a.at[2:10] for a in (mux_, muy_, muz_, mig_)), mc_.at[:, 2:10]
    quad = lane_of((16, LANES)) % 4
    field = [[None] * 8 for _ in range(7)]
    for i in range(2):
        for s in range(8):
            packed[...] = jnp.zeros((16, LANES), F32)
            packed[4:8] = xl[i, s, 2:6] if s < 3 else own[i, s - 3, 2:6] if s < 5 else xr[i, s - 5, 2:6]
            for j in range(3):
                packed[1 + j : 2 + j] = yl[i, j, s : s + 1]
                packed[8 + j : 9 + j] = yr[i, j, s : s + 1]
            v = packed[...]
            for k, u in enumerate(unpack(v, quad, 4 if i == 0 else 3)):
                field[4 * i + k][s] = u
    g = [jnp.where(v > 0.0, v, 1.0) for v in field[3]]
    inv = [1.0 / v for v in g]
    cx_, cy_, cz_ = field[4], field[5], field[6]
    ratio = eig_center / eig_halfwidth
    q0 = 1.0 / ratio
    q1 = 1.0 / (2.0 * ratio - q0)
    q2 = 1.0 / (2.0 * ratio - q1)
    for c in range(3):
        rhs = field[c]
        update = [rhs[s] * inv[s] * (1.0 / eig_center) for s in range(8)]
        iterate = list(update)
        for q_old, q_new, lo, hi in ((q0, q1, 1, 7), (q1, q2, 2, 6)):
            new = list(iterate)
            for s in range(lo, hi):
                near = neighbours(cx_[s], cx_[s - 1], cy_[s], cz_[s], iterate[s], iterate[s - 1], iterate[s + 1], 4)
                rest = rhs[s] - g[s] * iterate[s] + near
                update[s] = (q_new * q_old) * update[s] + (2.0 * q_new / eig_halfwidth) * (rest * inv[s])
                new[s] = iterate[s] + update[s]
            iterate = new
        for s in range(4):
            tmp16[...] = iterate[2 + s]
            v = tmp16[2:10]
            v = repeat_rows(cc, v)
            pm[c, 2 * s] = mc[c, 2 * s] + v
            pm[c, 2 * s + 1] = mc[c, 2 * s + 1] + v

    def mid(q, _):
        for c in range(3):
            near = neighbours(mux[q], mux[q - 1], muy[q], muz[q], pm[c, q], pm[c, q - 1], pm[c, q + 1], 2)
            v = keep * pm[c, q] + mc[c, q] + mig[q] * near
            v = repeat_rows(pf, v)
            for i in range(2):
                p = 2 * (q - 1) + i
                fr = free[c, p]
                fc = r[c, p] * (fr * ig[p] + damping * (1.0 - fr))
                corr = fc + v
                m1[c, p] = fr * corr
                base[c, p] = keep * corr + fc
        return 0

    lax.fori_loop(1, 7, mid, 0)

    def fine(p, _):
        for c in range(3):
            near = neighbours(ux[p], ux[p - 1], uy[p], uz[p], m1[c, p], m1[c, p - 1], m1[c, p + 1], 1)
            d[c, p] = base[c, p] + free[c, p] * ig[p] * near
        return 0

    lax.fori_loop(1, 11, fine, 0)

    mine = slice(8, 8 + CY)

    def last(p, total):
        first, second = total
        for c in range(3):
            here = free[c, p] * d[c, p]
            prev = free[c, p - 1] * d[c, p - 1]
            nxt = free[c, p + 1] * d[c, p + 1]
            near = neighbours(ux[p], ux[p - 1], uy[p], uz[p], here, prev, nxt, 1)
            fr = free[c, p]
            im = fr * (damping / ig[p] * d[c, p] - near) + (1.0 - fr) * d[c, p]
            im = im[mine, 0:CZ]
            dd = d[c, p, mine, 0:CZ]
            direction[c, p - 2] = dd
            image[c, p - 2] = im
            first = first + r[c, p, mine, 0:CZ] * dd
            second = second + dd * im
        return first, second

    zero = jnp.zeros((CY, CZ), F32)
    first, second = lax.fori_loop(2, 10, last, (zero, zero))
    sums[0:1] = jnp.full((1, CZ), jnp.sum(first), F32)
    sums[1:2] = jnp.full((1, CZ), jnp.sum(second), F32)


def ring(count, step):
    return [(i, (i + step) % count) for i in range(count)]


def all_sum(v, axes):
    n = 1
    for axis in axes:
        n *= lax.axis_size(axis)
    sent = jnp.broadcast_to(v[None], (n,) + v.shape)
    return lax.all_to_all(sent, axes, 0, 0).sum(axis=0)


def shards(solution, residual, density_bins, fixed_dofs):
    nx, nc, nz = lax.axis_size("gx"), lax.axis_size("gc"), lax.axis_size("gz")
    ny = 2 * nc
    y_axes = ("gc", "co")
    ix, iz = lax.axis_index("gx"), lax.axis_index("gz")
    iy = 2 * lax.axis_index("gc") + lax.axis_index("co")
    ends = jnp.stack([ix == 0, ix == nx - 1, iy == 0, iy == ny - 1, iz == 0, iz == nz - 1]).astype(jnp.int32)

    def both(v, axes, count):
        up, down = v if isinstance(v, tuple) else (v, v)
        return lax.ppermute(up, axes, ring(count, 1)), lax.ppermute(down, axes, ring(count, -1))

    slab, slabs = (FIELDS, CX, 8, CZ), (FIELDS, 2 * CX, 8, CZ)
    packs, halves = (FIELDS, 3, CY, CZ), (FIELDS, 6, 8, CZ)
    f = (density_bins.astype(F32) + 1.0) / BINS
    modulus = 0.05 + 0.95 * f * f * f
    x0 = jnp.concatenate([modulus[None], residual, 1.0 - fixed_dofs.astype(F32)], axis=0)
    xl, xr = both(x0, "gx", nx)
    lower0, upper0 = both(tuple(call(slab_kernel, [slab, slab])(x0)), y_axes, ny)
    xl, xr, lower0, upper0 = lax.optimization_barrier((xl, xr, lower0, upper0))
    to_right, to_left, up, down = call(edge_kernel, [packs, packs, slabs, slabs])(xl, x0, xr)
    zl, zr = both((to_right, to_left), "gz", nz)
    lower, upper = both((up, down), y_axes, ny)
    zlower, zupper = both(tuple(call(half_kernel, [halves, halves])(zl, zr)), y_axes, ny)

    full = (12, ROWS, LANES)
    half = (8, ROWS // 2, LANES)
    all_f = (PLANES, ROWS, LANES)
    all_m = (12, ROWS // 2, LANES)
    outs = [(FIELDS,) + all_f, all_f, all_f, all_f, all_f, all_m, all_m, all_m, all_m, (3,) + all_m]
    outs += [(2, 3, 8, LANES), (2, 3, 8, LANES), (2, 2, 8, LANES)]
    scratch = [(3,) + all_f, all_m, (3,) + all_m]
    scratch += [(5, 8, LANES)] * 4 + [(2, ROWS, CZ), (2, ROWS // 2, CZ)]
    fine = pl.pallas_call(
        fine_kernel,
        out_shape=[jax.ShapeDtypeStruct(s, F32) for s in outs],
        in_specs=[SMEM] + [VMEM] * 11,
        out_specs=[VMEM] * len(outs),
        scratch_shapes=[pltpu.VMEM(s, F32) for s in scratch],
        compiler_params=pltpu.CompilerParams(vmem_limit_bytes=LIMIT),
    )(ends, xl, x0, xr, lower0, upper0, lower, upper, zl, zr, zlower, zupper)
    kept, (to_right, to_left, own) = fine[:-3], fine[-3:]
    cl, cr = both((to_right, to_left), "gx", nx)
    up, down = call(turn_kernel, [(2, 3, 8, LANES)] * 2)(cl, own, cr)
    dl, dr = both((up, down), y_axes, ny)
    direction, image, sums = call(
        solve_kernel,
        [(3, CX, CY, CZ), (3, CX, CY, CZ), (2, CZ)],
        [(16, LANES), (2, ROWS // 2, CZ), (3,) + half, (2, ROWS, CZ), (3,) + full, (3,) + full, (3,) + full, (16, LANES)],
    )(cl, own, cr, dl, dr, *kept)
    sums = all_sum(all_sum(sums, ("gc", "gz")), ("gx", "co"))
    alpha = (sums[0] / sums[1])[None, None, None]
    return (solution + alpha * direction, residual - alpha * image, direction)


def solution(mesh):
    nx, ny, nz = mesh.devices.shape
    split = Mesh(mesh.devices.reshape(nx, ny // 2, 2, nz), ("gx", "gc", "co", "gz"))
    field = P(None, "gx", ("gc", "co"), "gz")
    return jax.shard_map(
        shards,
        mesh=split,
        in_specs=(field, field, P("gx", ("gc", "co"), "gz"), field),
        out_specs=(field, field, field),
        check_vma=False,
    )
```

```python
import functools

import jax
import jax.numpy as jnp
from jax import lax
from jax.experimental import pallas as pl
from jax.experimental.pallas import tpu as pltpu
from jax.sharding import Mesh
from jax.sharding import PartitionSpec as P

BINS = 16
damping = 0.6
keep = 1.0 - damping
eig_center = 1.05
eig_halfwidth = 0.95

F32 = jnp.float32
CX, CY, CZ = 8, 16, 128
LANES = 2 * CZ
ROWS = CY + 16
PLANES = CX + 16
ZH = 16
LIMIT = 20 * 1024 * 1024
GYX = CX + 2
FIELDS = 7

VMEM = pl.BlockSpec(memory_space=pltpu.VMEM)
SMEM = pl.BlockSpec(memory_space=pltpu.SMEM)


def call(kernel, outs, scratch=()):
    return pl.pallas_call(
        kernel,
        out_shape=[jax.ShapeDtypeStruct(s, F32) for s in outs],
        out_specs=[VMEM] * len(outs),
        scratch_shapes=[pltpu.VMEM(s, F32) for s in scratch],
        compiler_params=pltpu.CompilerParams(vmem_limit_bytes=LIMIT),
    )


def before(v, k, axis):
    return pltpu.roll(v, k, axis)


def after(v, k, axis):
    return pltpu.roll(v, v.shape[axis] - k, axis)


def lane_of(shape):
    return lax.broadcasted_iota(jnp.int32, shape, len(shape) - 1)


def pair_sum(v, k):
    low = lane_of(v.shape) % (2 * k) < k
    return v + jnp.where(low, after(v, k, 1), before(v, k, 1))


def odd_group(v, k):
    low = lane_of(v.shape) % (2 * k) < k
    return jnp.where(low, after(v, k, 1), v)


def neighbours(ux, ux_prev, uy, uz, here, prev, nxt, k):
    return (
        ux * nxt
        + ux_prev * prev
        + uy * after(here, 1, 0)
        + before(uy * here, 1, 0)
        + uz * after(here, k, 1)
        + before(uz * here, k, 1)
    )


def pack_kernel(density, residual, fixed, main, to_right, to_left):
    block = lane_of((CY, CZ)) // ZH

    def stage(f, planes):
        turned = [pltpu.roll(v, ZH * p, 1) if p else v for p, v in enumerate(planes)]
        right, left = turned[0], turned[0]
        for p in range(1, CX):
            right = jnp.where(block == p - 1, turned[p], right)
            left = jnp.where(block == p, turned[p], left)
        to_right[f] = right
        to_left[f] = left
        for p, v in enumerate(planes):
            main[f, p] = v

    def modulus(bins):
        f = (bins.astype(F32) + 1.0) / BINS
        return 0.05 + 0.95 * f * f * f

    stage(0, [modulus(density[p]) for p in range(CX)])
    for c in range(3):
        stage(1 + c, [residual[c, p] for p in range(CX)])
        stage(4 + c, [1.0 - fixed[c, p].astype(F32) for p in range(CX)])


def join_kernel(main, zl, zr, brick, up, down):
    brick[:, 0:CX] = main[...]
    brick[:, CX] = zl[...]
    brick[:, CX + 1] = zr[...]
    up[:, 0:CX] = main[:, :, 8:16]
    up[:, CX] = zl[:, 8:16]
    up[:, CX + 1] = zr[:, 8:16]
    down[:, 0:CX] = main[:, :, 0:8]
    down[:, CX] = zl[:, 0:8]
    down[:, CX + 1] = zr[:, 0:8]


def slab_kernel(xl, xr, up, down):
    for first, brick in ((0, xl), (GYX, xr)):
        up[:, first : first + GYX] = brick[:, :, 8:16]
        down[:, first : first + GYX] = brick[:, :, 0:8]


def steps(start, stop, each, body):
    def step(i, _):
        for j in range(each):
            body(start + each * i + j, j)
        return 0

    lax.fori_loop(0, (stop - start) // each, step, 0)


def restrict_rows(tmp, v):
    n = v.shape[0] // 2
    for h in range(2):
        tmp[h] = v[:, CZ * h : CZ * (h + 1)]
    return [jnp.concatenate([tmp[h, pl.ds(i, n, stride=2), :] for h in range(2)], axis=1) for i in range(2)]


def repeat_rows(tmp, v):
    n = v.shape[0]
    for h in range(2):
        for i in range(2):
            tmp[h, pl.ds(i, n, stride=2), :] = v[:, CZ * h : CZ * (h + 1)]
    return jnp.concatenate([tmp[0], tmp[1]], axis=1)


def fine_kernel(
    ends, xl, x0, xr, lower0, upper0, lower, upper,
    ext, ux, uy, uz, inv, mux, muy, muz, mig, mc, o_right, o_left, o_own,
    mm, spring, mrhs, cx_, cy_, cz_, cg, tmp32, tmp16,
):
    block = lane_of((CY, CZ)) // ZH
    block8 = lane_of((8, CZ)) // ZH

    def assemble(f, _):
        for b, brick in enumerate((xl, x0, xr)):
            below, above, first = (lower0, upper0, 0) if b == 1 else (lower, upper, 0 if b == 0 else GYX)
            parts = (
                (0, 8, below, first, block8),
                (8, CY, brick, 0, block),
                (8 + CY, 8, above, first, block8),
            )
            for start, rows, src, offset, at in parts:
                from_left, from_right = src[f, offset + CX], src[f, offset + CX + 1]
                for p in range(CX):
                    halo = jnp.where(at == p, from_right, from_left)
                    ext[f, CX * b + p, start : start + rows, 0:CZ] = src[f, offset + p]
                    ext[f, CX * b + p, start : start + rows, CZ:LANES] = pltpu.roll(halo, CZ - ZH * p, 1) if p else halo
        return 0

    lax.fori_loop(0, FIELDS, assemble, 0)

    lo_x, hi_x, lo_y, hi_y, lo_z, hi_z = (ends[i] for i in range(6))
    shape = (ROWS, LANES)
    row = lax.broadcasted_iota(jnp.int32, shape, 0)
    col = lane_of(shape)
    half_y = jnp.where(((row == 7) & (lo_y == 1)) | ((row == 7 + CY) & (hi_y == 1)), 0.0, 0.5)
    half_z = jnp.where(((col == LANES - 1) & (lo_z == 1)) | ((col == CZ - 1) & (hi_z == 1)), 0.0, 0.5)

    def links(p, _):
        here = ext[0, p]
        cut = ((p == 7) & (lo_x == 1)) | ((p == 7 + CX) & (hi_x == 1))
        ux[p] = jnp.where(cut, 0.0, 0.5) * (here + ext[0, jnp.minimum(p + 1, PLANES - 1)])
        uy[p] = half_y * (here + after(here, 1, 0))
        uz[p] = half_z * (here + after(here, 1, 1))

    steps(0, PLANES, 8, links)

    def smooth(p, _):
        g = 0.1 * ext[0, p] + ux[p] + ux[p - 1]
        g = g + uy[p] + before(uy[p], 1, 0) + uz[p] + before(uz[p], 1, 1)
        ig = damping / g
        inv[p] = ig
        for c in range(3):
            mm[c, p] = ext[4 + c, p] * ext[1 + c, p] * ig

    steps(1, PLANES - 1, 11, smooth)

    def mid_links(q, j):
        tmp = [tmp32.at[4 * j + i] for i in range(4)]
        p = 2 * q
        a, b = restrict_rows(tmp[0], ux[p + 1])
        mux[q] = pair_sum(a + b, 1)
        _, b = restrict_rows(tmp[1], uy[p] + uy[p + 1])
        muy[q] = pair_sum(b, 1)
        a, b = restrict_rows(tmp[2], uz[p] + uz[p + 1])
        muz[q] = odd_group(a + b, 1)
        a, b = restrict_rows(tmp[3], ext[0, p] + ext[0, p + 1])
        spring[q] = 0.1 * pair_sum(a + b, 1)

    steps(0, 12, 6, mid_links)

    def mid_rhs(q, j):
        p = 2 * q
        g = spring[q] + mux[q] + mux[q - 1]
        g = g + muy[q] + before(muy[q], 1, 0) + muz[q] + before(muz[q], 2, 1)
        ig = damping / g
        mig[q] = ig
        for c in range(3):
            total = jnp.zeros(shape, F32)
            for i in range(2):
                near = neighbours(ux[p + i], ux[p + i - 1], uy[p + i], uz[p + i], mm[c, p + i], mm[c, p + i - 1], mm[c, p + i + 1], 1)
                total = total + keep * ext[1 + c, p + i] + ext[4 + c, p + i] * near
            a, b = restrict_rows(tmp32.at[3 * j + c], total)
            rhs = pair_sum(a + b, 1)
            mrhs[c, q] = rhs
            mc[c, q] = ig * rhs

    steps(1, 11, 2, mid_rhs)

    for s in range(5):
        q = 2 * s
        a, b = restrict_rows(tmp16.at[4 * s], mux[q + 1])
        cx_[s] = pair_sum(a + b, 2)
        _, b = restrict_rows(tmp16.at[4 * s + 1], muy[q] + muy[q + 1])
        cy_[s] = pair_sum(b, 2)
        a, b = restrict_rows(tmp16.at[4 * s + 2], muz[q] + muz[q + 1])
        cz_[s] = odd_group(a + b, 2)
        a, b = restrict_rows(tmp16.at[4 * s + 3], spring[q] + spring[q + 1])
        cg[s] = pair_sum(a + b, 2)

    quad = lane_of((8, LANES)) % 4
    for s in range(1, 5):
        g = cg[s] + cx_[s] + cx_[s - 1]
        g = g + cy_[s] + before(cy_[s], 1, 0) + cz_[s] + before(cz_[s], 4, 1)
        rhs = []
        for c in range(3):
            total = jnp.zeros((ROWS // 2, LANES), F32)
            for q in (2 * s, 2 * s + 1):
                near = neighbours(mux[q], mux[q - 1], muy[q], muz[q], mc[c, q], mc[c, q - 1], mc[c, q + 1], 2)
                total = total + keep * mrhs[c, q] + near
            a, b = restrict_rows(tmp16.at[20 + 3 * (s - 1) + c], total)
            rhs.append(pair_sum(a + b, 2))
        first = jnp.where(quad == 0, rhs[0], jnp.where(quad == 1, rhs[1], jnp.where(quad == 2, rhs[2], g)))
        second = jnp.where(quad == 0, cx_[s], jnp.where(quad == 1, cy_[s], cz_[s]))
        for i, v in enumerate((first, second)):
            if s <= 3:
                o_right[i, s - 1] = v
            if s >= 2:
                o_left[i, s - 2] = v
            if s in (2, 3):
                o_own[i, s - 2] = v


def unpack(v, quad, count):
    at = {0: v}
    for k in range(1, 4):
        at[k] = before(v, k, 1)
    for k in range(1, count):
        at[-k] = after(v, k, 1)
    return [
        jnp.where(quad == 0, at[-j], jnp.where(quad == 1, at[1 - j], jnp.where(quad == 2, at[2 - j], at[3 - j])))
        for j in range(count)
    ]


def turn_kernel(xl, own, xr, up, down):
    for i in range(2):
        for s in range(8):
            for j in range(3):
                for out, first in ((up, 3), (down, 2)):
                    at = slice(first + j, first + j + 1)
                    src = xl[i, s, at] if s < 3 else own[i, s - 3, at] if s < 5 else xr[i, s - 5, at]
                    out[i, j, s : s + 1] = src


def solve_kernel(
    xl, own, xr, yl, yr, ext, ux_, uy_, uz_, ig_, mux_, muy_, muz_, mig_, mc_,
    direction, image, sums,
    packed, cc, pm, pf, m1, base, d, tmp16,
):
    r, free = ext.at[1:4, 6:18], ext.at[4:7, 6:18]
    ux, uy, uz, ig = (a.at[6:18] for a in (ux_, uy_, uz_, ig_))
    mux, muy, muz, mig, mc = *(a.at[2:10] for a in (mux_, muy_, muz_, mig_)), mc_.at[:, 2:10]
    quad = lane_of((16, LANES)) % 4
    field = [[None] * 8 for _ in range(7)]
    for i in range(2):
        for s in range(8):
            here = packed.at[8 * i + s]
            here[...] = jnp.zeros((16, LANES), F32)
            here[4:8] = xl[i, s, 2:6] if s < 3 else own[i, s - 3, 2:6] if s < 5 else xr[i, s - 5, 2:6]
            for j in range(3):
                here[1 + j : 2 + j] = yl[i, j, s : s + 1]
                here[8 + j : 9 + j] = yr[i, j, s : s + 1]
            v = here[...]
            for k, u in enumerate(unpack(v, quad, 4 if i == 0 else 3)):
                field[4 * i + k][s] = u
    g = [jnp.where(v > 0.0, v, 1.0) for v in field[3]]
    inv = [1.0 / v for v in g]
    cx_, cy_, cz_ = field[4], field[5], field[6]
    ratio = eig_center / eig_halfwidth
    q0 = 1.0 / ratio
    q1 = 1.0 / (2.0 * ratio - q0)
    q2 = 1.0 / (2.0 * ratio - q1)
    for c in range(3):
        rhs = field[c]
        update = [rhs[s] * inv[s] * (1.0 / eig_center) for s in range(8)]
        iterate = list(update)
        for q_old, q_new, lo, hi in ((q0, q1, 1, 7), (q1, q2, 2, 6)):
            new = list(iterate)
            for s in range(lo, hi):
                near = neighbours(cx_[s], cx_[s - 1], cy_[s], cz_[s], iterate[s], iterate[s - 1], iterate[s + 1], 4)
                rest = rhs[s] - g[s] * iterate[s] + near
                update[s] = (q_new * q_old) * update[s] + (2.0 * q_new / eig_halfwidth) * (rest * inv[s])
                new[s] = iterate[s] + update[s]
            iterate = new
        for s in range(4):
            tmp16[4 * c + s] = iterate[2 + s]
            v = tmp16[4 * c + s, 2:10]
            v = repeat_rows(cc.at[4 * c + s], v)
            pm[c, 2 * s] = mc[c, 2 * s] + v
            pm[c, 2 * s + 1] = mc[c, 2 * s + 1] + v

    def mid(q, j):
        for c in range(3):
            near = neighbours(mux[q], mux[q - 1], muy[q], muz[q], pm[c, q], pm[c, q - 1], pm[c, q + 1], 2)
            v = keep * pm[c, q] + mc[c, q] + mig[q] * near
            v = repeat_rows(pf.at[3 * j + c], v)
            for i in range(2):
                p = 2 * (q - 1) + i
                fr = free[c, p]
                fc = r[c, p] * (fr * ig[p] + damping * (1.0 - fr))
                corr = fc + v
                m1[c, p] = fr * corr
                base[c, p] = keep * corr + fc

    steps(1, 7, 3, mid)

    def fine(p, _):
        for c in range(3):
            near = neighbours(ux[p], ux[p - 1], uy[p], uz[p], m1[c, p], m1[c, p - 1], m1[c, p + 1], 1)
            d[c, p] = base[c, p] + free[c, p] * ig[p] * near

    steps(1, 11, 5, fine)

    mine = slice(8, 8 + CY)

    def last(i, total):
        first, second = total
        for p, c in ((2 + 4 * i + j, c) for j in range(4) for c in range(3)):
            here = free[c, p] * d[c, p]
            prev = free[c, p - 1] * d[c, p - 1]
            nxt = free[c, p + 1] * d[c, p + 1]
            near = neighbours(ux[p], ux[p - 1], uy[p], uz[p], here, prev, nxt, 1)
            fr = free[c, p]
            im = fr * (damping / ig[p] * d[c, p] - near) + (1.0 - fr) * d[c, p]
            im = im[mine, 0:CZ]
            dd = d[c, p, mine, 0:CZ]
            direction[c, p - 2] = dd
            image[c, p - 2] = im
            first = first + r[c, p, mine, 0:CZ] * dd
            second = second + dd * im
        return first, second

    zero = jnp.zeros((CY, CZ), F32)
    first, second = lax.fori_loop(0, 2, last, (zero, zero))
    sums[0:1] = jnp.full((1, CZ), jnp.sum(first), F32)
    sums[1:2] = jnp.full((1, CZ), jnp.sum(second), F32)


def ring(count, step):
    return [(i, (i + step) % count) for i in range(count)]


def all_sum(v, axes):
    n = 1
    for axis in axes:
        n *= lax.axis_size(axis)
    sent = jnp.broadcast_to(v[None], (n,) + v.shape)
    return lax.all_to_all(sent, axes, 0, 0).sum(axis=0)


def shards(solution, residual, density_bins, fixed_dofs):
    nx, nc, nz = lax.axis_size("gx"), lax.axis_size("gc"), lax.axis_size("gz")
    ny = 2 * nc
    y_axes = ("gc", "co")
    ix, iz = lax.axis_index("gx"), lax.axis_index("gz")
    iy = 2 * lax.axis_index("gc") + lax.axis_index("co")
    ends = jnp.stack([ix == 0, ix == nx - 1, iy == 0, iy == ny - 1, iz == 0, iz == nz - 1]).astype(jnp.int32)

    def both(v, axes, count):
        up, down = v if isinstance(v, tuple) else (v, v)
        return lax.ppermute(up, axes, ring(count, 1)), lax.ppermute(down, axes, ring(count, -1))

    main, brick = (FIELDS, CX, CY, CZ), (FIELDS, GYX, CY, CZ)
    pack, slab, slabs = (FIELDS, CY, CZ), (FIELDS, GYX, 8, CZ), (FIELDS, 2 * GYX, 8, CZ)
    x0, to_right, to_left = call(pack_kernel, [main, pack, pack])(density_bins, residual, fixed_dofs)
    zl, zr = both((to_right, to_left), "gz", nz)
    x0, up, down = lax.optimization_barrier(tuple(call(join_kernel, [brick, slab, slab])(x0, zl, zr)))
    xl, xr = both(x0, "gx", nx)
    lower0, upper0 = both((up, down), y_axes, ny)
    xl, xr, lower0, upper0 = lax.optimization_barrier((xl, xr, lower0, upper0))
    lower, upper = both(tuple(call(slab_kernel, [slabs, slabs])(xl, xr)), y_axes, ny)

    full = (12, ROWS, LANES)
    half = (8, ROWS // 2, LANES)
    all_f = (PLANES, ROWS, LANES)
    all_m = (12, ROWS // 2, LANES)
    outs = [(FIELDS,) + all_f, all_f, all_f, all_f, all_f, all_m, all_m, all_m, all_m, (3,) + all_m]
    outs += [(2, 3, 8, LANES), (2, 3, 8, LANES), (2, 2, 8, LANES)]
    scratch = [(3,) + all_f, all_m, (3,) + all_m]
    scratch += [(5, 8, LANES)] * 4 + [(24, 2, ROWS, CZ), (32, 2, ROWS // 2, CZ)]
    fine = pl.pallas_call(
        fine_kernel,
        out_shape=[jax.ShapeDtypeStruct(s, F32) for s in outs],
        in_specs=[SMEM] + [VMEM] * 7,
        out_specs=[VMEM] * len(outs),
        scratch_shapes=[pltpu.VMEM(s, F32) for s in scratch],
        compiler_params=pltpu.CompilerParams(vmem_limit_bytes=LIMIT),
    )(ends, xl, x0, xr, lower0, upper0, lower, upper)
    kept, (to_right, to_left, own) = fine[:-3], fine[-3:]
    cl, cr = both((to_right, to_left), "gx", nx)
    up, down = call(turn_kernel, [(2, 3, 8, LANES)] * 2)(cl, own, cr)
    dl, dr = both((up, down), y_axes, ny)
    direction, image, sums = call(
        solve_kernel,
        [(3, CX, CY, CZ), (3, CX, CY, CZ), (2, CZ)],
        [(16, 16, LANES), (12, 2, ROWS // 2, CZ), (3,) + half, (9, 2, ROWS, CZ), (3,) + full, (3,) + full, (3,) + full, (12, 16, LANES)],
    )(cl, own, cr, dl, dr, *kept)
    sums = all_sum(all_sum(sums, ("gc", "gz")), ("gx", "co"))
    alpha = (sums[0] / sums[1])[None, None, None]
    return (solution + alpha * direction, residual - alpha * image, direction)


def solution(mesh):
    nx, ny, nz = mesh.devices.shape
    split = Mesh(mesh.devices.reshape(nx, ny // 2, 2, nz), ("gx", "gc", "co", "gz"))
    field = P(None, "gx", ("gc", "co"), "gz")
    return jax.shard_map(
        shards,
        mesh=split,
        in_specs=(field, field, P("gx", ("gc", "co"), "gz"), field),
        out_specs=(field, field, field),
        check_vma=False,
    )
```

```python
import functools

import jax
import jax.numpy as jnp
from jax import lax
from jax.experimental import pallas as pl
from jax.experimental.pallas import tpu as pltpu
from jax.sharding import Mesh
from jax.sharding import PartitionSpec as P

BINS = 16
damping = 0.6
keep = 1.0 - damping
eig_center = 1.05
eig_halfwidth = 0.95

F32 = jnp.float32
CX, CY, CZ = 8, 16, 128
LANES = 2 * CZ
ROWS = CY + 16
PLANES = CX + 16
ZH = 16
MIB = 1024 * 1024
GYX = CX + 2
SLAB = 8
FIELDS = 7

VMEM = pl.BlockSpec(memory_space=pltpu.VMEM)
SMEM = pl.BlockSpec(memory_space=pltpu.SMEM)


def call(kernel, outs, scratch=(), limit=4, flops=0):
    return pl.pallas_call(
        kernel,
        out_shape=[jax.ShapeDtypeStruct(s, F32) for s in outs],
        out_specs=[VMEM] * len(outs),
        scratch_shapes=[pltpu.VMEM(s, F32) for s in scratch],
        compiler_params=pltpu.CompilerParams(vmem_limit_bytes=limit * MIB),
        cost_estimate=pl.CostEstimate(flops=flops, bytes_accessed=0, transcendentals=0) if flops else None,
    )


def before(v, k, axis):
    return pltpu.roll(v, k, axis)


def after(v, k, axis):
    return pltpu.roll(v, v.shape[axis] - k, axis)


def lane_of(shape):
    return lax.broadcasted_iota(jnp.int32, shape, len(shape) - 1)


def pair_sum(v, k):
    low = lane_of(v.shape) % (2 * k) < k
    return v + jnp.where(low, after(v, k, 1), before(v, k, 1))


def odd_group(v, k):
    low = lane_of(v.shape) % (2 * k) < k
    return jnp.where(low, after(v, k, 1), v)


def neighbours(ux, ux_prev, uy, uz, here, prev, nxt, k):
    return (
        ux * nxt
        + ux_prev * prev
        + uy * after(here, 1, 0)
        + before(uy * here, 1, 0)
        + uz * after(here, k, 1)
        + before(uz * here, k, 1)
    )


def modulus_of(bins):
    f = (bins.astype(F32) + 1.0) / BINS
    return 0.05 + 0.95 * f * f * f


def pack_kernel(density_in, residual_in, fixed_in, to_right, to_left, density, residual, fixed, sems):
    pairs = ((density_in, density), (residual_in, residual), (fixed_in, fixed))
    copies = [pltpu.make_async_copy(a, b, sems.at[i]) for i, (a, b) in enumerate(pairs)]
    for copy in copies:
        copy.start()
    block = lane_of((CY, CZ)) // ZH

    def stage(f, planes):
        turned = [pltpu.roll(v, ZH * p, 1) if p else v for p, v in enumerate(planes)]
        right, left = turned[0], turned[0]
        for p in range(1, CX):
            right = jnp.where(block == p - 1, turned[p], right)
            left = jnp.where(block == p, turned[p], left)
        to_right[f] = right
        to_left[f] = left

    for copy in copies:
        copy.wait()
    stage(0, [modulus_of(density[p]) for p in range(CX)])
    for c in range(3):
        stage(1 + c, [residual[c, p] for p in range(CX)])
        stage(4 + c, [1.0 - fixed[c, p].astype(F32) for p in range(CX)])


def main_kernel(density, residual, fixed, main):
    main[0] = modulus_of(density[...])
    main[1:4] = residual[...]
    main[4:7] = 1.0 - fixed[...].astype(F32)


def join_kernel(main, zl, zr, brick, up, down):
    brick[:, 0:CX] = main[...]
    brick[:, CX] = zl[...]
    brick[:, CX + 1] = zr[...]
    up[...] = brick[:, :, 8:16]
    down[...] = brick[:, :, 0:8]


def slab_kernel(xl, xr, up, down):
    for first, brick, near, far in ((0, xl, 4, 0), (SLAB, xr, 0, 4)):
        for out, row, row4 in ((up, 8, 12), (down, 0, 0)):
            out[:, first : first + 4] = brick[:, near : near + 4, row : row + 8]
            out[:, first + 4 : first + 6] = brick[:, CX : CX + 2, row : row + 8]
            for p in range(4):
                at = slice(4 * (p % 2), 4 * (p % 2) + 4)
                out[:, first + 6 + p // 2, at] = brick[:, far + p, row4 : row4 + 4]


def steps(start, stop, each, body):
    def step(i, _):
        for j in range(each):
            body(start + each * i + j, j)
        return 0

    lax.fori_loop(0, (stop - start) // each, step, 0)


def restrict_rows(tmp, v):
    n = v.shape[0] // 2
    for h in range(2):
        tmp[h] = v[:, CZ * h : CZ * (h + 1)]
    return [jnp.concatenate([tmp[h, pl.ds(i, n, stride=2), :] for h in range(2)], axis=1) for i in range(2)]


def repeat_rows(tmp, v):
    n = v.shape[0]
    for h in range(2):
        for i in range(2):
            tmp[h, pl.ds(i, n, stride=2), :] = v[:, CZ * h : CZ * (h + 1)]
    return jnp.concatenate([tmp[0], tmp[1]], axis=1)


def fine_kernel(
    ends, xl, x0, xr, lower0, upper0, lower, upper,
    ext, ux, uy, uz, inv, mux, muy, muz, mig, mc, o_right, o_left, o_own,
    mm, spring, mrhs, cx_, cy_, cz_, cg, tmp32, tmp16,
):
    block = lane_of((CY, CZ)) // ZH
    block8 = lane_of((8, CZ)) // ZH

    def put(f, p, start, main, from_left, from_right, at):
        halo = jnp.where(at == p % CX, from_right, from_left)
        rows = slice(start, start + main.shape[0])
        ext[f, p, rows, 0:CZ] = main
        ext[f, p, rows, CZ:LANES] = pltpu.roll(halo, CZ - ZH * (p % CX), 1) if p % CX else halo

    def assemble(f, _):
        for p in range(PLANES):
            b, q = p // CX, p % CX
            brick = (xl, x0, xr)[b]
            put(f, p, 8, brick[f, q], brick[f, CX], brick[f, CX + 1], block)
            for start, own, side, turn in ((0, lower0, lower, 0), (8 + CY, upper0, upper, 1)):
                if b == 1:
                    v, zs = own[f, q], (own[f, CX], own[f, CX + 1])
                else:
                    first = 0 if b == 0 else SLAB
                    zs = side[f, first + 4], side[f, first + 5]
                    if (q >= 4) == (b == 0):
                        v = side[f, first + q % 4]
                    else:
                        v = side[f, first + 6 + (q % 4) // 2]
                        v = before(v, 4, 0) if q % 2 == turn else v
                put(f, p, start, v, *zs, block8)
        return 0

    lax.fori_loop(0, FIELDS, assemble, 0)

    lo_x, hi_x, lo_y, hi_y, lo_z, hi_z = (ends[i] for i in range(6))
    shape = (ROWS, LANES)
    row = lax.broadcasted_iota(jnp.int32, shape, 0)
    col = lane_of(shape)
    half_y = jnp.where(((row == 7) & (lo_y == 1)) | ((row == 7 + CY) & (hi_y == 1)), 0.0, 0.5)
    half_z = jnp.where(((col == LANES - 1) & (lo_z == 1)) | ((col == CZ - 1) & (hi_z == 1)), 0.0, 0.5)

    def links(p, _):
        here = ext[0, p]
        cut = ((p == 7) & (lo_x == 1)) | ((p == 7 + CX) & (hi_x == 1))
        ux[p] = jnp.where(cut, 0.0, 0.5) * (here + ext[0, jnp.minimum(p + 1, PLANES - 1)])
        uy[p] = half_y * (here + after(here, 1, 0))
        uz[p] = half_z * (here + after(here, 1, 1))

    steps(0, PLANES, 8, links)

    def smooth(p, _):
        g = 0.1 * ext[0, p] + ux[p] + ux[p - 1]
        g = g + uy[p] + before(uy[p], 1, 0) + uz[p] + before(uz[p], 1, 1)
        ig = damping / g
        inv[p] = ig
        for c in range(3):
            mm[c, p] = ext[4 + c, p] * ext[1 + c, p] * ig

    steps(1, PLANES - 1, 11, smooth)

    def mid_links(q, j):
        tmp = [tmp32.at[4 * j + i] for i in range(4)]
        p = 2 * q
        a, b = restrict_rows(tmp[0], ux[p + 1])
        mux[q] = pair_sum(a + b, 1)
        _, b = restrict_rows(tmp[1], uy[p] + uy[p + 1])
        muy[q] = pair_sum(b, 1)
        a, b = restrict_rows(tmp[2], uz[p] + uz[p + 1])
        muz[q] = odd_group(a + b, 1)
        a, b = restrict_rows(tmp[3], ext[0, p] + ext[0, p + 1])
        spring[q] = 0.1 * pair_sum(a + b, 1)

    steps(0, 12, 6, mid_links)

    def mid_rhs(q, j):
        p = 2 * q
        g = spring[q] + mux[q] + mux[q - 1]
        g = g + muy[q] + before(muy[q], 1, 0) + muz[q] + before(muz[q], 2, 1)
        ig = damping / g
        mig[q] = ig
        for c in range(3):
            total = jnp.zeros(shape, F32)
            for i in range(2):
                near = neighbours(ux[p + i], ux[p + i - 1], uy[p + i], uz[p + i], mm[c, p + i], mm[c, p + i - 1], mm[c, p + i + 1], 1)
                total = total + keep * ext[1 + c, p + i] + ext[4 + c, p + i] * near
            a, b = restrict_rows(tmp32.at[3 * j + c], total)
            rhs = pair_sum(a + b, 1)
            mrhs[c, q] = rhs
            mc[c, q] = ig * rhs

    steps(1, 11, 2, mid_rhs)

    for s in range(5):
        q = 2 * s
        a, b = restrict_rows(tmp16.at[4 * s], mux[q + 1])
        cx_[s] = pair_sum(a + b, 2)
        _, b = restrict_rows(tmp16.at[4 * s + 1], muy[q] + muy[q + 1])
        cy_[s] = pair_sum(b, 2)
        a, b = restrict_rows(tmp16.at[4 * s + 2], muz[q] + muz[q + 1])
        cz_[s] = odd_group(a + b, 2)
        a, b = restrict_rows(tmp16.at[4 * s + 3], spring[q] + spring[q + 1])
        cg[s] = pair_sum(a + b, 2)

    quad = lane_of((8, LANES)) % 4
    for s in range(1, 5):
        g = cg[s] + cx_[s] + cx_[s - 1]
        g = g + cy_[s] + before(cy_[s], 1, 0) + cz_[s] + before(cz_[s], 4, 1)
        rhs = []
        for c in range(3):
            total = jnp.zeros((ROWS // 2, LANES), F32)
            for q in (2 * s, 2 * s + 1):
                near = neighbours(mux[q], mux[q - 1], muy[q], muz[q], mc[c, q], mc[c, q - 1], mc[c, q + 1], 2)
                total = total + keep * mrhs[c, q] + near
            a, b = restrict_rows(tmp16.at[20 + 3 * (s - 1) + c], total)
            rhs.append(pair_sum(a + b, 2))
        first = jnp.where(quad == 0, rhs[0], jnp.where(quad == 1, rhs[1], jnp.where(quad == 2, rhs[2], g)))
        second = jnp.where(quad == 0, cx_[s], jnp.where(quad == 1, cy_[s], cz_[s]))
        for i, v in enumerate((first, second)):
            if s <= 3:
                o_right[i, s - 1] = v
            if s >= 2:
                o_left[i, s - 2] = v
            if s in (2, 3):
                o_own[i, s - 2] = v


def unpack(v, quad, count):
    at = {0: v}
    for k in range(1, 4):
        at[k] = before(v, k, 1)
    for k in range(1, count):
        at[-k] = after(v, k, 1)
    return [
        jnp.where(quad == 0, at[-j], jnp.where(quad == 1, at[1 - j], jnp.where(quad == 2, at[2 - j], at[3 - j])))
        for j in range(count)
    ]


def turn_kernel(xl, own, xr, up, down):
    for i in range(2):
        for s in range(8):
            for j in range(3):
                for out, first in ((up, 3), (down, 2)):
                    at = slice(first + j, first + j + 1)
                    src = xl[i, s, at] if s < 3 else own[i, s - 3, at] if s < 5 else xr[i, s - 5, at]
                    out[i, j, s : s + 1] = src


def solve_kernel(
    xl, own, xr, yl, yr, ext, ux_, uy_, uz_, ig_, mux_, muy_, muz_, mig_, mc_,
    direction, image, sums,
    packed, cc, pm, pf, m1, base, d, tmp16,
):
    r, free = ext.at[1:4, 6:18], ext.at[4:7, 6:18]
    ux, uy, uz, ig = (a.at[6:18] for a in (ux_, uy_, uz_, ig_))
    mux, muy, muz, mig, mc = *(a.at[2:10] for a in (mux_, muy_, muz_, mig_)), mc_.at[:, 2:10]
    quad = lane_of((16, LANES)) % 4
    field = [[None] * 8 for _ in range(7)]
    for i in range(2):
        for s in range(8):
            here = packed.at[8 * i + s]
            here[...] = jnp.zeros((16, LANES), F32)
            here[4:8] = xl[i, s, 2:6] if s < 3 else own[i, s - 3, 2:6] if s < 5 else xr[i, s - 5, 2:6]
            for j in range(3):
                here[1 + j : 2 + j] = yl[i, j, s : s + 1]
                here[8 + j : 9 + j] = yr[i, j, s : s + 1]
            v = here[...]
            for k, u in enumerate(unpack(v, quad, 4 if i == 0 else 3)):
                field[4 * i + k][s] = u
    g = [jnp.where(v > 0.0, v, 1.0) for v in field[3]]
    inv = [1.0 / v for v in g]
    cx_, cy_, cz_ = field[4], field[5], field[6]
    ratio = eig_center / eig_halfwidth
    q0 = 1.0 / ratio
    q1 = 1.0 / (2.0 * ratio - q0)
    q2 = 1.0 / (2.0 * ratio - q1)
    for c in range(3):
        rhs = field[c]
        update = [rhs[s] * inv[s] * (1.0 / eig_center) for s in range(8)]
        iterate = list(update)
        for q_old, q_new, lo, hi in ((q0, q1, 1, 7), (q1, q2, 2, 6)):
            new = list(iterate)
            for s in range(lo, hi):
                near = neighbours(cx_[s], cx_[s - 1], cy_[s], cz_[s], iterate[s], iterate[s - 1], iterate[s + 1], 4)
                rest = rhs[s] - g[s] * iterate[s] + near
                update[s] = (q_new * q_old) * update[s] + (2.0 * q_new / eig_halfwidth) * (rest * inv[s])
                new[s] = iterate[s] + update[s]
            iterate = new
        for s in range(4):
            tmp16[4 * c + s] = iterate[2 + s]
            v = tmp16[4 * c + s, 2:10]
            v = repeat_rows(cc.at[4 * c + s], v)
            pm[c, 2 * s] = mc[c, 2 * s] + v
            pm[c, 2 * s + 1] = mc[c, 2 * s + 1] + v

    def mid(q, j):
        for c in range(3):
            near = neighbours(mux[q], mux[q - 1], muy[q], muz[q], pm[c, q], pm[c, q - 1], pm[c, q + 1], 2)
            v = keep * pm[c, q] + mc[c, q] + mig[q] * near
            v = repeat_rows(pf.at[3 * j + c], v)
            for i in range(2):
                p = 2 * (q - 1) + i
                fr = free[c, p]
                fc = r[c, p] * (fr * ig[p] + damping * (1.0 - fr))
                corr = fc + v
                m1[c, p] = fr * corr
                base[c, p] = keep * corr + fc

    steps(1, 7, 3, mid)

    def fine(p, _):
        for c in range(3):
            near = neighbours(ux[p], ux[p - 1], uy[p], uz[p], m1[c, p], m1[c, p - 1], m1[c, p + 1], 1)
            d[c, p] = base[c, p] + free[c, p] * ig[p] * near

    steps(1, 11, 5, fine)

    mine = slice(8, 8 + CY)

    def last(i, total):
        first, second = total
        for p, c in ((2 + 4 * i + j, c) for j in range(4) for c in range(3)):
            here = free[c, p] * d[c, p]
            prev = free[c, p - 1] * d[c, p - 1]
            nxt = free[c, p + 1] * d[c, p + 1]
            near = neighbours(ux[p], ux[p - 1], uy[p], uz[p], here, prev, nxt, 1)
            fr = free[c, p]
            im = fr * (damping / ig[p] * d[c, p] - near) + (1.0 - fr) * d[c, p]
            im = im[mine, 0:CZ]
            dd = d[c, p, mine, 0:CZ]
            direction[c, p - 2] = dd
            image[c, p - 2] = im
            first = first + r[c, p, mine, 0:CZ] * dd
            second = second + dd * im
        return first, second

    zero = jnp.zeros((CY, CZ), F32)
    first, second = lax.fori_loop(0, 2, last, (zero, zero))
    sums[0:1] = jnp.full((1, CZ), jnp.sum(first), F32)
    sums[1:2] = jnp.full((1, CZ), jnp.sum(second), F32)


def ring(count, step):
    return [(i, (i + step) % count) for i in range(count)]


def all_sum(v, axes):
    n = 1
    for axis in axes:
        n *= lax.axis_size(axis)
    sent = jnp.broadcast_to(v[None], (n,) + v.shape)
    return lax.all_to_all(sent, axes, 0, 0).sum(axis=0)


def shards(solution, residual, density_bins, fixed_dofs):
    nx, nc, nz = lax.axis_size("gx"), lax.axis_size("gc"), lax.axis_size("gz")
    ny = 2 * nc
    y_axes = ("gc", "co")
    ix, iz = lax.axis_index("gx"), lax.axis_index("gz")
    iy = 2 * lax.axis_index("gc") + lax.axis_index("co")
    ends = jnp.stack([ix == 0, ix == nx - 1, iy == 0, iy == ny - 1, iz == 0, iz == nz - 1]).astype(jnp.int32)

    def both(v, axes, count):
        up, down = v if isinstance(v, tuple) else (v, v)
        return lax.ppermute(up, axes, ring(count, 1)), lax.ppermute(down, axes, ring(count, -1))

    brick, pack = (FIELDS, GYX, CY, CZ), (FIELDS, CY, CZ)
    slab, slabs = (FIELDS, GYX, 8, CZ), (FIELDS, 2 * SLAB, 8, CZ)
    to_right, to_left = pl.pallas_call(
        pack_kernel,
        out_shape=[jax.ShapeDtypeStruct(pack, F32)] * 2,
        in_specs=[pl.BlockSpec(memory_space=pltpu.HBM)] * 3,
        out_specs=[VMEM] * 2,
        scratch_shapes=[
            pltpu.VMEM((CX, CY, CZ), jnp.int32),
            pltpu.VMEM((3, CX, CY, CZ), F32),
            pltpu.VMEM((3, CX, CY, CZ), jnp.int32),
            pltpu.SemaphoreType.DMA((3,)),
        ],
        compiler_params=pltpu.CompilerParams(vmem_limit_bytes=56 * MIB),
    )(density_bins, residual, fixed_dofs)
    zl, zr = both((to_right, to_left), "gz", nz)
    (main,) = call(main_kernel, [(FIELDS, CX, CY, CZ)], flops=10**9)(density_bins, residual, fixed_dofs)
    join = call(join_kernel, [brick, slab, slab])(main, zl, zr)
    x0, up, down, ends = lax.optimization_barrier((*join, ends))
    xl, xr = both(x0, "gx", nx)
    lower0, upper0 = both((up, down), y_axes, ny)
    xl, xr, lower0, upper0 = lax.optimization_barrier((xl, xr, lower0, upper0))
    lower, upper = both(tuple(call(slab_kernel, [slabs, slabs])(xl, xr)), y_axes, ny)

    full = (12, ROWS, LANES)
    half = (8, ROWS // 2, LANES)
    all_f = (PLANES, ROWS, LANES)
    all_m = (12, ROWS // 2, LANES)
    outs = [(FIELDS,) + all_f, all_f, all_f, all_f, all_f, all_m, all_m, all_m, all_m, (3,) + all_m]
    outs += [(2, 3, 8, LANES), (2, 3, 8, LANES), (2, 2, 8, LANES)]
    scratch = [(3,) + all_f, all_m, (3,) + all_m]
    scratch += [(5, 8, LANES)] * 4 + [(24, 2, ROWS, CZ), (32, 2, ROWS // 2, CZ)]
    fine = pl.pallas_call(
        fine_kernel,
        out_shape=[jax.ShapeDtypeStruct(s, F32) for s in outs],
        in_specs=[SMEM] + [VMEM] * 7,
        out_specs=[VMEM] * len(outs),
        scratch_shapes=[pltpu.VMEM(s, F32) for s in scratch],
        compiler_params=pltpu.CompilerParams(vmem_limit_bytes=8 * MIB),
    )(ends, xl, x0, xr, lower0, upper0, lower, upper)
    kept, (to_right, to_left, own) = fine[:-3], fine[-3:]
    cl, cr = both((to_right, to_left), "gx", nx)
    up, down = call(turn_kernel, [(2, 3, 8, LANES)] * 2)(cl, own, cr)
    dl, dr = both((up, down), y_axes, ny)
    direction, image, sums = call(
        solve_kernel,
        [(3, CX, CY, CZ), (3, CX, CY, CZ), (2, CZ)],
        [(16, 16, LANES), (12, 2, ROWS // 2, CZ), (3,) + half, (9, 2, ROWS, CZ), (3,) + full, (3,) + full, (3,) + full, (12, 16, LANES)],
        10,
    )(cl, own, cr, dl, dr, *kept)
    sums = all_sum(all_sum(sums, ("gc", "gz")), ("gx", "co"))
    alpha = (sums[0] / sums[1])[None, None, None]
    return (solution + alpha * direction, residual - alpha * image, direction)


def solution(mesh):
    nx, ny, nz = mesh.devices.shape
    split = Mesh(mesh.devices.reshape(nx, ny // 2, 2, nz), ("gx", "gc", "co", "gz"))
    field = P(None, "gx", ("gc", "co"), "gz")
    return jax.shard_map(
        shards,
        mesh=split,
        in_specs=(field, field, P("gx", ("gc", "co"), "gz"), field),
        out_specs=(field, field, field),
        check_vma=False,
    )
```

```python
import functools

import jax
import jax.numpy as jnp
from jax import lax
from jax.experimental import pallas as pl
from jax.experimental.pallas import tpu as pltpu
from jax.sharding import Mesh
from jax.sharding import PartitionSpec as P

BINS = 16
damping = 0.6
keep = 1.0 - damping
eig_center = 1.05
eig_halfwidth = 0.95

F32 = jnp.float32
CX, CY, CZ = 8, 16, 128
LANES = 2 * CZ
ROWS = CY + 16
PLANES = CX + 16
ZH = 16
MIB = 1024 * 1024
GYX = CX + 2
SLAB = 8
FIELDS = 7

VMEM = pl.BlockSpec(memory_space=pltpu.VMEM)


def call(kernel, outs, scratch=(), limit=4, flops=0):
    return pl.pallas_call(
        kernel,
        out_shape=[jax.ShapeDtypeStruct(s, F32) for s in outs],
        out_specs=[VMEM] * len(outs),
        scratch_shapes=[pltpu.VMEM(s, F32) for s in scratch],
        compiler_params=pltpu.CompilerParams(vmem_limit_bytes=limit * MIB),
        cost_estimate=pl.CostEstimate(flops=flops, bytes_accessed=0, transcendentals=0) if flops else None,
    )


def kernel_call(kernel, outs, arrays, scratch=(), limit=4):
    return pl.pallas_call(
        kernel,
        out_shape=[jax.ShapeDtypeStruct(s, F32) for s in outs],
        in_specs=[VMEM] * arrays,
        out_specs=[VMEM] * len(outs),
        scratch_shapes=[pltpu.VMEM(s, F32) for s in scratch],
        compiler_params=pltpu.CompilerParams(vmem_limit_bytes=limit * MIB),
    )


def before(v, k, axis):
    return pltpu.roll(v, k, axis)


def after(v, k, axis):
    return pltpu.roll(v, v.shape[axis] - k, axis)


def lane_of(shape):
    return lax.broadcasted_iota(jnp.int32, shape, len(shape) - 1)


def pair_sum(v, k):
    low = lane_of(v.shape) % (2 * k) < k
    return v + jnp.where(low, after(v, k, 1), before(v, k, 1))


def odd_group(v, k):
    low = lane_of(v.shape) % (2 * k) < k
    return jnp.where(low, after(v, k, 1), v)


def neighbours(ux, ux_prev, uy, uz, here, prev, nxt, k):
    return (
        ux * nxt
        + ux_prev * prev
        + uy * after(here, 1, 0)
        + before(uy * here, 1, 0)
        + uz * after(here, k, 1)
        + before(uz * here, k, 1)
    )


def modulus_of(bins):
    f = (bins.astype(F32) + 1.0) / BINS
    return 0.05 + 0.95 * f * f * f


def pack_kernel(density_in, residual_in, fixed_in, to_right, to_left, density, residual, fixed, sems):
    pairs = ((density_in, density), (residual_in, residual), (fixed_in, fixed))
    copies = [pltpu.make_async_copy(a, b, sems.at[i]) for i, (a, b) in enumerate(pairs)]
    for copy in copies:
        copy.start()
    block = lane_of((CY, CZ)) // ZH

    def stage(f, planes):
        turned = [pltpu.roll(v, ZH * p, 1) if p else v for p, v in enumerate(planes)]
        right, left = turned[0], turned[0]
        for p in range(1, CX):
            right = jnp.where(block == p - 1, turned[p], right)
            left = jnp.where(block == p, turned[p], left)
        to_right[f] = right
        to_left[f] = left

    for copy in copies:
        copy.wait()
    stage(0, [modulus_of(density[p]) for p in range(CX)])
    for c in range(3):
        stage(1 + c, [residual[c, p] for p in range(CX)])
        stage(4 + c, [1.0 - fixed[c, p].astype(F32) for p in range(CX)])


def main_kernel(density, residual, fixed, main):
    main[0] = modulus_of(density[...])
    main[1:4] = residual[...]
    main[4:7] = 1.0 - fixed[...].astype(F32)


def join_kernel(main, zl, zr, brick, up, down):
    brick[:, 0:CX] = main[...]
    brick[:, CX] = zl[...]
    brick[:, CX + 1] = zr[...]
    up[...] = brick[:, :, 8:16]
    down[...] = brick[:, :, 0:8]


def slab_kernel(xa, xb, up, down):
    for core in range(2):
        xl, xr = (xa, xb) if core else (xb, xa)

        @pl.when(lax.axis_index("co") == core)
        def _():
            for first, brick, near, far in ((0, xl, 4, 0), (SLAB, xr, 0, 4)):
                for out, row, row4 in ((up, 8, 12), (down, 0, 0)):
                    out[:, first : first + 4] = brick[:, near : near + 4, row : row + 8]
                    out[:, first + 4 : first + 6] = brick[:, CX : CX + 2, row : row + 8]
                    for p in range(4):
                        at = slice(4 * (p % 2), 4 * (p % 2) + 4)
                        out[:, first + 6 + p // 2, at] = brick[:, far + p, row4 : row4 + 4]


def steps(start, stop, each, body):
    def step(i, _):
        for j in range(each):
            body(start + each * i + j, j)
        return 0

    lax.fori_loop(0, (stop - start) // each, step, 0)


def restrict_rows(tmp, v):
    n = v.shape[0] // 2
    for h in range(2):
        tmp[h] = v[:, CZ * h : CZ * (h + 1)]
    return [jnp.concatenate([tmp[h, pl.ds(i, n, stride=2), :] for h in range(2)], axis=1) for i in range(2)]


def repeat_rows(tmp, v):
    n = v.shape[0]
    for h in range(2):
        for i in range(2):
            tmp[h, pl.ds(i, n, stride=2), :] = v[:, CZ * h : CZ * (h + 1)]
    return jnp.concatenate([tmp[0], tmp[1]], axis=1)


def fine_kernel(
    x0, xa, xb, lower0, upper0, lower, upper,
    ext, ux, uy, uz, inv, mux, muy, muz, mig, mc, o_a, o_b, o_own,
    mm, spring, mrhs, cx_, cy_, cz_, cg, tmp32, tmp16,
):
    block = lane_of((CY, CZ)) // ZH
    block8 = lane_of((8, CZ)) // ZH

    first_core = lax.axis_index("co") == 0

    def put(f, p, start, main, from_left, from_right, at):
        halo = jnp.where(at == p % CX, from_right, from_left)
        rows = slice(start, start + main.shape[0])
        ext[f, p, rows, 0:CZ] = main
        ext[f, p, rows, CZ:LANES] = pltpu.roll(halo, CZ - ZH * (p % CX), 1) if p % CX else halo

    def assemble(f, _):
        for p in range(PLANES):
            b, q = p // CX, p % CX

            def mine(at):
                if b == 1:
                    return x0[f, at]
                left, right = xb[f, at], xa[f, at]
                return jnp.where(first_core, left, right) if b == 0 else jnp.where(first_core, right, left)

            put(f, p, 8, mine(q), mine(CX), mine(CX + 1), block)
            for start, own, side, turn in ((0, lower0, lower, 0), (8 + CY, upper0, upper, 1)):
                if b == 1:
                    v, zs = own[f, q], (own[f, CX], own[f, CX + 1])
                else:
                    first = 0 if b == 0 else SLAB
                    zs = side[f, first + 4], side[f, first + 5]
                    if (q >= 4) == (b == 0):
                        v = side[f, first + q % 4]
                    else:
                        v = side[f, first + 6 + (q % 4) // 2]
                        v = before(v, 4, 0) if q % 2 == turn else v
                put(f, p, start, v, *zs, block8)
        return 0

    lax.fori_loop(0, FIELDS, assemble, 0)

    ix, iz = lax.axis_index("gx"), lax.axis_index("gz")
    iy = 2 * lax.axis_index("gc") + lax.axis_index("co")
    lo_x, lo_y, lo_z = ix == 0, iy == 0, iz == 0
    hi_x, hi_y, hi_z = ix == lax.axis_size("gx") - 1, iy == 2 * lax.axis_size("gc") - 1, iz == lax.axis_size("gz") - 1
    shape = (ROWS, LANES)
    row = lax.broadcasted_iota(jnp.int32, shape, 0)
    col = lane_of(shape)
    half_y = jnp.where(((row == 7) & lo_y) | ((row == 7 + CY) & hi_y), 0.0, 0.5)
    half_z = jnp.where(((col == LANES - 1) & lo_z) | ((col == CZ - 1) & hi_z), 0.0, 0.5)

    def links(p, _):
        here = ext[0, p]
        cut = ((p == 7) & lo_x) | ((p == 7 + CX) & hi_x)
        ux[p] = jnp.where(cut, 0.0, 0.5) * (here + ext[0, jnp.minimum(p + 1, PLANES - 1)])
        uy[p] = half_y * (here + after(here, 1, 0))
        uz[p] = half_z * (here + after(here, 1, 1))

    steps(0, PLANES, 8, links)

    def smooth(p, _):
        g = 0.1 * ext[0, p] + ux[p] + ux[p - 1]
        g = g + uy[p] + before(uy[p], 1, 0) + uz[p] + before(uz[p], 1, 1)
        ig = damping / g
        inv[p] = ig
        for c in range(3):
            mm[c, p] = ext[4 + c, p] * ext[1 + c, p] * ig

    steps(1, PLANES - 1, 11, smooth)

    def mid_links(q, j):
        tmp = [tmp32.at[4 * j + i] for i in range(4)]
        p = 2 * q
        a, b = restrict_rows(tmp[0], ux[p + 1])
        mux[q] = pair_sum(a + b, 1)
        _, b = restrict_rows(tmp[1], uy[p] + uy[p + 1])
        muy[q] = pair_sum(b, 1)
        a, b = restrict_rows(tmp[2], uz[p] + uz[p + 1])
        muz[q] = odd_group(a + b, 1)
        a, b = restrict_rows(tmp[3], ext[0, p] + ext[0, p + 1])
        spring[q] = 0.1 * pair_sum(a + b, 1)

    steps(0, 12, 6, mid_links)

    def mid_rhs(q, j):
        p = 2 * q
        g = spring[q] + mux[q] + mux[q - 1]
        g = g + muy[q] + before(muy[q], 1, 0) + muz[q] + before(muz[q], 2, 1)
        ig = damping / g
        mig[q] = ig
        for c in range(3):
            total = jnp.zeros(shape, F32)
            for i in range(2):
                near = neighbours(ux[p + i], ux[p + i - 1], uy[p + i], uz[p + i], mm[c, p + i], mm[c, p + i - 1], mm[c, p + i + 1], 1)
                total = total + keep * ext[1 + c, p + i] + ext[4 + c, p + i] * near
            a, b = restrict_rows(tmp32.at[3 * j + c], total)
            rhs = pair_sum(a + b, 1)
            mrhs[c, q] = rhs
            mc[c, q] = ig * rhs

    steps(1, 11, 2, mid_rhs)

    for s in range(5):
        q = 2 * s
        a, b = restrict_rows(tmp16.at[4 * s], mux[q + 1])
        cx_[s] = pair_sum(a + b, 2)
        _, b = restrict_rows(tmp16.at[4 * s + 1], muy[q] + muy[q + 1])
        cy_[s] = pair_sum(b, 2)
        a, b = restrict_rows(tmp16.at[4 * s + 2], muz[q] + muz[q + 1])
        cz_[s] = odd_group(a + b, 2)
        a, b = restrict_rows(tmp16.at[4 * s + 3], spring[q] + spring[q + 1])
        cg[s] = pair_sum(a + b, 2)

    quad = lane_of((8, LANES)) % 4
    sent = []
    for s in range(1, 5):
        g = cg[s] + cx_[s] + cx_[s - 1]
        g = g + cy_[s] + before(cy_[s], 1, 0) + cz_[s] + before(cz_[s], 4, 1)
        rhs = []
        for c in range(3):
            total = jnp.zeros((ROWS // 2, LANES), F32)
            for q in (2 * s, 2 * s + 1):
                near = neighbours(mux[q], mux[q - 1], muy[q], muz[q], mc[c, q], mc[c, q - 1], mc[c, q + 1], 2)
                total = total + keep * mrhs[c, q] + near
            a, b = restrict_rows(tmp16.at[20 + 3 * (s - 1) + c], total)
            rhs.append(pair_sum(a + b, 2))
        first = jnp.where(quad == 0, rhs[0], jnp.where(quad == 1, rhs[1], jnp.where(quad == 2, rhs[2], g)))
        second = jnp.where(quad == 0, cx_[s], jnp.where(quad == 1, cy_[s], cz_[s]))
        sent.append((first, second))
    for i in range(2):
        for k in range(3):
            right, left = sent[k][i], sent[k + 1][i]
            o_a[i, k] = jnp.where(first_core, left, right)
            o_b[i, k] = jnp.where(first_core, right, left)
        for k in range(2):
            o_own[i, k] = sent[1 + k][i]


def unpack(v, quad, count):
    at = {0: v}
    for k in range(1, 4):
        at[k] = before(v, k, 1)
    for k in range(1, count):
        at[-k] = after(v, k, 1)
    return [
        jnp.where(quad == 0, at[-j], jnp.where(quad == 1, at[1 - j], jnp.where(quad == 2, at[2 - j], at[3 - j])))
        for j in range(count)
    ]


def coarse_plane(xa, own, xb, i, s):
    if 3 <= s < 5:
        return own[i, s - 3]
    k = s % 5
    first = lax.axis_index("co") == 0
    return jnp.where(first, xb[i, k], xa[i, k]) if s < 3 else jnp.where(first, xa[i, k], xb[i, k])


def turn_kernel(xa, own, xb, up, down):
    for i in range(2):
        for s in range(8):
            v = coarse_plane(xa, own, xb, i, s)
            for j in range(3):
                up[i, j, s : s + 1] = v[3 + j : 4 + j]
                down[i, j, s : s + 1] = v[2 + j : 3 + j]


def solve_kernel(
    xa, own, xb, yl, yr, ext, ux_, uy_, uz_, ig_, mux_, muy_, muz_, mig_, mc_,
    direction, image, sums,
    packed, cc, pm, pf, m1, base, d, tmp16,
):
    r, free = ext.at[1:4, 6:18], ext.at[4:7, 6:18]
    ux, uy, uz, ig = (a.at[6:18] for a in (ux_, uy_, uz_, ig_))
    mux, muy, muz, mig, mc = *(a.at[2:10] for a in (mux_, muy_, muz_, mig_)), mc_.at[:, 2:10]
    quad = lane_of((16, LANES)) % 4
    field = [[None] * 8 for _ in range(7)]
    for i in range(2):
        for s in range(8):
            here = packed.at[8 * i + s]
            here[...] = jnp.zeros((16, LANES), F32)
            here[4:8] = coarse_plane(xa, own, xb, i, s)[2:6]
            for j in range(3):
                here[1 + j : 2 + j] = yl[i, j, s : s + 1]
                here[8 + j : 9 + j] = yr[i, j, s : s + 1]
            v = here[...]
            for k, u in enumerate(unpack(v, quad, 4 if i == 0 else 3)):
                field[4 * i + k][s] = u
    g = [jnp.where(v > 0.0, v, 1.0) for v in field[3]]
    inv = [1.0 / v for v in g]
    cx_, cy_, cz_ = field[4], field[5], field[6]
    ratio = eig_center / eig_halfwidth
    q0 = 1.0 / ratio
    q1 = 1.0 / (2.0 * ratio - q0)
    q2 = 1.0 / (2.0 * ratio - q1)
    for c in range(3):
        rhs = field[c]
        update = [rhs[s] * inv[s] * (1.0 / eig_center) for s in range(8)]
        iterate = list(update)
        for q_old, q_new, lo, hi in ((q0, q1, 1, 7), (q1, q2, 2, 6)):
            new = list(iterate)
            for s in range(lo, hi):
                near = neighbours(cx_[s], cx_[s - 1], cy_[s], cz_[s], iterate[s], iterate[s - 1], iterate[s + 1], 4)
                rest = rhs[s] - g[s] * iterate[s] + near
                update[s] = (q_new * q_old) * update[s] + (2.0 * q_new / eig_halfwidth) * (rest * inv[s])
                new[s] = iterate[s] + update[s]
            iterate = new
        for s in range(4):
            tmp16[4 * c + s] = iterate[2 + s]
            v = tmp16[4 * c + s, 2:10]
            v = repeat_rows(cc.at[4 * c + s], v)
            pm[c, 2 * s] = mc[c, 2 * s] + v
            pm[c, 2 * s + 1] = mc[c, 2 * s + 1] + v

    def mid(q, j):
        for c in range(3):
            near = neighbours(mux[q], mux[q - 1], muy[q], muz[q], pm[c, q], pm[c, q - 1], pm[c, q + 1], 2)
            v = keep * pm[c, q] + mc[c, q] + mig[q] * near
            v = repeat_rows(pf.at[3 * j + c], v)
            for i in range(2):
                p = 2 * (q - 1) + i
                fr = free[c, p]
                fc = r[c, p] * (fr * ig[p] + damping * (1.0 - fr))
                corr = fc + v
                m1[c, p] = fr * corr
                base[c, p] = keep * corr + fc

    steps(1, 7, 3, mid)

    def fine(p, _):
        for c in range(3):
            near = neighbours(ux[p], ux[p - 1], uy[p], uz[p], m1[c, p], m1[c, p - 1], m1[c, p + 1], 1)
            d[c, p] = base[c, p] + free[c, p] * ig[p] * near

    steps(1, 11, 5, fine)

    mine = slice(8, 8 + CY)

    def last(i, total):
        first, second = total
        for p, c in ((2 + 4 * i + j, c) for j in range(4) for c in range(3)):
            here = free[c, p] * d[c, p]
            prev = free[c, p - 1] * d[c, p - 1]
            nxt = free[c, p + 1] * d[c, p + 1]
            near = neighbours(ux[p], ux[p - 1], uy[p], uz[p], here, prev, nxt, 1)
            fr = free[c, p]
            im = fr * (damping / ig[p] * d[c, p] - near) + (1.0 - fr) * d[c, p]
            im = im[mine, 0:CZ]
            dd = d[c, p, mine, 0:CZ]
            direction[c, p - 2] = dd
            image[c, p - 2] = im
            first = first + r[c, p, mine, 0:CZ] * dd
            second = second + dd * im
        return first, second

    zero = jnp.zeros((CY, CZ), F32)
    first, second = lax.fori_loop(0, 2, last, (zero, zero))
    sums[0:1] = jnp.full((1, CZ), jnp.sum(first), F32)
    sums[1:2] = jnp.full((1, CZ), jnp.sum(second), F32)


def ring(count, step):
    return [(i, (i + step) % count) for i in range(count)]


def all_sum(v, axes):
    n = 1
    for axis in axes:
        n *= lax.axis_size(axis)
    sent = jnp.broadcast_to(v[None], (n,) + v.shape)
    return lax.all_to_all(sent, axes, 0, 0).sum(axis=0)


def shards(solution, residual, density_bins, fixed_dofs):
    nx, nc, nz = lax.axis_size("gx"), lax.axis_size("gc"), lax.axis_size("gz")
    ny = 2 * nc
    y_axes = ("gc", "co")
    def both(v, axes, count):
        up, down = v if isinstance(v, tuple) else (v, v)
        return lax.ppermute(up, axes, ring(count, 1)), lax.ppermute(down, axes, ring(count, -1))

    brick, pack = (FIELDS, GYX, CY, CZ), (FIELDS, CY, CZ)
    slab, slabs = (FIELDS, GYX, 8, CZ), (FIELDS, 2 * SLAB, 8, CZ)
    to_right, to_left = pl.pallas_call(
        pack_kernel,
        out_shape=[jax.ShapeDtypeStruct(pack, F32)] * 2,
        in_specs=[pl.BlockSpec(memory_space=pltpu.HBM)] * 3,
        out_specs=[VMEM] * 2,
        scratch_shapes=[
            pltpu.VMEM((CX, CY, CZ), jnp.int32),
            pltpu.VMEM((3, CX, CY, CZ), F32),
            pltpu.VMEM((3, CX, CY, CZ), jnp.int32),
            pltpu.SemaphoreType.DMA((3,)),
        ],
        compiler_params=pltpu.CompilerParams(vmem_limit_bytes=56 * MIB),
    )(density_bins, residual, fixed_dofs)
    zl, zr = both((to_right, to_left), "gz", nz)
    (main,) = call(main_kernel, [(FIELDS, CX, CY, CZ)], flops=10**9)(density_bins, residual, fixed_dofs)
    join = call(join_kernel, [brick, slab, slab])(main, zl, zr)
    x0, up, down = lax.optimization_barrier(tuple(join))

    def cross(a, b):
        return tuple(
            lax.ppermute(v, ("gx", "co"), [(2 * i + c, 2 * ((i + turn * (2 * c - 1)) % nx) + c) for i in range(nx) for c in range(2)])
            for v, turn in ((a, 1), (b, -1))
        )

    xa, xb = cross(x0, x0)
    lower0, upper0 = both((up, down), y_axes, ny)
    xa, xb, lower0, upper0 = lax.optimization_barrier((xa, xb, lower0, upper0))
    lower, upper = both(tuple(kernel_call(slab_kernel, [slabs, slabs], 2)(xa, xb)), y_axes, ny)

    full = (12, ROWS, LANES)
    half = (8, ROWS // 2, LANES)
    all_f = (PLANES, ROWS, LANES)
    all_m = (12, ROWS // 2, LANES)
    outs = [(FIELDS,) + all_f, all_f, all_f, all_f, all_f, all_m, all_m, all_m, all_m, (3,) + all_m]
    outs += [(2, 3, 8, LANES), (2, 3, 8, LANES), (2, 2, 8, LANES)]
    scratch = [(3,) + all_f, all_m, (3,) + all_m]
    scratch += [(5, 8, LANES)] * 4 + [(24, 2, ROWS, CZ), (32, 2, ROWS // 2, CZ)]
    fine = kernel_call(fine_kernel, outs, 7, scratch, 8)(x0, xa, xb, lower0, upper0, lower, upper)
    kept, (a, b, own) = fine[:-3], fine[-3:]
    ca, cb = cross(a, b)
    up, down = kernel_call(turn_kernel, [(2, 3, 8, LANES)] * 2, 3)(ca, own, cb)
    dl, dr = both((up, down), y_axes, ny)
    direction, image, sums = kernel_call(
        solve_kernel,
        [(3, CX, CY, CZ), (3, CX, CY, CZ), (2, CZ)],
        5 + len(kept),
        [(16, 16, LANES), (12, 2, ROWS // 2, CZ), (3,) + half, (9, 2, ROWS, CZ), (3,) + full, (3,) + full, (3,) + full, (12, 16, LANES)],
        10,
    )(ca, own, cb, dl, dr, *kept)
    sums = all_sum(all_sum(sums, ("gc", "gz")), ("gx", "co"))
    alpha = (sums[0] / sums[1])[None, None, None]
    return (solution + alpha * direction, residual - alpha * image, direction)


def solution(mesh):
    nx, ny, nz = mesh.devices.shape
    split = Mesh(mesh.devices.reshape(nx, ny // 2, 2, nz), ("gx", "gc", "co", "gz"))
    field = P(None, "gx", ("gc", "co"), "gz")
    return jax.shard_map(
        shards,
        mesh=split,
        in_specs=(field, field, P("gx", ("gc", "co"), "gz"), field),
        out_specs=(field, field, field),
        check_vma=False,
    )
```

```python
import functools

import jax
import jax.numpy as jnp
from jax import lax
from jax.experimental import pallas as pl
from jax.experimental.pallas import tpu as pltpu
from jax.sharding import Mesh
from jax.sharding import PartitionSpec as P

BINS = 16
damping = 0.6
keep = 1.0 - damping
eig_center = 1.05
eig_halfwidth = 0.95

F32 = jnp.float32
CX, CY, CZ = 8, 16, 128
LANES = 2 * CZ
ROWS = CY + 16
PLANES = CX + 16
ZH = 16
MIB = 1024 * 1024
GYX = CX + 2
SLAB = 8
FIELDS = 7

VMEM = pl.BlockSpec(memory_space=pltpu.VMEM)


def call(kernel, outs, scratch=(), limit=4, flops=0):
    return pl.pallas_call(
        kernel,
        out_shape=[jax.ShapeDtypeStruct(s, F32) for s in outs],
        out_specs=[VMEM] * len(outs),
        scratch_shapes=[pltpu.VMEM(s, F32) for s in scratch],
        compiler_params=pltpu.CompilerParams(vmem_limit_bytes=limit * MIB),
        cost_estimate=pl.CostEstimate(flops=flops, bytes_accessed=0, transcendentals=0) if flops else None,
    )


def kernel_call(kernel, outs, arrays, scratch=(), limit=4):
    return pl.pallas_call(
        kernel,
        out_shape=[jax.ShapeDtypeStruct(s, F32) for s in outs],
        in_specs=[VMEM] * arrays,
        out_specs=[VMEM] * len(outs),
        scratch_shapes=[pltpu.VMEM(s, F32) for s in scratch],
        compiler_params=pltpu.CompilerParams(vmem_limit_bytes=limit * MIB),
    )


def before(v, k, axis):
    return pltpu.roll(v, k, axis)


def after(v, k, axis):
    return pltpu.roll(v, v.shape[axis] - k, axis)


def lane_of(shape):
    return lax.broadcasted_iota(jnp.int32, shape, len(shape) - 1)


def pair_sum(v, k):
    low = lane_of(v.shape) % (2 * k) < k
    return v + jnp.where(low, after(v, k, 1), before(v, k, 1))


def odd_group(v, k):
    low = lane_of(v.shape) % (2 * k) < k
    return jnp.where(low, after(v, k, 1), v)


def neighbours(ux, ux_prev, uy, uz, here, prev, nxt, k):
    return (
        ux * nxt
        + ux_prev * prev
        + uy * after(here, 1, 0)
        + before(uy * here, 1, 0)
        + uz * after(here, k, 1)
        + before(uz * here, k, 1)
    )


def modulus_of(bins):
    f = (bins.astype(F32) + 1.0) / BINS
    return 0.05 + 0.95 * f * f * f


def pack_kernel(density_in, residual_in, fixed_in, to_right, to_left, density, residual, fixed, sems):
    pairs = ((density_in, density), (residual_in, residual), (fixed_in, fixed))
    copies = [pltpu.make_async_copy(a, b, sems.at[i]) for i, (a, b) in enumerate(pairs)]
    for copy in copies:
        copy.start()
    block = lane_of((CY, CZ)) // ZH

    def stage(f, planes):
        turned = [pltpu.roll(v, ZH * p, 1) if p else v for p, v in enumerate(planes)]
        right, left = turned[0], turned[0]
        for p in range(1, CX):
            right = jnp.where(block == p - 1, turned[p], right)
            left = jnp.where(block == p, turned[p], left)
        to_right[f] = right
        to_left[f] = left

    for copy in copies:
        copy.wait()
    stage(0, [modulus_of(density[p]) for p in range(CX)])
    for c in range(3):
        stage(1 + c, [residual[c, p] for p in range(CX)])
        stage(4 + c, [1.0 - fixed[c, p].astype(F32) for p in range(CX)])


def main_kernel(density, residual, fixed, main):
    main[0] = modulus_of(density[...])
    main[1:4] = residual[...]
    main[4:7] = 1.0 - fixed[...].astype(F32)


def join_kernel(main, zl, zr, brick, up, down):
    brick[:, 0:CX] = main[...]
    brick[:, CX] = zl[...]
    brick[:, CX + 1] = zr[...]
    up[...] = brick[:, :, 8:16]
    down[...] = brick[:, :, 0:8]


def slab_kernel(xa, xb, up, down):
    for core in range(2):
        xl, xr = (xa, xb) if core else (xb, xa)

        @pl.when(lax.axis_index("co") == core)
        def _():
            for first, brick, near, far in ((0, xl, 4, 0), (SLAB, xr, 0, 4)):
                for out, row, row4 in ((up, 8, 12), (down, 0, 0)):
                    out[:, first : first + 4] = brick[:, near : near + 4, row : row + 8]
                    out[:, first + 4 : first + 6] = brick[:, CX : CX + 2, row : row + 8]
                    for p in range(4):
                        at = slice(4 * (p % 2), 4 * (p % 2) + 4)
                        out[:, first + 6 + p // 2, at] = brick[:, far + p, row4 : row4 + 4]


def steps(start, stop, each, body):
    def step(i, _):
        for j in range(each):
            body(start + each * i + j, j)
        return 0

    lax.fori_loop(0, (stop - start) // each, step, 0)


def restrict_rows(tmp, v):
    n = v.shape[0] // 2
    for h in range(2):
        tmp[h] = v[:, CZ * h : CZ * (h + 1)]
    return [jnp.concatenate([tmp[h, pl.ds(i, n, stride=2), :] for h in range(2)], axis=1) for i in range(2)]


def repeat_rows(tmp, v):
    n = v.shape[0]
    for h in range(2):
        for i in range(2):
            tmp[h, pl.ds(i, n, stride=2), :] = v[:, CZ * h : CZ * (h + 1)]
    return jnp.concatenate([tmp[0], tmp[1]], axis=1)


def fine_kernel(
    x0, xa, xb, lower0, upper0, lower, upper,
    ext, ux, uy, uz, inv, mux, muy, muz, mig, mc, o_a, o_b, o_own,
    mm, spring, mrhs, cx_, cy_, cz_, cg, tmp32, tmp16,
):
    block = lane_of((CY, CZ)) // ZH
    block8 = lane_of((8, CZ)) // ZH

    first_core = lax.axis_index("co") == 0

    def put(f, p, start, main, from_left, from_right, at):
        halo = jnp.where(at == p % CX, from_right, from_left)
        rows = slice(start, start + main.shape[0])
        ext[f, p, rows, 0:CZ] = main
        ext[f, p, rows, CZ:LANES] = pltpu.roll(halo, CZ - ZH * (p % CX), 1) if p % CX else halo

    def assemble(f):
        for p in range(PLANES):
            b, q = p // CX, p % CX
            if f and p in (0, PLANES - 1):
                continue

            def mine(at):
                if b == 1:
                    return x0[f, at]
                left, right = xb[f, at], xa[f, at]
                return jnp.where(first_core, left, right) if b == 0 else jnp.where(first_core, right, left)

            put(f, p, 8, mine(q), mine(CX), mine(CX + 1), block)
            for start, own, side, turn in ((0, lower0, lower, 0), (8 + CY, upper0, upper, 1)):
                if b == 1:
                    v, zs = own[f, q], (own[f, CX], own[f, CX + 1])
                else:
                    first = 0 if b == 0 else SLAB
                    zs = side[f, first + 4], side[f, first + 5]
                    if (q >= 4) == (b == 0):
                        v = side[f, first + q % 4]
                    else:
                        v = side[f, first + 6 + (q % 4) // 2]
                        v = before(v, 4, 0) if q % 2 == turn else v
                put(f, p, start, v, *zs, block8)

    for f in range(FIELDS):
        assemble(f)

    ix, iz = lax.axis_index("gx"), lax.axis_index("gz")
    iy = 2 * lax.axis_index("gc") + lax.axis_index("co")
    lo_x, lo_y, lo_z = ix == 0, iy == 0, iz == 0
    hi_x, hi_y, hi_z = ix == lax.axis_size("gx") - 1, iy == 2 * lax.axis_size("gc") - 1, iz == lax.axis_size("gz") - 1
    shape = (ROWS, LANES)
    row = lax.broadcasted_iota(jnp.int32, shape, 0)
    col = lane_of(shape)
    half_y = jnp.where(((row == 7) & lo_y) | ((row == 7 + CY) & hi_y), 0.0, 0.5)
    half_z = jnp.where(((col == LANES - 1) & lo_z) | ((col == CZ - 1) & hi_z), 0.0, 0.5)

    def links(p, _):
        here = ext[0, p]
        cut = ((p == 7) & lo_x) | ((p == 7 + CX) & hi_x)
        ux[p] = jnp.where(cut, 0.0, 0.5) * (here + ext[0, jnp.minimum(p + 1, PLANES - 1)])
        uy[p] = half_y * (here + after(here, 1, 0))
        uz[p] = half_z * (here + after(here, 1, 1))

    steps(0, PLANES, 8, links)

    def smooth(p, _):
        g = 0.1 * ext[0, p] + ux[p] + ux[p - 1]
        g = g + uy[p] + before(uy[p], 1, 0) + uz[p] + before(uz[p], 1, 1)
        ig = damping / g
        inv[p] = ig
        for c in range(3):
            mm[c, p] = ext[4 + c, p] * ext[1 + c, p] * ig

    steps(1, PLANES - 1, 11, smooth)

    def mid_links(q, j):
        tmp = [tmp32.at[4 * j + i] for i in range(4)]
        p = 2 * q
        a, b = restrict_rows(tmp[0], ux[p + 1])
        mux[q] = pair_sum(a + b, 1)
        _, b = restrict_rows(tmp[1], uy[p] + uy[p + 1])
        muy[q] = pair_sum(b, 1)
        a, b = restrict_rows(tmp[2], uz[p] + uz[p + 1])
        muz[q] = odd_group(a + b, 1)
        a, b = restrict_rows(tmp[3], ext[0, p] + ext[0, p + 1])
        spring[q] = 0.1 * pair_sum(a + b, 1)

    steps(0, 12, 6, mid_links)

    def mid_rhs(q, j):
        p = 2 * q
        g = spring[q] + mux[q] + mux[q - 1]
        g = g + muy[q] + before(muy[q], 1, 0) + muz[q] + before(muz[q], 2, 1)
        ig = damping / g
        mig[q] = ig
        for c in range(3):
            total = jnp.zeros(shape, F32)
            for i in range(2):
                near = neighbours(ux[p + i], ux[p + i - 1], uy[p + i], uz[p + i], mm[c, p + i], mm[c, p + i - 1], mm[c, p + i + 1], 1)
                total = total + keep * ext[1 + c, p + i] + ext[4 + c, p + i] * near
            a, b = restrict_rows(tmp32.at[3 * j + c], total)
            rhs = pair_sum(a + b, 1)
            mrhs[c, q] = rhs
            mc[c, q] = ig * rhs

    steps(1, 11, 2, mid_rhs)

    for s in range(5):
        q = 2 * s
        a, b = restrict_rows(tmp16.at[4 * s], mux[q + 1])
        cx_[s] = pair_sum(a + b, 2)
        _, b = restrict_rows(tmp16.at[4 * s + 1], muy[q] + muy[q + 1])
        cy_[s] = pair_sum(b, 2)
        a, b = restrict_rows(tmp16.at[4 * s + 2], muz[q] + muz[q + 1])
        cz_[s] = odd_group(a + b, 2)
        a, b = restrict_rows(tmp16.at[4 * s + 3], spring[q] + spring[q + 1])
        cg[s] = pair_sum(a + b, 2)

    quad = lane_of((8, LANES)) % 4
    sent = []
    for s in range(1, 5):
        g = cg[s] + cx_[s] + cx_[s - 1]
        g = g + cy_[s] + before(cy_[s], 1, 0) + cz_[s] + before(cz_[s], 4, 1)
        rhs = []
        for c in range(3):
            total = jnp.zeros((ROWS // 2, LANES), F32)
            for q in (2 * s, 2 * s + 1):
                near = neighbours(mux[q], mux[q - 1], muy[q], muz[q], mc[c, q], mc[c, q - 1], mc[c, q + 1], 2)
                total = total + keep * mrhs[c, q] + near
            a, b = restrict_rows(tmp16.at[20 + 3 * (s - 1) + c], total)
            rhs.append(pair_sum(a + b, 2))
        first = jnp.where(quad == 0, rhs[0], jnp.where(quad == 1, rhs[1], jnp.where(quad == 2, rhs[2], g)))
        second = jnp.where(quad == 0, cx_[s], jnp.where(quad == 1, cy_[s], cz_[s]))
        sent.append((first, second))
    for i in range(2):
        for k in range(3):
            right, left = sent[k][i], sent[k + 1][i]
            o_a[i, k] = jnp.where(first_core, left, right)
            o_b[i, k] = jnp.where(first_core, right, left)
        for k in range(2):
            o_own[i, k] = sent[1 + k][i]


def unpack(v, quad, count):
    at = {0: v}
    for k in range(1, 4):
        at[k] = before(v, k, 1)
    for k in range(1, count):
        at[-k] = after(v, k, 1)
    return [
        jnp.where(quad == 0, at[-j], jnp.where(quad == 1, at[1 - j], jnp.where(quad == 2, at[2 - j], at[3 - j])))
        for j in range(count)
    ]


def coarse_plane(xa, own, xb, i, s):
    if 3 <= s < 5:
        return own[i, s - 3]
    k = s % 5
    first = lax.axis_index("co") == 0
    return jnp.where(first, xb[i, k], xa[i, k]) if s < 3 else jnp.where(first, xa[i, k], xb[i, k])


def turn_kernel(xa, own, xb, up, down):
    for i in range(2):
        for s in range(8):
            v = coarse_plane(xa, own, xb, i, s)
            for j in range(3):
                up[i, j, s : s + 1] = v[3 + j : 4 + j]
                down[i, j, s : s + 1] = v[2 + j : 3 + j]


def solve_kernel(
    xa, own, xb, yl, yr, ext, ux_, uy_, uz_, ig_, mux_, muy_, muz_, mig_, mc_,
    direction, image, sums,
    packed, cc, pm, pf, m1, base, d, tmp16,
):
    r, free = ext.at[1:4, 6:18], ext.at[4:7, 6:18]
    ux, uy, uz, ig = (a.at[6:18] for a in (ux_, uy_, uz_, ig_))
    mux, muy, muz, mig, mc = *(a.at[2:10] for a in (mux_, muy_, muz_, mig_)), mc_.at[:, 2:10]
    quad = lane_of((16, LANES)) % 4
    field = [[None] * 8 for _ in range(7)]
    for i in range(2):
        for s in range(8):
            here = packed.at[8 * i + s]
            here[...] = jnp.zeros((16, LANES), F32)
            here[4:8] = coarse_plane(xa, own, xb, i, s)[2:6]
            for j in range(3):
                here[1 + j : 2 + j] = yl[i, j, s : s + 1]
                here[8 + j : 9 + j] = yr[i, j, s : s + 1]
            v = here[...]
            for k, u in enumerate(unpack(v, quad, 4 if i == 0 else 3)):
                field[4 * i + k][s] = u
    g = [jnp.where(v > 0.0, v, 1.0) for v in field[3]]
    inv = [1.0 / v for v in g]
    cx_, cy_, cz_ = field[4], field[5], field[6]
    ratio = eig_center / eig_halfwidth
    q0 = 1.0 / ratio
    q1 = 1.0 / (2.0 * ratio - q0)
    q2 = 1.0 / (2.0 * ratio - q1)
    for c in range(3):
        rhs = field[c]
        update = [rhs[s] * inv[s] * (1.0 / eig_center) for s in range(8)]
        iterate = list(update)
        for q_old, q_new, lo, hi in ((q0, q1, 1, 7), (q1, q2, 2, 6)):
            new = list(iterate)
            for s in range(lo, hi):
                near = neighbours(cx_[s], cx_[s - 1], cy_[s], cz_[s], iterate[s], iterate[s - 1], iterate[s + 1], 4)
                rest = rhs[s] - g[s] * iterate[s] + near
                update[s] = (q_new * q_old) * update[s] + (2.0 * q_new / eig_halfwidth) * (rest * inv[s])
                new[s] = iterate[s] + update[s]
            iterate = new
        for s in range(4):
            tmp16[4 * c + s] = iterate[2 + s]
            v = tmp16[4 * c + s, 2:10]
            v = repeat_rows(cc.at[4 * c + s], v)
            pm[c, 2 * s] = mc[c, 2 * s] + v
            pm[c, 2 * s + 1] = mc[c, 2 * s + 1] + v

    def mid(q, j):
        for c in range(3):
            near = neighbours(mux[q], mux[q - 1], muy[q], muz[q], pm[c, q], pm[c, q - 1], pm[c, q + 1], 2)
            v = keep * pm[c, q] + mc[c, q] + mig[q] * near
            v = repeat_rows(pf.at[3 * j + c], v)
            for i in range(2):
                p = 2 * (q - 1) + i
                fr = free[c, p]
                fc = r[c, p] * (fr * ig[p] + damping * (1.0 - fr))
                corr = fc + v
                m1[c, p] = fr * corr
                base[c, p] = keep * corr + fc

    steps(1, 7, 3, mid)

    def fine(p, _):
        for c in range(3):
            near = neighbours(ux[p], ux[p - 1], uy[p], uz[p], m1[c, p], m1[c, p - 1], m1[c, p + 1], 1)
            d[c, p] = base[c, p] + free[c, p] * ig[p] * near

    steps(1, 11, 5, fine)

    mine = slice(8, 8 + CY)

    def last(i, total):
        first, second = total
        for p, c in ((2 + 4 * i + j, c) for j in range(4) for c in range(3)):
            here = free[c, p] * d[c, p]
            prev = free[c, p - 1] * d[c, p - 1]
            nxt = free[c, p + 1] * d[c, p + 1]
            near = neighbours(ux[p], ux[p - 1], uy[p], uz[p], here, prev, nxt, 1)
            fr = free[c, p]
            im = fr * (damping / ig[p] * d[c, p] - near) + (1.0 - fr) * d[c, p]
            im = im[mine, 0:CZ]
            dd = d[c, p, mine, 0:CZ]
            direction[c, p - 2] = dd
            image[c, p - 2] = im
            first = first + r[c, p, mine, 0:CZ] * dd
            second = second + dd * im
        return first, second

    zero = jnp.zeros((CY, CZ), F32)
    first, second = lax.fori_loop(0, 2, last, (zero, zero))
    sums[0:1] = jnp.full((1, CZ), jnp.sum(first), F32)
    sums[1:2] = jnp.full((1, CZ), jnp.sum(second), F32)


def ring(count, step):
    return [(i, (i + step) % count) for i in range(count)]


def all_sum(v, axes):
    n = 1
    for axis in axes:
        n *= lax.axis_size(axis)
    sent = jnp.broadcast_to(v[None], (n,) + v.shape)
    return lax.all_to_all(sent, axes, 0, 0).sum(axis=0)


def shards(solution, residual, density_bins, fixed_dofs):
    nx, nc, nz = lax.axis_size("gx"), lax.axis_size("gc"), lax.axis_size("gz")
    ny = 2 * nc
    y_axes = ("gc", "co")
    def both(v, axes, count):
        up, down = v if isinstance(v, tuple) else (v, v)
        return lax.ppermute(up, axes, ring(count, 1)), lax.ppermute(down, axes, ring(count, -1))

    brick, pack = (FIELDS, GYX, CY, CZ), (FIELDS, CY, CZ)
    slab, slabs = (FIELDS, GYX, 8, CZ), (FIELDS, 2 * SLAB, 8, CZ)
    to_right, to_left = pl.pallas_call(
        pack_kernel,
        out_shape=[jax.ShapeDtypeStruct(pack, F32)] * 2,
        in_specs=[pl.BlockSpec(memory_space=pltpu.HBM)] * 3,
        out_specs=[VMEM] * 2,
        scratch_shapes=[
            pltpu.VMEM((CX, CY, CZ), jnp.int32),
            pltpu.VMEM((3, CX, CY, CZ), F32),
            pltpu.VMEM((3, CX, CY, CZ), jnp.int32),
            pltpu.SemaphoreType.DMA((3,)),
        ],
        compiler_params=pltpu.CompilerParams(vmem_limit_bytes=56_410_000),
    )(density_bins, residual, fixed_dofs)
    zl, zr = both((to_right, to_left), "gz", nz)
    (main,) = call(main_kernel, [(FIELDS, CX, CY, CZ)], flops=10**9)(density_bins, residual, fixed_dofs)
    join = call(join_kernel, [brick, slab, slab])(main, zl, zr)
    x0, up, down = lax.optimization_barrier(tuple(join))

    def cross(a, b):
        return tuple(
            lax.ppermute(v, ("gx", "co"), [(2 * i + c, 2 * ((i + turn * (2 * c - 1)) % nx) + c) for i in range(nx) for c in range(2)])
            for v, turn in ((a, 1), (b, -1))
        )

    xa, xb = cross(x0, x0)
    lower0, upper0 = both((up, down), y_axes, ny)
    xa, xb, lower0, upper0 = lax.optimization_barrier((xa, xb, lower0, upper0))
    lower, upper = both(tuple(kernel_call(slab_kernel, [slabs, slabs], 2)(xa, xb)), y_axes, ny)

    full = (12, ROWS, LANES)
    half = (8, ROWS // 2, LANES)
    all_f = (PLANES, ROWS, LANES)
    all_m = (12, ROWS // 2, LANES)
    outs = [(FIELDS,) + all_f, all_f, all_f, all_f, all_f, all_m, all_m, all_m, all_m, (3,) + all_m]
    outs += [(2, 3, 8, LANES), (2, 3, 8, LANES), (2, 2, 8, LANES)]
    scratch = [(3,) + all_f, all_m, (3,) + all_m]
    scratch += [(5, 8, LANES)] * 4 + [(24, 2, ROWS, CZ), (32, 2, ROWS // 2, CZ)]
    fine = kernel_call(fine_kernel, outs, 7, scratch, 8)(x0, xa, xb, lower0, upper0, lower, upper)
    kept, (a, b, own) = fine[:-3], fine[-3:]
    ca, cb = cross(a, b)
    up, down = kernel_call(turn_kernel, [(2, 3, 8, LANES)] * 2, 3)(ca, own, cb)
    dl, dr = both((up, down), y_axes, ny)
    direction, image, sums = kernel_call(
        solve_kernel,
        [(3, CX, CY, CZ), (3, CX, CY, CZ), (2, CZ)],
        5 + len(kept),
        [(16, 16, LANES), (12, 2, ROWS // 2, CZ), (3,) + half, (9, 2, ROWS, CZ), (3,) + full, (3,) + full, (3,) + full, (12, 16, LANES)],
        10,
    )(ca, own, cb, dl, dr, *kept)
    sums = all_sum(all_sum(sums, ("gc", "gz")), ("gx", "co"))
    alpha = (sums[0] / sums[1])[None, None, None]
    return (solution + alpha * direction, residual - alpha * image, direction)


def solution(mesh):
    nx, ny, nz = mesh.devices.shape
    split = Mesh(mesh.devices.reshape(nx, ny // 2, 2, nz), ("gx", "gc", "co", "gz"))
    field = P(None, "gx", ("gc", "co"), "gz")
    return jax.shard_map(
        shards,
        mesh=split,
        in_specs=(field, field, P("gx", ("gc", "co"), "gz"), field),
        out_specs=(field, field, field),
        check_vma=False,
    )
```

```python
import functools

import jax
import jax.numpy as jnp
from jax import lax
from jax.experimental import pallas as pl
from jax.experimental.pallas import tpu as pltpu
from jax.sharding import Mesh
from jax.sharding import PartitionSpec as P

BINS = 16
damping = 0.6
keep = 1.0 - damping
eig_center = 1.05
eig_halfwidth = 0.95

F32 = jnp.float32
CX, CY, CZ = 8, 16, 128
LANES = 2 * CZ
ROWS = CY + 16
PLANES = CX + 16
ZH = 16
MIB = 1024 * 1024
GYX = CX + 2
CROSS = CX + 6 * (CX - 1) + 14
SLAB = 8
FIELDS = 7

VMEM = pl.BlockSpec(memory_space=pltpu.VMEM)


def call(kernel, outs, scratch=(), limit=4, flops=0):
    return pl.pallas_call(
        kernel,
        out_shape=[jax.ShapeDtypeStruct(s, F32) for s in outs],
        out_specs=[VMEM] * len(outs),
        scratch_shapes=[pltpu.VMEM(s, F32) for s in scratch],
        compiler_params=pltpu.CompilerParams(vmem_limit_bytes=limit * MIB),
        cost_estimate=pl.CostEstimate(flops=flops, bytes_accessed=0, transcendentals=0) if flops else None,
    )


def kernel_call(kernel, outs, arrays, scratch=(), limit=4):
    return pl.pallas_call(
        kernel,
        out_shape=[jax.ShapeDtypeStruct(s, F32) for s in outs],
        in_specs=[VMEM] * arrays,
        out_specs=[VMEM] * len(outs),
        scratch_shapes=[pltpu.VMEM(s, F32) for s in scratch],
        compiler_params=pltpu.CompilerParams(vmem_limit_bytes=limit * MIB),
    )


def before(v, k, axis):
    return pltpu.roll(v, k, axis)


def after(v, k, axis):
    return pltpu.roll(v, v.shape[axis] - k, axis)


def lane_of(shape):
    return lax.broadcasted_iota(jnp.int32, shape, len(shape) - 1)


def pair_sum(v, k):
    low = lane_of(v.shape) % (2 * k) < k
    return v + jnp.where(low, after(v, k, 1), before(v, k, 1))


def odd_group(v, k):
    low = lane_of(v.shape) % (2 * k) < k
    return jnp.where(low, after(v, k, 1), v)


def neighbours(ux, ux_prev, uy, uz, here, prev, nxt, k):
    return (
        ux * nxt
        + ux_prev * prev
        + uy * after(here, 1, 0)
        + before(uy * here, 1, 0)
        + uz * after(here, k, 1)
        + before(uz * here, k, 1)
    )


def modulus_of(bins):
    f = (bins.astype(F32) + 1.0) / BINS
    return 0.05 + 0.95 * f * f * f


def pack_kernel(density_in, residual_in, fixed_in, to_right, to_left, density, residual, fixed, sems):
    pairs = ((density_in, density), (residual_in, residual), (fixed_in, fixed))
    copies = [pltpu.make_async_copy(a, b, sems.at[i]) for i, (a, b) in enumerate(pairs)]
    for copy in copies:
        copy.start()
    block = lane_of((CY, CZ)) // ZH

    def stage(f, planes):
        turned = [pltpu.roll(v, ZH * p, 1) if p else v for p, v in enumerate(planes)]
        right, left = turned[0], turned[0]
        for p in range(1, CX):
            right = jnp.where(block == p - 1, turned[p], right)
            left = jnp.where(block == p, turned[p], left)
        to_right[f] = right
        to_left[f] = left

    for copy in copies:
        copy.wait()
    stage(0, [modulus_of(density[p]) for p in range(CX)])
    for c in range(3):
        stage(1 + c, [residual[c, p] for p in range(CX)])
        stage(4 + c, [1.0 - fixed[c, p].astype(F32) for p in range(CX)])


def main_kernel(density, residual, fixed, main):
    main[0] = modulus_of(density[...])
    main[1:4] = residual[...]
    main[4:7] = 1.0 - fixed[...].astype(F32)


def join_kernel(main, zl, zr, brick, up, down, a, b):
    brick[:, 0:CX] = main[...]
    brick[:, CX] = zl[...]
    brick[:, CX + 1] = zr[...]
    up[...] = brick[:, :, 8:16]
    down[...] = brick[:, :, 0:8]
    for core in range(2):
        left, right = (b, a) if core else (a, b)

        @pl.when(lax.axis_index("co") == core)
        def _():
            for out, near in ((left, 0), (right, 1)):
                out[0:CX] = main[0]
                for f in range(1, FIELDS):
                    out[7 * f + 1 : 7 * f + 8] = main[f, near : near + 7]
                for f in range(FIELDS):
                    out[50 + 2 * f] = zl[f]
                    out[51 + 2 * f] = zr[f]


def crossed(f, p, left):
    return p if f == 0 else 7 * f + 1 + p - left


def slab_kernel(xa, xb, up, down):
    for core in range(2):
        xl, xr = (xa, xb) if core else (xb, xa)

        @pl.when(lax.axis_index("co") == core)
        def _():
            for first, brick, near, far, left in ((0, xl, 4, 0, 1), (SLAB, xr, 0, 4, 0)):
                for f in range(FIELDS):
                    k = crossed(f, near, left)
                    for out, row, row4 in ((up, 8, 12), (down, 0, 0)):
                        out[f, first : first + 4] = brick[k : k + 4, row : row + 8]
                        out[f, first + 4 : first + 6] = brick[50 + 2 * f : 52 + 2 * f, row : row + 8]
                        for p in range(4):
                            if f and far + p == (0 if left else 7):
                                continue
                            at = slice(4 * (p % 2), 4 * (p % 2) + 4)
                            out[f, first + 6 + p // 2, at] = brick[crossed(f, far + p, left), row4 : row4 + 4]


def steps(start, stop, each, body):
    def step(i, _):
        for j in range(each):
            body(start + each * i + j, j)
        return 0

    lax.fori_loop(0, (stop - start) // each, step, 0)


def restrict_rows(tmp, v):
    n = v.shape[0] // 2
    for h in range(2):
        tmp[h] = v[:, CZ * h : CZ * (h + 1)]
    return [jnp.concatenate([tmp[h, pl.ds(i, n, stride=2), :] for h in range(2)], axis=1) for i in range(2)]


def repeat_rows(tmp, v):
    n = v.shape[0]
    for h in range(2):
        for i in range(2):
            tmp[h, pl.ds(i, n, stride=2), :] = v[:, CZ * h : CZ * (h + 1)]
    return jnp.concatenate([tmp[0], tmp[1]], axis=1)


def fine_kernel(
    x0, xa, xb, lower0, upper0, lower, upper,
    ext, ux, uy, uz, inv, mux, muy, muz, mig, mc, o_a, o_b, o_own,
    mm, spring, mrhs, cx_, cy_, cz_, cg, tmp32, tmp16,
):
    block = lane_of((CY, CZ)) // ZH
    block8 = lane_of((8, CZ)) // ZH

    first_core = lax.axis_index("co") == 0

    def put(f, p, start, main, from_left, from_right, at):
        halo = jnp.where(at == p % CX, from_right, from_left)
        rows = slice(start, start + main.shape[0])
        ext[f, p, rows, 0:CZ] = main
        ext[f, p, rows, CZ:LANES] = pltpu.roll(halo, CZ - ZH * (p % CX), 1) if p % CX else halo

    def assemble(f):
        for p in range(PLANES):
            b, q = p // CX, p % CX

            if f and p in (0, PLANES - 1):
                continue

            def mine(at):
                if b == 1:
                    return x0[f, at]
                k = 50 + 2 * f + at - CX if at >= CX else crossed(f, at, b == 0)
                left, right = xb[k], xa[k]
                return jnp.where(first_core, left, right) if b == 0 else jnp.where(first_core, right, left)

            put(f, p, 8, mine(q), mine(CX), mine(CX + 1), block)
            for start, own, side, turn in ((0, lower0, lower, 0), (8 + CY, upper0, upper, 1)):
                if b == 1:
                    v, zs = own[f, q], (own[f, CX], own[f, CX + 1])
                else:
                    first = 0 if b == 0 else SLAB
                    zs = side[f, first + 4], side[f, first + 5]
                    if (q >= 4) == (b == 0):
                        v = side[f, first + q % 4]
                    else:
                        v = side[f, first + 6 + (q % 4) // 2]
                        v = before(v, 4, 0) if q % 2 == turn else v
                put(f, p, start, v, *zs, block8)

    for f in range(FIELDS):
        assemble(f)

    ix, iz = lax.axis_index("gx"), lax.axis_index("gz")
    iy = 2 * lax.axis_index("gc") + lax.axis_index("co")
    lo_x, lo_y, lo_z = ix == 0, iy == 0, iz == 0
    hi_x, hi_y, hi_z = ix == lax.axis_size("gx") - 1, iy == 2 * lax.axis_size("gc") - 1, iz == lax.axis_size("gz") - 1
    shape = (ROWS, LANES)
    row = lax.broadcasted_iota(jnp.int32, shape, 0)
    col = lane_of(shape)
    half_y = jnp.where(((row == 7) & lo_y) | ((row == 7 + CY) & hi_y), 0.0, 0.5)
    half_z = jnp.where(((col == LANES - 1) & lo_z) | ((col == CZ - 1) & hi_z), 0.0, 0.5)

    def links(p, _):
        here = ext[0, p]
        cut = ((p == 7) & lo_x) | ((p == 7 + CX) & hi_x)
        ux[p] = jnp.where(cut, 0.0, 0.5) * (here + ext[0, jnp.minimum(p + 1, PLANES - 1)])
        uy[p] = half_y * (here + after(here, 1, 0))
        uz[p] = half_z * (here + after(here, 1, 1))

    steps(0, PLANES, 8, links)

    def smooth(p, _):
        g = 0.1 * ext[0, p] + ux[p] + ux[p - 1]
        g = g + uy[p] + before(uy[p], 1, 0) + uz[p] + before(uz[p], 1, 1)
        ig = damping / g
        inv[p] = ig
        for c in range(3):
            mm[c, p] = ext[4 + c, p] * ext[1 + c, p] * ig

    steps(1, PLANES - 1, 11, smooth)

    def mid_links(q, j):
        tmp = [tmp32.at[4 * j + i] for i in range(4)]
        p = 2 * q
        a, b = restrict_rows(tmp[0], ux[p + 1])
        mux[q] = pair_sum(a + b, 1)
        _, b = restrict_rows(tmp[1], uy[p] + uy[p + 1])
        muy[q] = pair_sum(b, 1)
        a, b = restrict_rows(tmp[2], uz[p] + uz[p + 1])
        muz[q] = odd_group(a + b, 1)
        a, b = restrict_rows(tmp[3], ext[0, p] + ext[0, p + 1])
        spring[q] = 0.1 * pair_sum(a + b, 1)

    steps(0, 12, 6, mid_links)

    def mid_rhs(q, j):
        p = 2 * q
        g = spring[q] + mux[q] + mux[q - 1]
        g = g + muy[q] + before(muy[q], 1, 0) + muz[q] + before(muz[q], 2, 1)
        ig = damping / g
        mig[q] = ig
        for c in range(3):
            total = jnp.zeros(shape, F32)
            for i in range(2):
                near = neighbours(ux[p + i], ux[p + i - 1], uy[p + i], uz[p + i], mm[c, p + i], mm[c, p + i - 1], mm[c, p + i + 1], 1)
                total = total + keep * ext[1 + c, p + i] + ext[4 + c, p + i] * near
            a, b = restrict_rows(tmp32.at[3 * j + c], total)
            rhs = pair_sum(a + b, 1)
            mrhs[c, q] = rhs
            mc[c, q] = ig * rhs

    steps(1, 11, 2, mid_rhs)

    for s in range(5):
        q = 2 * s
        a, b = restrict_rows(tmp16.at[4 * s], mux[q + 1])
        cx_[s] = pair_sum(a + b, 2)
        _, b = restrict_rows(tmp16.at[4 * s + 1], muy[q] + muy[q + 1])
        cy_[s] = pair_sum(b, 2)
        a, b = restrict_rows(tmp16.at[4 * s + 2], muz[q] + muz[q + 1])
        cz_[s] = odd_group(a + b, 2)
        a, b = restrict_rows(tmp16.at[4 * s + 3], spring[q] + spring[q + 1])
        cg[s] = pair_sum(a + b, 2)

    quad = lane_of((8, LANES)) % 4
    sent = []
    for s in range(1, 5):
        g = cg[s] + cx_[s] + cx_[s - 1]
        g = g + cy_[s] + before(cy_[s], 1, 0) + cz_[s] + before(cz_[s], 4, 1)
        rhs = []
        for c in range(3):
            total = jnp.zeros((ROWS // 2, LANES), F32)
            for q in (2 * s, 2 * s + 1):
                near = neighbours(mux[q], mux[q - 1], muy[q], muz[q], mc[c, q], mc[c, q - 1], mc[c, q + 1], 2)
                total = total + keep * mrhs[c, q] + near
            a, b = restrict_rows(tmp16.at[20 + 3 * (s - 1) + c], total)
            rhs.append(pair_sum(a + b, 2))
        first = jnp.where(quad == 0, rhs[0], jnp.where(quad == 1, rhs[1], jnp.where(quad == 2, rhs[2], g)))
        second = jnp.where(quad == 0, cx_[s], jnp.where(quad == 1, cy_[s], cz_[s]))
        sent.append((first, second))
    for i in range(2):
        for k in range(3):
            right, left = sent[k][i], sent[k + 1][i]
            o_a[i, k] = jnp.where(first_core, left, right)
            o_b[i, k] = jnp.where(first_core, right, left)
        for k in range(2):
            o_own[i, k] = sent[1 + k][i]


def unpack(v, quad, count):
    at = {0: v}
    for k in range(1, 4):
        at[k] = before(v, k, 1)
    for k in range(1, count):
        at[-k] = after(v, k, 1)
    return [
        jnp.where(quad == 0, at[-j], jnp.where(quad == 1, at[1 - j], jnp.where(quad == 2, at[2 - j], at[3 - j])))
        for j in range(count)
    ]


def coarse_plane(xa, own, xb, i, s):
    if 3 <= s < 5:
        return own[i, s - 3]
    k = s % 5
    first = lax.axis_index("co") == 0
    return jnp.where(first, xb[i, k], xa[i, k]) if s < 3 else jnp.where(first, xa[i, k], xb[i, k])


def turn_kernel(xa, own, xb, up, down):
    for i in range(2):
        for s in range(8):
            v = coarse_plane(xa, own, xb, i, s)
            for j in range(3):
                up[i, j, s : s + 1] = v[3 + j : 4 + j]
                down[i, j, s : s + 1] = v[2 + j : 3 + j]


def solve_kernel(
    xa, own, xb, yl, yr, ext, ux_, uy_, uz_, ig_, mux_, muy_, muz_, mig_, mc_,
    direction, image, sums,
    packed, cc, pm, pf, m1, base, d, tmp16,
):
    r, free = ext.at[1:4, 6:18], ext.at[4:7, 6:18]
    ux, uy, uz, ig = (a.at[6:18] for a in (ux_, uy_, uz_, ig_))
    mux, muy, muz, mig, mc = *(a.at[2:10] for a in (mux_, muy_, muz_, mig_)), mc_.at[:, 2:10]
    quad = lane_of((16, LANES)) % 4
    field = [[None] * 8 for _ in range(7)]
    for i in range(2):
        for s in range(8):
            here = packed.at[8 * i + s]
            here[...] = jnp.zeros((16, LANES), F32)
            here[4:8] = coarse_plane(xa, own, xb, i, s)[2:6]
            for j in range(3):
                here[1 + j : 2 + j] = yl[i, j, s : s + 1]
                here[8 + j : 9 + j] = yr[i, j, s : s + 1]
            v = here[...]
            for k, u in enumerate(unpack(v, quad, 4 if i == 0 else 3)):
                field[4 * i + k][s] = u
    g = [jnp.where(v > 0.0, v, 1.0) for v in field[3]]
    inv = [1.0 / v for v in g]
    cx_, cy_, cz_ = field[4], field[5], field[6]
    ratio = eig_center / eig_halfwidth
    q0 = 1.0 / ratio
    q1 = 1.0 / (2.0 * ratio - q0)
    q2 = 1.0 / (2.0 * ratio - q1)
    for c in range(3):
        rhs = field[c]
        update = [rhs[s] * inv[s] * (1.0 / eig_center) for s in range(8)]
        iterate = list(update)
        for q_old, q_new, lo, hi in ((q0, q1, 1, 7), (q1, q2, 2, 6)):
            new = list(iterate)
            for s in range(lo, hi):
                near = neighbours(cx_[s], cx_[s - 1], cy_[s], cz_[s], iterate[s], iterate[s - 1], iterate[s + 1], 4)
                rest = rhs[s] - g[s] * iterate[s] + near
                update[s] = (q_new * q_old) * update[s] + (2.0 * q_new / eig_halfwidth) * (rest * inv[s])
                new[s] = iterate[s] + update[s]
            iterate = new
        for s in range(4):
            tmp16[4 * c + s] = iterate[2 + s]
            v = tmp16[4 * c + s, 2:10]
            v = repeat_rows(cc.at[4 * c + s], v)
            pm[c, 2 * s] = mc[c, 2 * s] + v
            pm[c, 2 * s + 1] = mc[c, 2 * s + 1] + v

    def mid(q, j):
        for c in range(3):
            near = neighbours(mux[q], mux[q - 1], muy[q], muz[q], pm[c, q], pm[c, q - 1], pm[c, q + 1], 2)
            v = keep * pm[c, q] + mc[c, q] + mig[q] * near
            v = repeat_rows(pf.at[3 * j + c], v)
            for i in range(2):
                p = 2 * (q - 1) + i
                fr = free[c, p]
                fc = r[c, p] * (fr * ig[p] + damping * (1.0 - fr))
                corr = fc + v
                m1[c, p] = fr * corr
                base[c, p] = keep * corr + fc

    steps(1, 7, 3, mid)

    def fine(p, _):
        for c in range(3):
            near = neighbours(ux[p], ux[p - 1], uy[p], uz[p], m1[c, p], m1[c, p - 1], m1[c, p + 1], 1)
            d[c, p] = base[c, p] + free[c, p] * ig[p] * near

    steps(1, 11, 5, fine)

    mine = slice(8, 8 + CY)

    def last(i, total):
        first, second = total
        for p, c in ((2 + 4 * i + j, c) for j in range(4) for c in range(3)):
            here = free[c, p] * d[c, p]
            prev = free[c, p - 1] * d[c, p - 1]
            nxt = free[c, p + 1] * d[c, p + 1]
            near = neighbours(ux[p], ux[p - 1], uy[p], uz[p], here, prev, nxt, 1)
            fr = free[c, p]
            im = fr * (damping / ig[p] * d[c, p] - near) + (1.0 - fr) * d[c, p]
            im = im[mine, 0:CZ]
            dd = d[c, p, mine, 0:CZ]
            direction[c, p - 2] = dd
            image[c, p - 2] = im
            first = first + r[c, p, mine, 0:CZ] * dd
            second = second + dd * im
        return first, second

    zero = jnp.zeros((CY, CZ), F32)
    first, second = lax.fori_loop(0, 2, last, (zero, zero))
    sums[0:1] = jnp.full((1, CZ), jnp.sum(first), F32)
    sums[1:2] = jnp.full((1, CZ), jnp.sum(second), F32)


def ring(count, step):
    return [(i, (i + step) % count) for i in range(count)]


def all_sum(v, axes):
    n = 1
    for axis in axes:
        n *= lax.axis_size(axis)
    sent = jnp.broadcast_to(v[None], (n,) + v.shape)
    return lax.all_to_all(sent, axes, 0, 0).sum(axis=0)


def shards(solution, residual, density_bins, fixed_dofs):
    nx, nc, nz = lax.axis_size("gx"), lax.axis_size("gc"), lax.axis_size("gz")
    ny = 2 * nc
    y_axes = ("gc", "co")
    def both(v, axes, count):
        up, down = v if isinstance(v, tuple) else (v, v)
        return lax.ppermute(up, axes, ring(count, 1)), lax.ppermute(down, axes, ring(count, -1))

    brick, pack = (FIELDS, GYX, CY, CZ), (FIELDS, CY, CZ)
    slab, slabs = (FIELDS, GYX, 8, CZ), (FIELDS, 2 * SLAB, 8, CZ)
    to_right, to_left = pl.pallas_call(
        pack_kernel,
        out_shape=[jax.ShapeDtypeStruct(pack, F32)] * 2,
        in_specs=[pl.BlockSpec(memory_space=pltpu.HBM)] * 3,
        out_specs=[VMEM] * 2,
        scratch_shapes=[
            pltpu.VMEM((CX, CY, CZ), jnp.int32),
            pltpu.VMEM((3, CX, CY, CZ), F32),
            pltpu.VMEM((3, CX, CY, CZ), jnp.int32),
            pltpu.SemaphoreType.DMA((3,)),
        ],
        compiler_params=pltpu.CompilerParams(vmem_limit_bytes=56_410_000),
    )(density_bins, residual, fixed_dofs)
    zl, zr = both((to_right, to_left), "gz", nz)
    (main,) = call(main_kernel, [(FIELDS, CX, CY, CZ)], flops=10**9)(density_bins, residual, fixed_dofs)
    join = kernel_call(join_kernel, [brick, slab, slab, (CROSS, CY, CZ), (CROSS, CY, CZ)], 3, limit=8)(main, zl, zr)
    x0, up, down, a, b = lax.optimization_barrier(tuple(join))

    def cross(a, b):
        return tuple(
            lax.ppermute(v, ("gx", "co"), [(2 * i + c, 2 * ((i + turn * (2 * c - 1)) % nx) + c) for i in range(nx) for c in range(2)])
            for v, turn in ((a, 1), (b, -1))
        )

    xa, xb = cross(a, b)
    lower0, upper0 = both((up, down), y_axes, ny)
    xa, xb, lower0, upper0 = lax.optimization_barrier((xa, xb, lower0, upper0))
    lower, upper = both(tuple(kernel_call(slab_kernel, [slabs, slabs], 2)(xa, xb)), y_axes, ny)

    full = (12, ROWS, LANES)
    half = (8, ROWS // 2, LANES)
    all_f = (PLANES, ROWS, LANES)
    all_m = (12, ROWS // 2, LANES)
    outs = [(FIELDS,) + all_f, all_f, all_f, all_f, all_f, all_m, all_m, all_m, all_m, (3,) + all_m]
    outs += [(2, 3, 8, LANES), (2, 3, 8, LANES), (2, 2, 8, LANES)]
    scratch = [(3,) + all_f, all_m, (3,) + all_m]
    scratch += [(5, 8, LANES)] * 4 + [(24, 2, ROWS, CZ), (32, 2, ROWS // 2, CZ)]
    fine = kernel_call(fine_kernel, outs, 7, scratch, 8)(x0, xa, xb, lower0, upper0, lower, upper)
    kept, (a, b, own) = fine[:-3], fine[-3:]
    ca, cb = cross(a, b)
    up, down = kernel_call(turn_kernel, [(2, 3, 8, LANES)] * 2, 3)(ca, own, cb)
    dl, dr = both((up, down), y_axes, ny)
    direction, image, sums = kernel_call(
        solve_kernel,
        [(3, CX, CY, CZ), (3, CX, CY, CZ), (2, CZ)],
        5 + len(kept),
        [(16, 16, LANES), (12, 2, ROWS // 2, CZ), (3,) + half, (9, 2, ROWS, CZ), (3,) + full, (3,) + full, (3,) + full, (12, 16, LANES)],
        10,
    )(ca, own, cb, dl, dr, *kept)
    sums = all_sum(all_sum(sums, ("gc", "gz")), ("gx", "co"))
    alpha = (sums[0] / sums[1])[None, None, None]
    return (solution + alpha * direction, residual - alpha * image, direction)


def solution(mesh):
    nx, ny, nz = mesh.devices.shape
    split = Mesh(mesh.devices.reshape(nx, ny // 2, 2, nz), ("gx", "gc", "co", "gz"))
    field = P(None, "gx", ("gc", "co"), "gz")
    return jax.shard_map(
        shards,
        mesh=split,
        in_specs=(field, field, P("gx", ("gc", "co"), "gz"), field),
        out_specs=(field, field, field),
        check_vma=False,
    )
```
